32 devices in a mesh: req: 8 (over y, x, core), tp: 4 (over z).
Axes of the slice: x: 2, y: 2, z: 4, core: 2. Of those that a mesh axis runs over, the one named last changes fastest.
Arguments:
- hidden: bfloat16 [16, 128, 7168], P('req', None, 'tp'), may hold values from -7 to 7
- norm_gain: float32 [7168], replicated, may hold values from 0.5 to 1.5
- w_query: bfloat16 [7168, 2048], P(None, 'tp'), may hold values from -13 to 13
- w_kv: bfloat16 [7168, 2, 512], P(None, None, 'tp'), may hold values from -13 to 13
- w_out: bfloat16 [2048, 7168], P('tp'), may hold values from -0.125 to 0.125
- prefix_cache: bfloat16 [8, 2048, 2, 512], P('req', None, None, 'tp'), may hold values from -60 to 60
- lengths: int32 [16], P('req'), may hold values from 1 to 128, as said below
- groups: int32 [16], replicated, may hold values from 0 to 7, as said below
- owners: int32 [8], replicated, may hold values from 0 to 7, each once
Outputs:
- out_hidden: bfloat16 [16, 128, 7168], P('req', None, 'tp')
- suffix_cache: bfloat16 [16, 128, 2, 512], P('req', None, None, 'tp')
The draws below stay inside these ranges and needn't reach their ends.
Inputs may be any that keep to these rules, and one draw needn't show every extreme that they name: `lengths`: some request has all 128 positions live in every draw. The 2 requests of one req index belong to different groups; exactly one group has 4 requests; every other group has at most 2. `owners`: each req index once.
All inputs are finite; a program needn't handle non-finite values.
Results may differ from the reference program's by a relative error of at most 0.014.
Values may be sent and summed in bfloat16 or wider, within the bound.
No kernel may reach another device: no remote copies, remote signals or barrier semaphores. Data moves between devices by JAX's collectives and lax.ppermute only.
A program may use at most 192 MiB of HBM per device.

```python
import jax
import jax.numpy as jnp
from jax import lax

D = 7168
HD = 128
GROUP = 4
SUF = 128
PREFIX = 2048
REQ_DEV = 2
KVH = 4
HEADS = 16
REQUESTS = 16
N_REQ = 8


def draw_prefix_cache(key, part):
    shape = (N_REQ, PREFIX, 2, KVH * HD)
    values = jnp.clip(jax.random.normal(key, shape, jnp.float32), -6.0, 6.0)
    return values.astype(jnp.bfloat16)


def draw_hidden(key, part):
    noise = jnp.clip(jax.random.normal(jax.random.fold_in(key, 21), (REQUESTS, SUF, D), jnp.float32), -6.0, 6.0)
    return noise.astype(jnp.bfloat16)


def key_weights(key):
    base = jax.random.normal(jax.random.fold_in(key, 102), (D, KVH, HD), jnp.float32)
    return jnp.clip(base, -6.0, 6.0) * D ** (-0.5)


def draw_w_kv(key, part):
    keys_part = key_weights(key)
    values_part = jnp.clip(jax.random.normal(jax.random.fold_in(key, 104), (D, KVH, HD), jnp.float32), -6.0, 6.0) * D ** (-0.5)
    stacked = jnp.stack([keys_part, values_part], axis=1)
    return stacked.reshape(D, 2, KVH * HD).astype(jnp.bfloat16)


def draw_w_query(key, part):
    own = jnp.clip(jax.random.normal(jax.random.fold_in(key, 103), (D, KVH, GROUP, HD), jnp.float32), -6.0, 6.0) * D ** (-0.5)
    return own.reshape(D, KVH * GROUP * HD).astype(jnp.bfloat16)


def draw_lengths(key, part):
    drawn = jax.random.randint(jax.random.fold_in(key, 1), (REQUESTS,), 1, SUF + 1)
    longest = jax.random.randint(jax.random.fold_in(key, 2), (), 0, REQUESTS)
    return jnp.where(jnp.arange(REQUESTS) == longest, SUF, drawn).astype(jnp.int32)


def draw_groups(key, part):
    busiest = jax.random.randint(jax.random.fold_in(key, 1), (), 0, N_REQ)
    device_ids = jnp.arange(N_REQ)[:, None]
    slot_ids = jnp.arange(REQ_DEV)[None, :]
    base = (device_ids + slot_ids) % N_REQ
    offset = (busiest - device_ids) % N_REQ
    donor = (offset >= REQ_DEV) & (offset < 2 * REQ_DEV)
    labels = jnp.where(donor & (slot_ids == 0), busiest, base)
    relabel = jax.random.permutation(jax.random.fold_in(key, 2), N_REQ).astype(jnp.int32)
    labels = jnp.take(relabel, labels, axis=0)
    device_order = jax.random.permutation(jax.random.fold_in(key, 3), N_REQ).astype(jnp.int32)
    labels = jnp.take(labels, device_order, axis=0)
    return labels.reshape(REQUESTS).astype(jnp.int32)


def steps_of(stream_key, dims, shards, low, largest):
    loudness = 1.0
    for dim, parts in shards:
        draws = jax.random.uniform(jax.random.fold_in(jax.random.fold_in(stream_key, 6), dim), (parts,), jnp.float32, low / len(shards), largest / len(shards))
        loudness = loudness * jnp.repeat(jnp.exp(draws), dims[dim] // parts).reshape((-1,) + (1,) * (len(dims) - 1 - dim))
    return loudness


def scatter_about(stream_key, extent, spread, limit, split=(), kind=jnp.bfloat16):
    entries = jax.random.normal(stream_key, extent, jnp.float32) * spread
    if len(split) > 0:
        entries = steps_of(stream_key, extent, split, -0.22, 0.18) * entries
    return jnp.clip(entries, min=-limit, max=limit).astype(kind)


def setup_inputs(seed: int = 0) -> dict:
    arg_keys = jax.random.split(jax.random.key(seed), 10)
    hidden = draw_hidden(jax.random.fold_in(arg_keys[9], 71), 0)
    norm_gain = jnp.clip(1.0 + 0.1 * jax.random.normal(arg_keys[1], (D,), jnp.float32), 0.5, 1.5)
    w_query = draw_w_query(jax.random.fold_in(arg_keys[9], 71), 0)
    w_kv = draw_w_kv(jax.random.fold_in(arg_keys[9], 71), 0)
    w_out = scatter_about(arg_keys[4], (HEADS * HD, D), (HEADS * HD) ** -0.5, 0.125, ((0, 4),))
    prefix_cache = draw_prefix_cache(jax.random.fold_in(arg_keys[9], 71), 0)
    lengths = draw_lengths(jax.random.fold_in(arg_keys[9], 71), 0)
    groups = draw_groups(jax.random.fold_in(arg_keys[9], 71), 0)
    owners = jax.random.permutation(arg_keys[8], N_REQ).astype(jnp.int32)
    return {"hidden": hidden, "norm_gain": norm_gain, "w_query": w_query, "w_kv": w_kv, "w_out": w_out, "prefix_cache": prefix_cache, "lengths": lengths, "groups": groups, "owners": owners}


EPSILON = 1e-05
ROPE_BASE = 5000000.0

def rope_tables():
    positions = (PREFIX + jnp.arange(SUF)).astype(jnp.float32)
    inverse = ROPE_BASE ** (-(2.0 * jnp.arange(HD // 2).astype(jnp.float32)) / HD)
    angles = positions[:, None] * inverse[None, :]
    cosine_table = jnp.concatenate([jnp.cos(angles), jnp.cos(angles)], axis=-1)
    sine_table = jnp.concatenate([jnp.sin(angles), jnp.sin(angles)], axis=-1)
    return (cosine_table, sine_table)

def rotate(vector, cosine_table, sine_table):
    half_size = vector.shape[-1] // 2
    turned = jnp.concatenate([-vector[..., half_size:], vector[..., :half_size]], axis=-1)
    return vector * cosine_table + turned * sine_table

def soft_part(scores, values_f, form):
    highest = lax.optimization_barrier(jnp.max(scores, axis=-1))
    weights = jnp.exp(scores - highest[..., None])
    totals = lax.optimization_barrier(jnp.sum(weights, axis=-1))
    rounded = lax.optimization_barrier(weights.astype(jnp.bfloat16)).astype(jnp.float32)
    output = jnp.einsum(form, rounded, values_f) / totals[..., None]
    return (output, highest + jnp.log(totals))

def reference(hidden, norm_gain, w_query, w_kv, w_out, prefix_cache, lengths, groups, owners):
    residual = hidden.astype(jnp.float32)
    normed = (residual * lax.rsqrt(lax.optimization_barrier(jnp.mean(residual * residual, axis=-1, keepdims=True)) + EPSILON) * norm_gain).astype(jnp.bfloat16)
    normed_rows = normed.reshape(REQUESTS * SUF, D)
    queries = jnp.dot(normed_rows, w_query, preferred_element_type=jnp.float32).reshape(REQUESTS, SUF, KVH, GROUP, HD)
    key_value = jnp.dot(normed_rows, w_kv.reshape(D, 2 * KVH * HD), preferred_element_type=jnp.float32).reshape(REQUESTS, SUF, 2, KVH, HD)
    cosine_table, sine_table = rope_tables()
    queries = rotate(queries, cosine_table[None, :, None, None, :], sine_table[None, :, None, None, :]).astype(jnp.bfloat16)
    rotated = rotate(key_value[:, :, 0], cosine_table[None, :, None, :], sine_table[None, :, None, :])
    kv_rows = jnp.stack([rotated, key_value[:, :, 1]], axis=2).astype(jnp.bfloat16)
    position_ids = jnp.arange(SUF)
    live_rows = position_ids[None, :] < lengths[:, None]
    suffix_cache = jnp.where(live_rows[:, :, None, None, None], kv_rows, jnp.zeros_like(kv_rows)).reshape(REQUESTS, SUF, 2, KVH * HD)
    slot_ids = lax.optimization_barrier(jnp.sum(jnp.where(groups[:, None] == jnp.arange(N_REQ)[None, :], owners[None, :], 0), axis=-1)).astype(jnp.int32)
    score_scale = HD ** (-0.5)

    def attend(request):
        one_query, one_kv, length, slot = request
        query_f = one_query.astype(jnp.float32)
        block_kv = lax.dynamic_index_in_dim(prefix_cache, slot, 0, keepdims=False).reshape(PREFIX, 2, KVH, HD).astype(jnp.float32)
        prefix_scores = jnp.einsum('tkgd,pkd->tkgp', query_f, block_kv[:, 0]) * score_scale
        prefix_out, prefix_lse = soft_part(prefix_scores, block_kv[:, 1], 'tkgp,pkd->tkgd')
        own_kv = one_kv.astype(jnp.float32)
        suffix_scores = jnp.einsum('tkgd,skd->tkgs', query_f, own_kv[:, 0]) * score_scale
        causal = (position_ids[None, :] <= position_ids[:, None]) & (position_ids[None, :] < length)
        suffix_scores = jnp.where(causal[:, None, None, :], suffix_scores, -jnp.inf)
        suffix_out, suffix_lse = soft_part(suffix_scores, own_kv[:, 1], 'tkgs,skd->tkgd')
        highest = jnp.maximum(prefix_lse, suffix_lse)
        prefix_share = jnp.exp(prefix_lse - highest)
        suffix_share = jnp.exp(suffix_lse - highest)
        mixed_out = (prefix_share[..., None] * prefix_out + suffix_share[..., None] * suffix_out) / (prefix_share + suffix_share)[..., None]
        return mixed_out.astype(jnp.bfloat16)
    attention = lax.map(attend, (queries, kv_rows, lengths, slot_ids))
    attention_rows = attention.reshape(REQUESTS * SUF, KVH, GROUP * HD)
    out_blocks = w_out.reshape(KVH, GROUP * HD, D)
    summed = jnp.zeros((REQUESTS * SUF, D), jnp.float32)
    for kv_head in range(KVH):
        partial_value = jnp.dot(attention_rows[:, kv_head], out_blocks[kv_head], preferred_element_type=jnp.float32).astype(jnp.bfloat16)
        summed = summed + lax.optimization_barrier(partial_value).astype(jnp.float32)
    mixed = residual + summed.reshape(REQUESTS, SUF, D)
    out_hidden = jnp.where(live_rows[:, :, None], mixed, 0.0).astype(jnp.bfloat16)
    return (out_hidden, suffix_cache)
```

```python
import jax
import jax.numpy as jnp
from jax import lax
from jax.sharding import PartitionSpec as P

PREFIX = 2048


EPSILON = 1e-05
ROPE_BASE = 5000000.0


def rope_tables(suffix_len, head_size):
    positions = (PREFIX + jnp.arange(suffix_len)).astype(jnp.float32)
    inverse = ROPE_BASE ** (-(2.0 * jnp.arange(head_size // 2).astype(jnp.float32)) / head_size)
    angles = positions[:, None] * inverse[None, :]
    cosine_table = jnp.concatenate([jnp.cos(angles), jnp.cos(angles)], axis=-1)
    sine_table = jnp.concatenate([jnp.sin(angles), jnp.sin(angles)], axis=-1)
    return (cosine_table, sine_table)


def rotate(vector, cosine_table, sine_table):
    half_size = vector.shape[-1] // 2
    turned = jnp.concatenate([-vector[..., half_size:], vector[..., :half_size]], axis=-1)
    return vector * cosine_table + turned * sine_table


def line_gather(block):
    n = lax.axis_size("tp")
    place = lax.axis_index("tp")
    slots = [(block, place)]
    below, above = block, block
    for step in range(1, n):
        below = lax.ppermute(below, "tp", [(i, i + 1) for i in range(step - 1, n - 1)])
        above = lax.ppermute(above, "tp", [(i, i - 1) for i in range(1, n - step + 1)])
        source_below = jnp.maximum(place - step, 0)
        source_above = jnp.minimum(place + step, n - 1)
        if 2 * step <= n - 1:
            slots.append((below, source_below))
            slots.append((above, source_above))
        else:
            is_below = place >= step
            slots.append(
                (jnp.where(is_below, below, above), jnp.where(is_below, source_below, source_above))
            )
    return slots


def prefix_part(one_query, keys, values):
    score_scale = one_query.shape[-1] ** (-0.5)
    scores = (
        jnp.einsum("tgd,pd->tgp", one_query, keys, preferred_element_type=jnp.float32) * score_scale
    )
    highest = jnp.max(scores, axis=-1)
    weights = jnp.exp(scores - highest[..., None])
    totals = jnp.sum(weights, axis=-1)
    output = (
        jnp.einsum(
            "tgp,pd->tgd", weights.astype(jnp.bfloat16), values, preferred_element_type=jnp.float32
        )
        / totals[..., None]
    )
    return (output, highest + jnp.log(totals))


def shards(hidden, norm_gain, w_query, w_kv, w_out, prefix_cache, lengths, groups, owners):
    n_tp = lax.axis_size("tp")
    n_owners = lax.axis_size("req")
    my_index = lax.axis_index("req")
    req_count, suffix_len, features = hidden.shape
    rows = req_count * suffix_len
    head_size = w_kv.shape[2]
    per_group = w_query.shape[1] // head_size
    model_width = w_query.shape[0]

    share = w_out.shape[0] // n_owners
    my_rows = lax.dynamic_slice_in_dim(w_out, my_index * share, share, axis=0)
    turned = lax.all_to_all(
        jnp.stack([my_rows[:, i * features : (i + 1) * features] for i in range(n_tp)]),
        "tp",
        0,
        0,
        tiled=True,
    )
    w_columns = lax.all_gather(turned, "req", axis=0)

    own_prefix = prefix_cache[0].transpose(1, 0, 2)
    prefixes = lax.all_gather(own_prefix, "req", axis=0)

    flat_kv = w_kv.reshape(model_width, 2 * head_size)
    flat = hidden.reshape(rows, features)
    query_sum = jnp.zeros((rows, per_group * head_size), jnp.float32)
    kv_sum = jnp.zeros((rows, 2 * head_size), jnp.float32)
    square_sum = jnp.zeros((rows, 1), jnp.float32)
    for block, source in line_gather(flat):
        begin = source * features
        gain = lax.dynamic_slice_in_dim(norm_gain, begin, features)
        block_f = block.astype(jnp.float32)
        square_sum = square_sum + jnp.sum(block_f * block_f, axis=-1, keepdims=True)
        scaled = (block_f * gain).astype(jnp.bfloat16)
        query_sum = query_sum + jnp.dot(
            scaled,
            lax.dynamic_slice_in_dim(w_query, begin, features, axis=0),
            preferred_element_type=jnp.float32,
        )
        kv_sum = kv_sum + jnp.dot(
            scaled,
            lax.dynamic_slice_in_dim(flat_kv, begin, features, axis=0),
            preferred_element_type=jnp.float32,
        )
    row_scale = lax.rsqrt(square_sum / model_width + EPSILON)
    queries = (query_sum * row_scale).reshape(req_count, suffix_len, per_group, head_size)
    key_value = (kv_sum * row_scale).reshape(req_count, suffix_len, 2, head_size)

    cosine_table, sine_table = rope_tables(suffix_len, head_size)
    queries = rotate(queries, cosine_table[None, :, None, :], sine_table[None, :, None, :]).astype(
        jnp.bfloat16
    )
    rotated = rotate(key_value[:, :, 0], cosine_table[None], sine_table[None])
    kv_rows = jnp.stack([rotated, key_value[:, :, 1]], axis=2).astype(jnp.bfloat16)
    position_ids = jnp.arange(suffix_len)
    live_rows = position_ids[None, :] < lengths[:, None]
    suffix_cache = jnp.where(live_rows[:, :, None, None], kv_rows, jnp.zeros_like(kv_rows))
    score_scale = head_size ** (-0.5)
    suffix_scores = (
        jnp.einsum("rtgd,rsd->rtgs", queries, kv_rows[:, :, 0], preferred_element_type=jnp.float32)
        * score_scale
    )
    causal = (position_ids[None, None, :] <= position_ids[None, :, None]) & (
        position_ids[None, None, :] < lengths[:, None, None]
    )
    suffix_scores = jnp.where(causal[:, :, None, :], suffix_scores, -jnp.inf)
    suffix_max = jnp.max(suffix_scores, axis=-1)
    suffix_weights = jnp.exp(suffix_scores - suffix_max[..., None])
    suffix_total = jnp.sum(suffix_weights, axis=-1)
    suffix_out = (
        jnp.einsum(
            "rtgs,rsd->rtgd",
            suffix_weights.astype(jnp.bfloat16),
            kv_rows[:, :, 1],
            preferred_element_type=jnp.float32,
        )
        / suffix_total[..., None]
    )
    suffix_lse = suffix_max + jnp.log(suffix_total)

    local_groups = lax.dynamic_slice_in_dim(groups, my_index * req_count, req_count)
    owner_of = jnp.sum(
        jnp.where(local_groups[:, None] == jnp.arange(n_owners)[None, :], owners[None, :], 0), axis=-1
    )
    parts = []
    for r in range(req_count):
        pair = lax.dynamic_index_in_dim(prefixes, owner_of[r], 0, keepdims=False)
        parts.append(prefix_part(queries[r], pair[0], pair[1]))
    prefix_out = jnp.stack([part[0] for part in parts])
    prefix_lse = jnp.stack([part[1] for part in parts])
    highest = jnp.maximum(prefix_lse, suffix_lse)
    prefix_share = jnp.exp(prefix_lse - highest)
    suffix_share = jnp.exp(suffix_lse - highest)
    attention = (
        (prefix_share[..., None] * prefix_out + suffix_share[..., None] * suffix_out)
        / (prefix_share + suffix_share)[..., None]
    ).astype(jnp.bfloat16)

    mixed = hidden.astype(jnp.float32).reshape(rows, features)
    for block, source in line_gather(attention.reshape(rows, per_group * head_size)):
        mixed = mixed + jnp.dot(
            block,
            lax.dynamic_index_in_dim(w_columns, source, 1, keepdims=False).reshape(
                n_owners * share, features
            ),
            preferred_element_type=jnp.float32,
        )
    mixed = mixed.reshape(req_count, suffix_len, features)
    out_hidden = jnp.where(live_rows[:, :, None], mixed, 0.0).astype(jnp.bfloat16)
    return (out_hidden, suffix_cache)


def solution(mesh):
    return jax.shard_map(
        shards,
        mesh=mesh,
        in_specs=(
            P("req", None, "tp"),
            P(),
            P(None, "tp"),
            P(None, None, "tp"),
            P("tp", None),
            P("req", None, None, "tp"),
            P("req"),
            P(),
            P(),
        ),
        out_specs=(P("req", None, "tp"), P("req", None, None, "tp")),
        check_vma=False,
    )
```

```python
import jax
import jax.numpy as jnp
from jax import lax
from jax.sharding import PartitionSpec as P

PREFIX = 2048


EPSILON = 1e-05
ROPE_BASE = 5000000.0


def rope_tables(suffix_len, head_size):
    positions = (PREFIX + jnp.arange(suffix_len)).astype(jnp.float32)
    inverse = ROPE_BASE ** (-(2.0 * jnp.arange(head_size // 2).astype(jnp.float32)) / head_size)
    angles = positions[:, None] * inverse[None, :]
    cosine_table = jnp.concatenate([jnp.cos(angles), jnp.cos(angles)], axis=-1)
    sine_table = jnp.concatenate([jnp.sin(angles), jnp.sin(angles)], axis=-1)
    return (cosine_table, sine_table)


def rotate(vector, cosine_table, sine_table):
    half_size = vector.shape[-1] // 2
    turned = jnp.concatenate([-vector[..., half_size:], vector[..., :half_size]], axis=-1)
    return vector * cosine_table + turned * sine_table


def line_gather(block):
    n = lax.axis_size("tp")
    place = lax.axis_index("tp")
    slots = [(block, place)]
    below, above = block, block
    for step in range(1, n):
        below = lax.ppermute(below, "tp", [(i, i + 1) for i in range(step - 1, n - 1)])
        above = lax.ppermute(above, "tp", [(i, i - 1) for i in range(1, n - step + 1)])
        source_below = jnp.maximum(place - step, 0)
        source_above = jnp.minimum(place + step, n - 1)
        if 2 * step <= n - 1:
            slots.append((below, source_below))
            slots.append((above, source_above))
        else:
            is_below = place >= step
            slots.append(
                (jnp.where(is_below, below, above), jnp.where(is_below, source_below, source_above))
            )
    return slots


def rotate_line(block, j):
    n = lax.axis_size("tp")
    return lax.ppermute(block, "tp", [((i + j) % n, i) for i in range(n)])


def prefix_part(one_query, keys, values):
    score_scale = one_query.shape[-1] ** (-0.5)
    scores = (
        jnp.einsum("tgd,pd->tgp", one_query, keys, preferred_element_type=jnp.float32) * score_scale
    )
    highest = jnp.max(scores, axis=-1)
    weights = jnp.exp(scores - highest[..., None])
    totals = jnp.sum(weights, axis=-1)
    output = (
        jnp.einsum(
            "tgp,pd->tgd", weights.astype(jnp.bfloat16), values, preferred_element_type=jnp.float32
        )
        / totals[..., None]
    )
    return (output, highest + jnp.log(totals))


def shards(hidden, norm_gain, w_query, w_kv, w_out, prefix_cache, lengths, groups, owners):
    n_tp = lax.axis_size("tp")
    n_owners = lax.axis_size("req")
    my_index = lax.axis_index("req")
    req_count, suffix_len, features = hidden.shape
    rows = req_count * suffix_len
    head_size = w_kv.shape[2]
    per_group = w_query.shape[1] // head_size
    model_width = w_query.shape[0]

    own_prefix = prefix_cache[0].transpose(1, 0, 2)
    prefixes = lax.all_gather(own_prefix, "req", axis=0)

    place = lax.axis_index("tp")
    share = w_out.shape[0] // n_owners
    my_rows = lax.dynamic_slice_in_dim(w_out, my_index * share, share, axis=0)
    w_slots = [lax.dynamic_slice_in_dim(w_out, place * features, features, axis=1)]
    for j in range(1, n_tp):
        target = (place - j) % n_tp
        piece = lax.dynamic_slice_in_dim(my_rows, target * features, features, axis=1)
        w_slots.append(lax.all_gather(rotate_line(piece, j), "req", axis=0, tiled=True))

    flat_kv = w_kv.reshape(model_width, 2 * head_size)
    query_sums, kv_sums, square_sums = [], [], []
    chains = [line_gather(hidden[r]) for r in range(req_count)]
    for slots in chains:
        query_sum = jnp.zeros((suffix_len, per_group * head_size), jnp.float32)
        kv_sum = jnp.zeros((suffix_len, 2 * head_size), jnp.float32)
        square_sum = jnp.zeros((suffix_len, 1), jnp.float32)
        for block, source in slots:
            begin = source * features
            gain = lax.dynamic_slice_in_dim(norm_gain, begin, features)
            block_f = block.astype(jnp.float32)
            square_sum = square_sum + jnp.sum(block_f * block_f, axis=-1, keepdims=True)
            scaled = (block_f * gain).astype(jnp.bfloat16)
            query_sum = query_sum + jnp.dot(
                scaled,
                lax.dynamic_slice_in_dim(w_query, begin, features, axis=0),
                preferred_element_type=jnp.float32,
            )
            kv_sum = kv_sum + jnp.dot(
                scaled,
                lax.dynamic_slice_in_dim(flat_kv, begin, features, axis=0),
                preferred_element_type=jnp.float32,
            )
        query_sums.append(query_sum)
        kv_sums.append(kv_sum)
        square_sums.append(square_sum)
    query_sum = jnp.concatenate(query_sums)
    kv_sum = jnp.concatenate(kv_sums)
    square_sum = jnp.concatenate(square_sums)
    row_scale = lax.rsqrt(square_sum / model_width + EPSILON)
    queries = (query_sum * row_scale).reshape(req_count, suffix_len, per_group, head_size)
    key_value = (kv_sum * row_scale).reshape(req_count, suffix_len, 2, head_size)

    cosine_table, sine_table = rope_tables(suffix_len, head_size)
    queries = rotate(queries, cosine_table[None, :, None, :], sine_table[None, :, None, :]).astype(
        jnp.bfloat16
    )
    rotated = rotate(key_value[:, :, 0], cosine_table[None], sine_table[None])
    kv_rows = jnp.stack([rotated, key_value[:, :, 1]], axis=2).astype(jnp.bfloat16)
    position_ids = jnp.arange(suffix_len)
    live_rows = position_ids[None, :] < lengths[:, None]
    suffix_cache = jnp.where(live_rows[:, :, None, None], kv_rows, jnp.zeros_like(kv_rows))
    score_scale = head_size ** (-0.5)
    suffix_scores = (
        jnp.einsum("rtgd,rsd->rtgs", queries, kv_rows[:, :, 0], preferred_element_type=jnp.float32)
        * score_scale
    )
    causal = (position_ids[None, None, :] <= position_ids[None, :, None]) & (
        position_ids[None, None, :] < lengths[:, None, None]
    )
    suffix_scores = jnp.where(causal[:, :, None, :], suffix_scores, -jnp.inf)
    suffix_max = jnp.max(suffix_scores, axis=-1)
    suffix_weights = jnp.exp(suffix_scores - suffix_max[..., None])
    suffix_total = jnp.sum(suffix_weights, axis=-1)
    suffix_out = (
        jnp.einsum(
            "rtgs,rsd->rtgd",
            suffix_weights.astype(jnp.bfloat16),
            kv_rows[:, :, 1],
            preferred_element_type=jnp.float32,
        )
        / suffix_total[..., None]
    )
    suffix_lse = suffix_max + jnp.log(suffix_total)

    local_groups = lax.dynamic_slice_in_dim(groups, my_index * req_count, req_count)
    owner_of = jnp.sum(
        jnp.where(local_groups[:, None] == jnp.arange(n_owners)[None, :], owners[None, :], 0), axis=-1
    )
    gathered = []
    for r in range(req_count):
        pair = lax.dynamic_index_in_dim(prefixes, owner_of[r], 0, keepdims=False)
        prefix_out, prefix_lse = prefix_part(queries[r], pair[0], pair[1])
        highest = jnp.maximum(prefix_lse, suffix_lse[r])
        prefix_share = jnp.exp(prefix_lse - highest)
        suffix_share = jnp.exp(suffix_lse[r] - highest)
        attention = (
            (prefix_share[..., None] * prefix_out + suffix_share[..., None] * suffix_out[r])
            / (prefix_share + suffix_share)[..., None]
        ).astype(jnp.bfloat16)
        attention = attention.reshape(suffix_len, per_group * head_size)
        gathered.append([attention] + [rotate_line(attention, j) for j in range(1, n_tp)])

    mixed = hidden.astype(jnp.float32).reshape(rows, features)
    for j in range(n_tp):
        block = jnp.concatenate([slots[j] for slots in gathered])
        mixed = mixed + jnp.dot(block, w_slots[j], preferred_element_type=jnp.float32)
    mixed = mixed.reshape(req_count, suffix_len, features)
    out_hidden = jnp.where(live_rows[:, :, None], mixed, 0.0).astype(jnp.bfloat16)
    return (out_hidden, suffix_cache)


def solution(mesh):
    return jax.shard_map(
        shards,
        mesh=mesh,
        in_specs=(
            P("req", None, "tp"),
            P(),
            P(None, "tp"),
            P(None, None, "tp"),
            P("tp", None),
            P("req", None, None, "tp"),
            P("req"),
            P(),
            P(),
        ),
        out_specs=(P("req", None, "tp"), P("req", None, None, "tp")),
        check_vma=False,
    )
```

```python
import functools

import jax
import jax.numpy as jnp
from jax import lax
from jax.experimental import pallas as pl
from jax.experimental.pallas import tpu as pltpu
from jax.sharding import PartitionSpec as P

PREFIX = 2048


EPSILON = 1e-05
ROPE_BASE = 5000000.0
VMEM_BYTES = 40 * 1024 * 1024
LANES = 128


def rope_tables(suffix_len, head_size):
    positions = (PREFIX + jnp.arange(suffix_len)).astype(jnp.float32)
    inverse = ROPE_BASE ** (-(2.0 * jnp.arange(head_size // 2).astype(jnp.float32)) / head_size)
    angles = positions[:, None] * inverse[None, :]
    cosine_table = jnp.concatenate([jnp.cos(angles), jnp.cos(angles)], axis=-1)
    sine_table = jnp.concatenate([-jnp.sin(angles), jnp.sin(angles)], axis=-1)
    return (cosine_table, sine_table)


def line_steps(block):
    n = lax.axis_size("tp")
    below, above = block, block
    steps = []
    for step in range(1, n):
        below = lax.ppermute(below, "tp", [(i, i + 1) for i in range(step - 1, n - 1)])
        above = lax.ppermute(above, "tp", [(i, i - 1) for i in range(1, n - step + 1)])
        steps.append((below, above))
    return steps


def rotate_line(block, j):
    n = lax.axis_size("tp")
    return lax.ppermute(block, "tp", [((i + j) % n, i) for i in range(n)])


def project_kernel(n_blocks, first, source_ref, *refs):
    blocks, rest = refs[:n_blocks], refs[n_blocks:]
    gain_ref, wq_ref, wkv_ref = rest[:3]
    sums_in, sums = rest[3:-3], rest[-3:]
    block_f = blocks[0][...].astype(jnp.float32)
    for other in blocks[1:]:
        block_f = block_f + other[...].astype(jnp.float32)
    scaled = (block_f * gain_ref[...]).astype(jnp.bfloat16)
    squares = block_f * block_f
    square = squares[:, :LANES]
    for i in range(1, squares.shape[1] // LANES):
        square = square + squares[:, i * LANES : (i + 1) * LANES]
    parts = (
        jnp.dot(scaled, wq_ref[...], preferred_element_type=jnp.float32),
        jnp.dot(scaled, wkv_ref[...], preferred_element_type=jnp.float32),
        square,
    )

    @pl.when(pl.program_id(0) == 0)
    def _():
        for i in range(3):
            sums[i][...] = parts[i] if first else sums_in[i][...] + parts[i]

    @pl.when(pl.program_id(0) > 0)
    def _():
        for i in range(3):
            sums[i][...] += parts[i]


def project(blocks, source, gain, w_query, flat_kv, sums):
    rows, features = blocks[0].shape
    chunk = features // 2 if features % (2 * LANES) == 0 else features
    steps = features // chunk
    widths = (w_query.shape[1], flat_kv.shape[1], LANES)
    first = sums is None

    def by_source(k, source_ref):
        return (source_ref[0] * steps + k, 0)

    def whole(k, source_ref):
        return (0, 0)

    sum_specs = [pl.BlockSpec((rows, width), whole) for width in widths]
    return pl.pallas_call(
        functools.partial(project_kernel, len(blocks), first),
        grid_spec=pltpu.PrefetchScalarGridSpec(
            num_scalar_prefetch=1,
            grid=(steps,),
            in_specs=[pl.BlockSpec((rows, chunk), lambda k, source_ref: (0, k)) for _ in blocks]
            + [
                pl.BlockSpec((1, chunk), lambda k, source_ref: (0, source_ref[0] * steps + k)),
                pl.BlockSpec((chunk, widths[0]), by_source),
                pl.BlockSpec((chunk, widths[1]), by_source),
            ]
            + ([] if first else sum_specs),
            out_specs=sum_specs,
        ),
        out_shape=[jax.ShapeDtypeStruct((rows, width), jnp.float32) for width in widths],
        compiler_params=pltpu.CompilerParams(vmem_limit_bytes=VMEM_BYTES),
        cost_estimate=pl.CostEstimate(
            flops=2 * rows * features * (widths[0] + widths[1]),
            bytes_accessed=2 * features * (widths[0] + widths[1] + rows),
            transcendentals=0,
        ),
    )(source.reshape(1).astype(jnp.int32), *blocks, gain, w_query, flat_kv, *([] if first else sums))


def attend_kernel(
    r, model_width, owner_ref, length_ref, q_ref, kv_ref, square_ref, cos_ref, sin_ref, pair_ref, att_ref, cache_ref
):
    rows = q_ref.shape[0]
    head_size = pair_ref.shape[-1]
    heads = q_ref.shape[1] // head_size
    per_dot = 2 if heads % 2 == 0 else 1
    scale = head_size ** (-0.5)
    length = length_ref[r]
    cosine, sine = cos_ref[...], sin_ref[...]
    mean = jnp.sum(square_ref[...], axis=-1, keepdims=True) / model_width
    row_scale = lax.rsqrt(mean + EPSILON)

    def turn(vector):
        vector = vector * row_scale
        return vector * cosine + pltpu.roll(vector, head_size // 2, 1) * sine

    keys_f = turn(kv_ref[:, :head_size])
    values_f = kv_ref[:, head_size:] * row_scale
    live = lax.broadcasted_iota(jnp.int32, (rows, head_size), 0) < length
    cache_ref[:, :head_size] = jnp.where(live, keys_f, 0.0).astype(jnp.bfloat16)
    cache_ref[:, head_size:] = jnp.where(live, values_f, 0.0).astype(jnp.bfloat16)
    own_keys, own_values = keys_f.astype(jnp.bfloat16), values_f.astype(jnp.bfloat16)

    position = lax.broadcasted_iota(jnp.int32, (per_dot * rows, rows), 0) % rows
    other = lax.broadcasted_iota(jnp.int32, (per_dot * rows, rows), 1)
    causal = (other <= position) & (other < length)
    against = (((1,), (1,)), ((), ()))
    for g in range(0, heads, per_dot):
        query = jnp.concatenate(
            [turn(q_ref[:, (g + i) * head_size : (g + i + 1) * head_size]) for i in range(per_dot)]
        ).astype(jnp.bfloat16)
        scores = lax.dot_general(query, pair_ref[0, 0], against, preferred_element_type=jnp.float32)
        own_scores = lax.dot_general(query, own_keys, against, preferred_element_type=jnp.float32)
        own_scores = jnp.where(causal, own_scores, -jnp.inf)
        highest = jnp.maximum(
            jnp.max(scores, axis=-1, keepdims=True), jnp.max(own_scores, axis=-1, keepdims=True)
        )
        weights = jnp.exp((scores - highest) * scale)
        own_weights = jnp.exp((own_scores - highest) * scale)
        total = jnp.sum(weights, axis=-1, keepdims=True) + jnp.sum(own_weights, axis=-1, keepdims=True)
        mixed = jnp.dot(weights.astype(jnp.bfloat16), pair_ref[0, 1], preferred_element_type=jnp.float32)
        mixed = mixed + jnp.dot(
            own_weights.astype(jnp.bfloat16), own_values, preferred_element_type=jnp.float32
        )
        mixed = (mixed / total).astype(jnp.bfloat16)
        for i in range(per_dot):
            att_ref[:, (g + i) * head_size : (g + i + 1) * head_size] = mixed[i * rows : (i + 1) * rows]


def attend(r, suffix_len, model_width, owner_of, lengths, sums, tables, prefixes):
    q_sum, kv_sum, square_sum = sums
    head_size = prefixes.shape[-1]
    prefix_len = prefixes.shape[2]
    width = q_sum.shape[1]

    def by_request(k, owner_ref, length_ref):
        return (r, 0)

    def whole(k, owner_ref, length_ref):
        return (0, 0)

    return pl.pallas_call(
        functools.partial(attend_kernel, r, model_width),
        grid_spec=pltpu.PrefetchScalarGridSpec(
            num_scalar_prefetch=2,
            grid=(1,),
            in_specs=[
                pl.BlockSpec((suffix_len, width), by_request),
                pl.BlockSpec((suffix_len, kv_sum.shape[1]), by_request),
                pl.BlockSpec((suffix_len, LANES), by_request),
                pl.BlockSpec((suffix_len, head_size), whole),
                pl.BlockSpec((suffix_len, head_size), whole),
                pl.BlockSpec(
                    (1, 2, prefix_len, head_size),
                    lambda k, owner_ref, length_ref: (owner_ref[r], 0, 0, 0),
                ),
            ],
            out_specs=[
                pl.BlockSpec((suffix_len, width), whole),
                pl.BlockSpec((suffix_len, kv_sum.shape[1]), whole),
            ],
        ),
        out_shape=[
            jax.ShapeDtypeStruct((suffix_len, width), jnp.bfloat16),
            jax.ShapeDtypeStruct((suffix_len, kv_sum.shape[1]), jnp.bfloat16),
        ],
        compiler_params=pltpu.CompilerParams(vmem_limit_bytes=VMEM_BYTES),
        cost_estimate=pl.CostEstimate(
            flops=4 * suffix_len * width * (prefix_len + suffix_len),
            bytes_accessed=4 * prefix_len * head_size + 4 * suffix_len * (width + 2 * head_size),
            transcendentals=suffix_len * width // head_size * prefix_len,
        ),
    )(owner_of, lengths, q_sum, kv_sum, square_sum, *tables, prefixes)


def output_kernel(req_count, n_tp, place_ref, length_ref, *refs):
    attention, rest = refs[: n_tp * req_count], refs[n_tp * req_count :]
    own_ref, others, hidden_ref, out_ref = rest[0], rest[1:n_tp], rest[n_tp], rest[n_tp + 1]
    suffix_len = hidden_ref.shape[1]
    mixed = None
    for j in range(n_tp):
        block = jnp.concatenate([attention[j * req_count + r][...] for r in range(req_count)])
        if j == 0:
            weights = own_ref[...]
        else:
            weights = others[j - 1][...].reshape(own_ref.shape)
        part = jnp.dot(block, weights, preferred_element_type=jnp.float32)
        mixed = part if mixed is None else mixed + part
    position = lax.broadcasted_iota(jnp.int32, (suffix_len, out_ref.shape[2]), 0)
    for r in range(req_count):
        part = mixed[r * suffix_len : (r + 1) * suffix_len] + hidden_ref[r].astype(jnp.float32)
        out_ref[r] = jnp.where(position < length_ref[r], part, 0.0).astype(jnp.bfloat16)


def project_out(place, lengths, attention, w_out, w_others, hidden):
    req_count, suffix_len, features = hidden.shape
    n_tp = len(attention)
    n_owners, _, share, _ = w_others.shape
    chunk = 256 if features % 256 == 0 else LANES
    steps = features // chunk
    depth = w_out.shape[0]

    def other_spec(j):
        return pl.BlockSpec(
            (n_owners, 1, share, chunk), lambda k, place_ref, length_ref: (0, j, 0, k)
        )

    def by_column(k, place_ref, length_ref):
        return (0, 0, k)

    return pl.pallas_call(
        functools.partial(output_kernel, req_count, n_tp),
        grid_spec=pltpu.PrefetchScalarGridSpec(
            num_scalar_prefetch=2,
            grid=(steps,),
            in_specs=[
                pl.BlockSpec((suffix_len, depth), lambda k, place_ref, length_ref: (0, 0))
                for _ in range(n_tp * req_count)
            ]
            + [pl.BlockSpec((depth, chunk), lambda k, place_ref, length_ref: (0, place_ref[0] * steps + k))]
            + [other_spec(j) for j in range(n_tp - 1)]
            + [pl.BlockSpec((req_count, suffix_len, chunk), by_column)],
            out_specs=pl.BlockSpec((req_count, suffix_len, chunk), by_column),
        ),
        out_shape=jax.ShapeDtypeStruct(hidden.shape, jnp.bfloat16),
        compiler_params=pltpu.CompilerParams(vmem_limit_bytes=VMEM_BYTES),
        cost_estimate=pl.CostEstimate(
            flops=2 * req_count * suffix_len * features * depth * n_tp,
            bytes_accessed=2 * features * (depth * n_tp + 2 * req_count * suffix_len),
            transcendentals=0,
        ),
    )(
        place.reshape(1).astype(jnp.int32),
        lengths,
        *[block for slot in attention for block in slot],
        w_out,
        *[w_others] * (n_tp - 1),
        hidden,
    )


def shards(hidden, norm_gain, w_query, w_kv, w_out, prefix_cache, lengths, groups, owners):
    n_tp = lax.axis_size("tp")
    n_owners = lax.axis_size("req")
    my_index = lax.axis_index("req")
    place = lax.axis_index("tp")
    req_count, suffix_len, features = hidden.shape
    rows = req_count * suffix_len
    head_size = w_kv.shape[2]
    model_width = w_query.shape[0]

    own_prefix = prefix_cache[0].transpose(1, 0, 2)
    prefixes = lax.all_gather(own_prefix, "req", axis=0)
    local_groups = lax.dynamic_slice_in_dim(groups, my_index * req_count, req_count)
    owner_of = jnp.sum(
        jnp.where(local_groups[:, None] == jnp.arange(n_owners)[None, :], owners[None, :], 0), axis=-1
    ).astype(jnp.int32)

    flat = hidden.reshape(rows, features)
    steps = line_steps(flat)

    share = w_out.shape[0] // n_owners
    my_rows = lax.dynamic_slice_in_dim(w_out, my_index * share, share, axis=0)
    pieces = []
    for j in range(1, n_tp):
        target = (place - j) % n_tp
        pieces.append(lax.dynamic_slice_in_dim(my_rows, target * features, features, axis=1))
    moved = jnp.stack([rotate_line(pieces[j - 1], j) for j in range(1, n_tp)])
    moved, _ = lax.optimization_barrier((moved, steps[-2]))
    w_others = lax.all_gather(moved, "req", axis=0)

    flat_kv = w_kv.reshape(model_width, 2 * head_size)
    gain = norm_gain.reshape(1, model_width)
    sums = project([flat], place, gain, w_query, flat_kv, None)
    for step, (below, above) in enumerate(steps, 1):
        source_below = jnp.maximum(place - step, 0)
        source_above = jnp.minimum(place + step, n_tp - 1)
        if 2 * step <= n_tp - 1:
            sums = project([below], source_below, gain, w_query, flat_kv, sums)
            sums = project([above], source_above, gain, w_query, flat_kv, sums)
        else:
            source = jnp.where(place >= step, source_below, source_above)
            sums = project([below, above], source, gain, w_query, flat_kv, sums)

    tables = rope_tables(suffix_len, head_size)
    caches, gathered = [], []
    for r in range(req_count):
        attention, cache = attend(
            r, suffix_len, model_width, owner_of, lengths, sums, tables, prefixes
        )
        caches.append(cache)
        gathered.append([attention] + [rotate_line(attention, j) for j in range(1, n_tp)])
    suffix_cache = jnp.stack(caches).reshape(req_count, suffix_len, 2, head_size)
    slots = [[chain[j] for chain in gathered] for j in range(n_tp)]
    out_hidden = project_out(place, lengths, slots, w_out, w_others, hidden)
    return (out_hidden, suffix_cache)


def solution(mesh):
    return jax.shard_map(
        shards,
        mesh=mesh,
        in_specs=(
            P("req", None, "tp"),
            P(),
            P(None, "tp"),
            P(None, None, "tp"),
            P("tp", None),
            P("req", None, None, "tp"),
            P("req"),
            P(),
            P(),
        ),
        out_specs=(P("req", None, "tp"), P("req", None, None, "tp")),
        check_vma=False,
    )
```

```python
import functools

import jax
import jax.numpy as jnp
from jax import lax
from jax.experimental import pallas as pl
from jax.experimental.pallas import tpu as pltpu
from jax.sharding import PartitionSpec as P

PREFIX = 2048


EPSILON = 1e-05
ROPE_BASE = 5000000.0
VMEM_BYTES = 40 * 1024 * 1024
OUTPUT_VMEM_BYTES = 24 * 1024 * 1024
LANES = 128


def rope_tables(suffix_len, head_size):
    positions = (PREFIX + jnp.arange(suffix_len)).astype(jnp.float32)
    inverse = ROPE_BASE ** (-(2.0 * jnp.arange(head_size // 2).astype(jnp.float32)) / head_size)
    angles = positions[:, None] * inverse[None, :]
    cosine_table = jnp.concatenate([jnp.cos(angles), jnp.cos(angles)], axis=-1)
    sine_table = jnp.concatenate([-jnp.sin(angles), jnp.sin(angles)], axis=-1)
    return (cosine_table, sine_table)


def ring_order(n):
    return [0] + list(range(1, n, 2)) + list(range(n - 2 if n % 2 == 0 else n - 1, 0, -2))


def ring_place(distance):
    n = lax.axis_size("tp")
    ring = ring_order(n)
    place = lax.axis_index("tp")
    return sum(jnp.where(place == ring[p], ring[(p + distance) % n], 0) for p in range(n))


def shift(block, distance):
    n = lax.axis_size("tp")
    ring = ring_order(n)
    return lax.ppermute(block, "tp", [(ring[p], ring[(p + distance) % n]) for p in range(n)])


def project_kernel(first, source_ref, block_ref, gain_ref, wq_ref, wkv_ref, *refs):
    sums_in, sums = refs[:-3], refs[-3:]
    block_f = block_ref[...].astype(jnp.float32)
    scaled = (block_f * gain_ref[...]).astype(jnp.bfloat16)
    squares = block_f * block_f
    square = squares[:, :LANES]
    for i in range(1, squares.shape[1] // LANES):
        square = square + squares[:, i * LANES : (i + 1) * LANES]
    parts = (
        jnp.dot(scaled, wq_ref[...], preferred_element_type=jnp.float32),
        jnp.dot(scaled, wkv_ref[...], preferred_element_type=jnp.float32),
        square,
    )

    @pl.when(pl.program_id(0) == 0)
    def _():
        for i in range(3):
            sums[i][...] = parts[i] if first else sums_in[i][...] + parts[i]

    @pl.when(pl.program_id(0) > 0)
    def _():
        for i in range(3):
            sums[i][...] += parts[i]


def project(block, source, gain, w_query, flat_kv, sums):
    rows, features = block.shape
    chunk = features // 2 if features % (2 * LANES) == 0 else features
    steps = features // chunk
    widths = (w_query.shape[1], flat_kv.shape[1], LANES)
    first = sums is None

    def by_source(k, source_ref):
        return (source_ref[0] * steps + k, 0)

    def whole(k, source_ref):
        return (0, 0)

    sum_specs = [pl.BlockSpec((rows, width), whole) for width in widths]
    return pl.pallas_call(
        functools.partial(project_kernel, first),
        grid_spec=pltpu.PrefetchScalarGridSpec(
            num_scalar_prefetch=1,
            grid=(steps,),
            in_specs=[
                pl.BlockSpec((rows, chunk), lambda k, source_ref: (0, k)),
                pl.BlockSpec((1, chunk), lambda k, source_ref: (0, source_ref[0] * steps + k)),
                pl.BlockSpec((chunk, widths[0]), by_source),
                pl.BlockSpec((chunk, widths[1]), by_source),
            ]
            + ([] if first else sum_specs),
            out_specs=sum_specs,
        ),
        out_shape=[jax.ShapeDtypeStruct((rows, width), jnp.float32) for width in widths],
        compiler_params=pltpu.CompilerParams(vmem_limit_bytes=VMEM_BYTES),
        cost_estimate=pl.CostEstimate(
            flops=2 * rows * features * (widths[0] + widths[1]),
            bytes_accessed=2 * features * (widths[0] + widths[1] + rows),
            transcendentals=0,
        ),
    )(source.reshape(1).astype(jnp.int32), block, gain, w_query, flat_kv, *([] if first else sums))


def attend_kernel(
    r, model_width, length_ref, q_ref, kv_ref, square_ref, cos_ref, sin_ref, pair_ref, att_ref, cache_ref
):
    rows = q_ref.shape[0]
    head_size = pair_ref.shape[-1]
    heads = q_ref.shape[1] // head_size
    per_dot = 2 if heads % 2 == 0 else 1
    scale = head_size ** (-0.5)
    length = length_ref[r]
    cosine, sine = cos_ref[...], sin_ref[...]
    mean = jnp.sum(square_ref[...], axis=-1, keepdims=True) / model_width
    row_scale = lax.rsqrt(mean + EPSILON)

    def turn(vector):
        vector = vector * row_scale
        return vector * cosine + pltpu.roll(vector, head_size // 2, 1) * sine

    keys_f = turn(kv_ref[:, :head_size])
    values_f = kv_ref[:, head_size:] * row_scale
    live = lax.broadcasted_iota(jnp.int32, (rows, head_size), 0) < length
    cache_ref[:, :head_size] = jnp.where(live, keys_f, 0.0).astype(jnp.bfloat16)
    cache_ref[:, head_size:] = jnp.where(live, values_f, 0.0).astype(jnp.bfloat16)
    own_keys, own_values = keys_f.astype(jnp.bfloat16), values_f.astype(jnp.bfloat16)

    position = lax.broadcasted_iota(jnp.int32, (per_dot * rows, rows), 0) % rows
    other = lax.broadcasted_iota(jnp.int32, (per_dot * rows, rows), 1)
    causal = (other <= position) & (other < length)
    against = (((1,), (1,)), ((), ()))
    for g in range(0, heads, per_dot):
        query = jnp.concatenate(
            [turn(q_ref[:, (g + i) * head_size : (g + i + 1) * head_size]) for i in range(per_dot)]
        ).astype(jnp.bfloat16)
        scores = lax.dot_general(query, pair_ref[0], against, preferred_element_type=jnp.float32)
        own_scores = lax.dot_general(query, own_keys, against, preferred_element_type=jnp.float32)
        own_scores = jnp.where(causal, own_scores, -jnp.inf)
        highest = jnp.maximum(
            jnp.max(scores, axis=-1, keepdims=True), jnp.max(own_scores, axis=-1, keepdims=True)
        )
        weights = jnp.exp((scores - highest) * scale)
        own_weights = jnp.exp((own_scores - highest) * scale)
        total = jnp.sum(weights, axis=-1, keepdims=True) + jnp.sum(own_weights, axis=-1, keepdims=True)
        mixed = jnp.dot(weights.astype(jnp.bfloat16), pair_ref[1], preferred_element_type=jnp.float32)
        mixed = mixed + jnp.dot(
            own_weights.astype(jnp.bfloat16), own_values, preferred_element_type=jnp.float32
        )
        mixed = (mixed / total).astype(jnp.bfloat16)
        for i in range(per_dot):
            att_ref[:, (g + i) * head_size : (g + i + 1) * head_size] = mixed[i * rows : (i + 1) * rows]


def attend(r, suffix_len, model_width, lengths, sums, tables, pair):
    q_sum, kv_sum, square_sum = sums
    _, prefix_len, head_size = pair.shape
    width = q_sum.shape[1]

    def by_request(k, length_ref):
        return (r, 0)

    def whole(k, length_ref):
        return (0, 0)

    return pl.pallas_call(
        functools.partial(attend_kernel, r, model_width),
        grid_spec=pltpu.PrefetchScalarGridSpec(
            num_scalar_prefetch=1,
            grid=(1,),
            in_specs=[
                pl.BlockSpec((suffix_len, width), by_request),
                pl.BlockSpec((suffix_len, kv_sum.shape[1]), by_request),
                pl.BlockSpec((suffix_len, LANES), by_request),
                pl.BlockSpec((suffix_len, head_size), whole),
                pl.BlockSpec((suffix_len, head_size), whole),
                pl.BlockSpec((2, prefix_len, head_size), lambda k, length_ref: (0, 0, 0)),
            ],
            out_specs=[
                pl.BlockSpec((suffix_len, width), whole),
                pl.BlockSpec((suffix_len, kv_sum.shape[1]), whole),
            ],
        ),
        out_shape=[
            jax.ShapeDtypeStruct((suffix_len, width), jnp.bfloat16),
            jax.ShapeDtypeStruct((suffix_len, kv_sum.shape[1]), jnp.bfloat16),
        ],
        compiler_params=pltpu.CompilerParams(vmem_limit_bytes=VMEM_BYTES),
        cost_estimate=pl.CostEstimate(
            flops=4 * suffix_len * width * (prefix_len + suffix_len),
            bytes_accessed=4 * prefix_len * head_size + 4 * suffix_len * (width + 2 * head_size),
            transcendentals=suffix_len * width // head_size * prefix_len,
        ),
    )(lengths, q_sum, kv_sum, square_sum, *tables, pair)


def output_kernel(n_tp, length_ref, *refs):
    own_ref, others_ref, hidden_ref, out_ref = refs[-4:]
    req_count, suffix_len, features = hidden_ref.shape
    chunk = 2 * LANES if features % (2 * LANES) == 0 else LANES
    position = lax.broadcasted_iota(jnp.int32, (suffix_len, chunk), 0)
    attention = [
        jnp.concatenate([refs[r * n_tp + j][...] for r in range(req_count)]) for j in range(n_tp)
    ]
    for begin in range(0, features, chunk):
        columns = slice(begin, begin + chunk)
        mixed = jnp.dot(attention[0], own_ref[:, columns], preferred_element_type=jnp.float32)
        for j in range(1, n_tp):
            weights = others_ref[:, j - 1, :, columns].reshape(own_ref.shape[0], chunk)
            mixed = mixed + jnp.dot(attention[j], weights, preferred_element_type=jnp.float32)
        for r in range(req_count):
            part = mixed[r * suffix_len : (r + 1) * suffix_len]
            part = part + hidden_ref[r, :, columns].astype(jnp.float32)
            part = jnp.where(position < length_ref[r], part, 0.0)
            out_ref[r, :, columns] = part.astype(jnp.bfloat16)


def project_out(lengths, attention, w_own, w_others, hidden):
    req_count, suffix_len, features = hidden.shape
    n_tp = len(attention[0])
    vmem = pl.BlockSpec(memory_space=pltpu.VMEM)
    return pl.pallas_call(
        functools.partial(output_kernel, n_tp),
        in_specs=[pl.BlockSpec(memory_space=pltpu.SMEM)] + [vmem] * (req_count * n_tp + 3),
        out_specs=vmem,
        out_shape=jax.ShapeDtypeStruct(hidden.shape, jnp.bfloat16),
        compiler_params=pltpu.CompilerParams(vmem_limit_bytes=OUTPUT_VMEM_BYTES),
        cost_estimate=pl.CostEstimate(
            flops=2 * req_count * suffix_len * features * w_own.shape[0] * n_tp,
            bytes_accessed=2 * features * (w_own.shape[0] * n_tp + 2 * req_count * suffix_len),
            transcendentals=0,
        ),
    )(lengths, *[block for slots in attention for block in slots], w_own, w_others, hidden)


def shards(hidden, norm_gain, w_query, w_kv, w_out, prefix_cache, lengths, groups, owners):
    n_tp = lax.axis_size("tp")
    n_owners = lax.axis_size("req")
    my_index = lax.axis_index("req")
    place = lax.axis_index("tp")
    req_count, suffix_len, features = hidden.shape
    head_size = w_kv.shape[2]
    model_width = w_query.shape[0]

    flat_kv = w_kv.reshape(model_width, 2 * head_size)
    gain = norm_gain.reshape(1, model_width)
    tables = rope_tables(suffix_len, head_size)

    share = w_out.shape[0] // n_owners
    my_rows = lax.dynamic_slice_in_dim(w_out, my_index * share, share, axis=0)
    moved = []
    for j in range(1, n_tp):
        piece = lax.dynamic_slice_in_dim(my_rows, ring_place(j) * features, features, axis=1)
        moved.append(shift(piece, j))
    w_own = lax.dynamic_slice_in_dim(w_out, place * features, features, axis=1)

    prefixes = lax.all_gather(prefix_cache[0], "req", axis=0)
    local_groups = lax.dynamic_slice_in_dim(groups, my_index * req_count, req_count)
    owner_of = jnp.sum(
        jnp.where(local_groups[:, None] == jnp.arange(n_owners)[None, :], owners[None, :], 0), axis=-1
    ).astype(jnp.int32)

    block = hidden.reshape(req_count * suffix_len, features)
    sums = None
    for step in range(n_tp):
        coming = shift(block, 1) if step < n_tp - 1 else block
        sums = project(block, ring_place(-step), gain, w_query, flat_kv, sums)
        if step == 0:
            coming, sums, moved = lax.optimization_barrier((coming, sums, moved))
            w_others = lax.all_gather(jnp.stack(moved), "req", axis=0)
        elif step < n_tp - 2:
            coming, sums = lax.optimization_barrier((coming, sums))
        elif step == n_tp - 2:
            pairs = [
                lax.dynamic_index_in_dim(prefixes, owner_of[r], 0, keepdims=False).transpose(1, 0, 2)
                for r in range(req_count)
            ]
            coming, sums, pairs, tables, w_own = lax.optimization_barrier(
                (coming, sums, pairs, tables, w_own)
            )
        block = coming

    caches, gathered = [], []
    for r in range(req_count):
        attention, cache = attend(r, suffix_len, model_width, lengths, sums, tables, pairs[r])
        caches.append(cache)
        gathered.append([attention] + [shift(attention, j) for j in range(1, n_tp)])

    suffix_cache = jnp.stack(caches).reshape(req_count, suffix_len, 2, head_size)
    out_hidden = project_out(lengths, gathered, w_own, w_others, hidden)
    return (out_hidden, suffix_cache)


def solution(mesh):
    return jax.shard_map(
        shards,
        mesh=mesh,
        in_specs=(
            P("req", None, "tp"),
            P(),
            P(None, "tp"),
            P(None, None, "tp"),
            P("tp", None),
            P("req", None, None, "tp"),
            P("req"),
            P(),
            P(),
        ),
        out_specs=(P("req", None, "tp"), P("req", None, None, "tp")),
        check_vma=False,
    )
```

```python
import functools

import jax
import jax.numpy as jnp
from jax import lax
from jax.experimental import pallas as pl
from jax.experimental.pallas import tpu as pltpu
from jax.sharding import PartitionSpec as P

PREFIX = 2048


EPSILON = 1e-05
ROPE_BASE = 5000000.0
PROJECT_VMEM_BYTES = 12 * 1024 * 1024
VMEM_BYTES = 16 * 1024 * 1024
OUTPUT_VMEM_BYTES = 16 * 1024 * 1024
LANES = 128


def rope_tables(suffix_len, head_size):
    positions = (PREFIX + jnp.arange(suffix_len)).astype(jnp.float32)
    inverse = ROPE_BASE ** (-(2.0 * jnp.arange(head_size // 2).astype(jnp.float32)) / head_size)
    angles = positions[:, None] * inverse[None, :]
    cosine_table = jnp.concatenate([jnp.cos(angles), jnp.cos(angles)], axis=-1)
    sine_table = jnp.concatenate([-jnp.sin(angles), jnp.sin(angles)], axis=-1)
    return (cosine_table, sine_table)


def ring_order(n):
    return [0] + list(range(1, n, 2)) + list(range(n - 2 if n % 2 == 0 else n - 1, 0, -2))


def ring_place(distance):
    n = lax.axis_size("tp")
    ring = ring_order(n)
    place = lax.axis_index("tp")
    return sum(jnp.where(place == ring[p], ring[(p + distance) % n], 0) for p in range(n))


def shift(block, distance):
    n = lax.axis_size("tp")
    ring = ring_order(n)
    return lax.ppermute(block, "tp", [(ring[p], ring[(p + distance) % n]) for p in range(n)])


def project_kernel(first, source_ref, block_ref, gain_ref, wq_ref, wkv_ref, *refs):
    sums_in, sums = refs[:-3], refs[-3:]
    block_f = block_ref[...].astype(jnp.float32)
    scaled = (block_f * gain_ref[...]).astype(jnp.bfloat16)
    squares = block_f * block_f
    square = squares[:, :LANES]
    for i in range(1, squares.shape[1] // LANES):
        square = square + squares[:, i * LANES : (i + 1) * LANES]
    parts = (
        jnp.dot(scaled, wq_ref[...], preferred_element_type=jnp.float32),
        jnp.dot(scaled, wkv_ref[...], preferred_element_type=jnp.float32),
        square,
    )

    @pl.when(pl.program_id(0) == 0)
    def _():
        for i in range(3):
            sums[i][...] = parts[i] if first else sums_in[i][...] + parts[i]

    @pl.when(pl.program_id(0) > 0)
    def _():
        for i in range(3):
            sums[i][...] += parts[i]


def project(block, source, gain, w_query, flat_kv, sums):
    rows, features = block.shape
    chunk = features // 2 if features % (2 * LANES) == 0 else features
    steps = features // chunk
    widths = (w_query.shape[1], flat_kv.shape[1], LANES)
    first = sums is None

    def by_source(k, source_ref):
        return (source_ref[0] * steps + k, 0)

    def whole(k, source_ref):
        return (0, 0)

    sum_specs = [pl.BlockSpec((rows, width), whole) for width in widths]
    return pl.pallas_call(
        functools.partial(project_kernel, first),
        grid_spec=pltpu.PrefetchScalarGridSpec(
            num_scalar_prefetch=1,
            grid=(steps,),
            in_specs=[
                pl.BlockSpec((rows, chunk), lambda k, source_ref: (0, k)),
                pl.BlockSpec((1, chunk), lambda k, source_ref: (0, source_ref[0] * steps + k)),
                pl.BlockSpec((chunk, widths[0]), by_source),
                pl.BlockSpec((chunk, widths[1]), by_source),
            ]
            + ([] if first else sum_specs),
            out_specs=sum_specs,
        ),
        out_shape=[jax.ShapeDtypeStruct((rows, width), jnp.float32) for width in widths],
        compiler_params=pltpu.CompilerParams(vmem_limit_bytes=PROJECT_VMEM_BYTES),
        cost_estimate=pl.CostEstimate(
            flops=2 * rows * features * (widths[0] + widths[1]),
            bytes_accessed=2 * features * (widths[0] + widths[1] + rows),
            transcendentals=0,
        ),
    )(source.reshape(1).astype(jnp.int32), block, gain, w_query, flat_kv, *([] if first else sums))


def attend_kernel(
    r, model_width, length_ref, q_ref, kv_ref, square_ref, cos_ref, sin_ref, pair_ref, att_ref, cache_ref
):
    rows = q_ref.shape[0]
    head_size = pair_ref.shape[-1]
    heads = q_ref.shape[1] // head_size
    per_dot = 2 if heads % 2 == 0 else 1
    scale = head_size ** (-0.5)
    length = length_ref[r]
    cosine, sine = cos_ref[...], sin_ref[...]
    mean = jnp.sum(square_ref[...], axis=-1, keepdims=True) / model_width
    row_scale = lax.rsqrt(mean + EPSILON)

    def turn(vector):
        vector = vector * row_scale
        return vector * cosine + pltpu.roll(vector, head_size // 2, 1) * sine

    keys_f = turn(kv_ref[:, :head_size])
    values_f = kv_ref[:, head_size:] * row_scale
    live = lax.broadcasted_iota(jnp.int32, (rows, head_size), 0) < length
    cache_ref[:, :head_size] = jnp.where(live, keys_f, 0.0).astype(jnp.bfloat16)
    cache_ref[:, head_size:] = jnp.where(live, values_f, 0.0).astype(jnp.bfloat16)
    own_keys, own_values = keys_f.astype(jnp.bfloat16), values_f.astype(jnp.bfloat16)

    position = lax.broadcasted_iota(jnp.int32, (per_dot * rows, rows), 0) % rows
    other = lax.broadcasted_iota(jnp.int32, (per_dot * rows, rows), 1)
    causal = (other <= position) & (other < length)
    against = (((1,), (1,)), ((), ()))
    for g in range(0, heads, per_dot):
        query = jnp.concatenate(
            [turn(q_ref[:, (g + i) * head_size : (g + i + 1) * head_size]) for i in range(per_dot)]
        ).astype(jnp.bfloat16)
        scores = lax.dot_general(query, pair_ref[0], against, preferred_element_type=jnp.float32)
        own_scores = lax.dot_general(query, own_keys, against, preferred_element_type=jnp.float32)
        own_scores = jnp.where(causal, own_scores, -jnp.inf)
        highest = jnp.maximum(
            jnp.max(scores, axis=-1, keepdims=True), jnp.max(own_scores, axis=-1, keepdims=True)
        )
        weights = jnp.exp((scores - highest) * scale)
        own_weights = jnp.exp((own_scores - highest) * scale)
        total = jnp.sum(weights, axis=-1, keepdims=True) + jnp.sum(own_weights, axis=-1, keepdims=True)
        mixed = jnp.dot(weights.astype(jnp.bfloat16), pair_ref[1], preferred_element_type=jnp.float32)
        mixed = mixed + jnp.dot(
            own_weights.astype(jnp.bfloat16), own_values, preferred_element_type=jnp.float32
        )
        mixed = (mixed / total).astype(jnp.bfloat16)
        for i in range(per_dot):
            att_ref[:, (g + i) * head_size : (g + i + 1) * head_size] = mixed[i * rows : (i + 1) * rows]


def attend(r, suffix_len, model_width, lengths, sums, tables, pair):
    q_sum, kv_sum, square_sum = sums
    _, prefix_len, head_size = pair.shape
    width = q_sum.shape[1]

    def by_request(k, length_ref):
        return (r, 0)

    def whole(k, length_ref):
        return (0, 0)

    return pl.pallas_call(
        functools.partial(attend_kernel, r, model_width),
        grid_spec=pltpu.PrefetchScalarGridSpec(
            num_scalar_prefetch=1,
            grid=(1,),
            in_specs=[
                pl.BlockSpec((suffix_len, width), by_request),
                pl.BlockSpec((suffix_len, kv_sum.shape[1]), by_request),
                pl.BlockSpec((suffix_len, LANES), by_request),
                pl.BlockSpec((suffix_len, head_size), whole),
                pl.BlockSpec((suffix_len, head_size), whole),
                pl.BlockSpec((2, prefix_len, head_size), lambda k, length_ref: (0, 0, 0)),
            ],
            out_specs=[
                pl.BlockSpec((suffix_len, width), whole),
                pl.BlockSpec((suffix_len, kv_sum.shape[1]), whole),
            ],
        ),
        out_shape=[
            jax.ShapeDtypeStruct((suffix_len, width), jnp.bfloat16),
            jax.ShapeDtypeStruct((suffix_len, kv_sum.shape[1]), jnp.bfloat16),
        ],
        compiler_params=pltpu.CompilerParams(vmem_limit_bytes=VMEM_BYTES),
        cost_estimate=pl.CostEstimate(
            flops=4 * suffix_len * width * (prefix_len + suffix_len),
            bytes_accessed=4 * prefix_len * head_size + 4 * suffix_len * (width + 2 * head_size),
            transcendentals=suffix_len * width // head_size * prefix_len,
        ),
    )(lengths, q_sum, kv_sum, square_sum, *tables, pair)


def output_kernel(n_tp, length_ref, *refs):
    own_ref, others_ref, hidden_ref, out_ref = refs[-4:]
    req_count, suffix_len, features = hidden_ref.shape
    chunk = 2 * LANES if features % (2 * LANES) == 0 else LANES
    position = lax.broadcasted_iota(jnp.int32, (suffix_len, chunk), 0)
    attention = [
        jnp.concatenate([refs[r * n_tp + j][...] for r in range(req_count)]) for j in range(n_tp)
    ]
    for begin in range(0, features, chunk):
        columns = slice(begin, begin + chunk)
        mixed = jnp.dot(attention[0], own_ref[:, columns], preferred_element_type=jnp.float32)
        for j in range(1, n_tp):
            mixed = mixed + jnp.dot(
                attention[j], others_ref[j - 1, :, columns], preferred_element_type=jnp.float32
            )
        for r in range(req_count):
            part = mixed[r * suffix_len : (r + 1) * suffix_len]
            part = part + hidden_ref[r, :, columns].astype(jnp.float32)
            part = jnp.where(position < length_ref[r], part, 0.0)
            out_ref[r, :, columns] = part.astype(jnp.bfloat16)


def project_out(lengths, attention, w_own, w_others, hidden):
    req_count, suffix_len, features = hidden.shape
    n_tp = len(attention[0])
    vmem = pl.BlockSpec(memory_space=pltpu.VMEM)
    return pl.pallas_call(
        functools.partial(output_kernel, n_tp),
        in_specs=[pl.BlockSpec(memory_space=pltpu.SMEM)] + [vmem] * (req_count * n_tp + 3),
        out_specs=vmem,
        out_shape=jax.ShapeDtypeStruct(hidden.shape, jnp.bfloat16),
        compiler_params=pltpu.CompilerParams(vmem_limit_bytes=OUTPUT_VMEM_BYTES),
        cost_estimate=pl.CostEstimate(
            flops=2 * req_count * suffix_len * features * w_own.shape[0] * n_tp,
            bytes_accessed=2 * features * (w_own.shape[0] * n_tp + 2 * req_count * suffix_len),
            transcendentals=0,
        ),
    )(lengths, *[block for slots in attention for block in slots], w_own, w_others, hidden)


def shards(hidden, norm_gain, w_query, w_kv, w_out, prefix_cache, lengths, groups, owners):
    n_tp = lax.axis_size("tp")
    n_owners = lax.axis_size("req")
    my_index = lax.axis_index("req")
    place = lax.axis_index("tp")
    req_count, suffix_len, features = hidden.shape
    head_size = w_kv.shape[2]
    model_width = w_query.shape[0]

    flat_kv = w_kv.reshape(model_width, 2 * head_size)
    gain = norm_gain.reshape(1, model_width)
    tables = rope_tables(suffix_len, head_size)

    share = w_out.shape[0] // n_owners
    my_rows = lax.dynamic_slice_in_dim(w_out, my_index * share, share, axis=0)
    moved = []
    for j in range(1, n_tp):
        piece = lax.dynamic_slice_in_dim(my_rows, ring_place(j) * features, features, axis=1)
        moved.append(shift(piece, j))
    w_own = lax.dynamic_slice_in_dim(w_out, place * features, features, axis=1)

    _, prefix_len, _, head_size = prefix_cache.shape
    prefixes = lax.all_gather(prefix_cache.reshape(prefix_len * 2, head_size), "req", axis=0)
    local_groups = lax.dynamic_slice_in_dim(groups, my_index * req_count, req_count)
    owner_of = jnp.sum(
        jnp.where(local_groups[:, None] == jnp.arange(n_owners)[None, :], owners[None, :], 0), axis=-1
    ).astype(jnp.int32)

    block = hidden.reshape(req_count * suffix_len, features)
    sums = None
    for step in range(n_tp):
        coming = shift(block, 1) if step < n_tp - 1 else block
        sums = project(block, ring_place(-step), gain, w_query, flat_kv, sums)
        if step == 0:
            coming, sums, moved = lax.optimization_barrier((coming, sums, moved))
            moved = jnp.stack(moved)
        elif step == 1:
            coming, sums, moved = lax.optimization_barrier((coming, sums, moved))
            w_others = lax.all_gather(moved, "req", axis=0)
        elif step < n_tp - 2:
            coming, sums = lax.optimization_barrier((coming, sums))
        elif step == n_tp - 2:
            pairs = [
                lax.dynamic_index_in_dim(prefixes, owner_of[r], 0, keepdims=False)
                .reshape(prefix_len, 2, head_size)
                .transpose(1, 0, 2)
                for r in range(req_count)
            ]
            coming, sums, pairs, tables, w_own = lax.optimization_barrier(
                (coming, sums, pairs, tables, w_own)
            )
        block = coming

    caches, gathered = [], []
    for r in range(req_count):
        attention, cache = attend(r, suffix_len, model_width, lengths, sums, tables, pairs[r])
        caches.append(cache)
        gathered.append([attention] + [shift(attention, j) for j in range(1, n_tp)])

    suffix_cache = jnp.stack(caches).reshape(req_count, suffix_len, 2, head_size)
    w_others = w_others.transpose(1, 0, 2, 3).reshape(n_tp - 1, n_owners * share, features)
    out_hidden = project_out(lengths, gathered, w_own, w_others, hidden)
    return (out_hidden, suffix_cache)


def solution(mesh):
    return jax.shard_map(
        shards,
        mesh=mesh,
        in_specs=(
            P("req", None, "tp"),
            P(),
            P(None, "tp"),
            P(None, None, "tp"),
            P("tp", None),
            P("req", None, None, "tp"),
            P("req"),
            P(),
            P(),
        ),
        out_specs=(P("req", None, "tp"), P("req", None, None, "tp")),
        check_vma=False,
    )
```

```python
import functools

import jax
import jax.numpy as jnp
from jax import lax
from jax.experimental import pallas as pl
from jax.experimental.pallas import tpu as pltpu
from jax.sharding import PartitionSpec as P

PREFIX = 2048


EPSILON = 1e-05
ROPE_BASE = 5000000.0
VMEM_BYTES = 12 * 1024 * 1024
LANES = 128


def rope_tables(suffix_len, head_size):
    positions = (PREFIX + jnp.arange(suffix_len)).astype(jnp.float32)
    inverse = ROPE_BASE ** (-(2.0 * jnp.arange(head_size // 2).astype(jnp.float32)) / head_size)
    angles = positions[:, None] * inverse[None, :]
    cosine_table = jnp.concatenate([jnp.cos(angles), jnp.cos(angles)], axis=-1)
    sine_table = jnp.concatenate([-jnp.sin(angles), jnp.sin(angles)], axis=-1)
    return (cosine_table, sine_table)


def ring_order(n):
    return [0] + list(range(1, n, 2)) + list(range(n - 2 if n % 2 == 0 else n - 1, 0, -2))


def ring_place(place, distance):
    n = lax.axis_size("tp")
    ring = ring_order(n)
    return sum(jnp.where(place == ring[p], ring[(p + distance) % n], 0) for p in range(n))


def shift(block, distance):
    n = lax.axis_size("tp")
    ring = ring_order(n)
    return lax.ppermute(block, "tp", [(ring[p], ring[(p + distance) % n]) for p in range(n)])


def project_kernel(block_ref, gain_ref, wq_ref, wkv_ref, *refs):
    sums_in, sums = refs[:-3], refs[-3:]
    block_f = block_ref[...].astype(jnp.float32)
    scaled = (block_f * gain_ref[...]).astype(jnp.bfloat16)
    squares = block_f * block_f
    square = squares[:, :LANES]
    for i in range(1, squares.shape[1] // LANES):
        square = square + squares[:, i * LANES : (i + 1) * LANES]
    parts = (
        jnp.dot(scaled, wq_ref[...], preferred_element_type=jnp.float32),
        jnp.dot(scaled, wkv_ref[...], preferred_element_type=jnp.float32),
        square,
    )
    for i in range(3):
        sums[i][...] = sums_in[i][...] + parts[i] if sums_in else parts[i]


def project(block, weights, sums):
    rows, features = block.shape
    gain, w_query, flat_kv = weights
    widths = (w_query.shape[1], flat_kv.shape[1], LANES)
    vmem = pl.BlockSpec(memory_space=pltpu.VMEM)
    return pl.pallas_call(
        project_kernel,
        in_specs=[vmem] * (4 + len(sums)),
        out_specs=[vmem] * 3,
        out_shape=[jax.ShapeDtypeStruct((rows, width), jnp.float32) for width in widths],
        compiler_params=pltpu.CompilerParams(vmem_limit_bytes=VMEM_BYTES),
        cost_estimate=pl.CostEstimate(
            flops=2 * rows * features * (widths[0] + widths[1]),
            bytes_accessed=2 * features * (widths[0] + widths[1] + rows),
            transcendentals=0,
        ),
    )(block, gain, w_query, flat_kv, *sums)


def attend_kernel(
    r, model_width, length_ref, q_ref, kv_ref, square_ref, cos_ref, sin_ref, pair_ref, att_ref, cache_ref
):
    rows = q_ref.shape[0]
    head_size = pair_ref.shape[-1]
    heads = q_ref.shape[1] // head_size
    per_dot = 2 if heads % 2 == 0 else 1
    scale = head_size ** (-0.5)
    length = length_ref[r]
    cosine, sine = cos_ref[...], sin_ref[...]
    mean = jnp.sum(square_ref[...], axis=-1, keepdims=True) / model_width
    row_scale = lax.rsqrt(mean + EPSILON)

    def turn(vector):
        vector = vector * row_scale
        return vector * cosine + pltpu.roll(vector, head_size // 2, 1) * sine

    keys_f = turn(kv_ref[:, :head_size])
    values_f = kv_ref[:, head_size:] * row_scale
    live = lax.broadcasted_iota(jnp.int32, (rows, head_size), 0) < length
    cache_ref[:, :head_size] = jnp.where(live, keys_f, 0.0).astype(jnp.bfloat16)
    cache_ref[:, head_size:] = jnp.where(live, values_f, 0.0).astype(jnp.bfloat16)
    own_keys, own_values = keys_f.astype(jnp.bfloat16), values_f.astype(jnp.bfloat16)

    position = lax.broadcasted_iota(jnp.int32, (per_dot * rows, rows), 0) % rows
    other = lax.broadcasted_iota(jnp.int32, (per_dot * rows, rows), 1)
    causal = (other <= position) & (other < length)
    against = (((1,), (1,)), ((), ()))
    for g in range(0, heads, per_dot):
        query = jnp.concatenate(
            [turn(q_ref[:, (g + i) * head_size : (g + i + 1) * head_size]) for i in range(per_dot)]
        ).astype(jnp.bfloat16)
        scores = lax.dot_general(query, pair_ref[0], against, preferred_element_type=jnp.float32)
        own_scores = lax.dot_general(query, own_keys, against, preferred_element_type=jnp.float32)
        own_scores = jnp.where(causal, own_scores, -jnp.inf)
        highest = jnp.maximum(
            jnp.max(scores, axis=-1, keepdims=True), jnp.max(own_scores, axis=-1, keepdims=True)
        )
        weights = jnp.exp((scores - highest) * scale)
        own_weights = jnp.exp((own_scores - highest) * scale)
        total = jnp.sum(weights, axis=-1, keepdims=True) + jnp.sum(own_weights, axis=-1, keepdims=True)
        mixed = jnp.dot(weights.astype(jnp.bfloat16), pair_ref[1], preferred_element_type=jnp.float32)
        mixed = mixed + jnp.dot(
            own_weights.astype(jnp.bfloat16), own_values, preferred_element_type=jnp.float32
        )
        mixed = (mixed / total).astype(jnp.bfloat16)
        for i in range(per_dot):
            att_ref[:, (g + i) * head_size : (g + i + 1) * head_size] = mixed[i * rows : (i + 1) * rows]


def attend(r, suffix_len, model_width, lengths, sums, tables, pair):
    q_sum, kv_sum, square_sum = sums
    _, prefix_len, head_size = pair.shape
    width = q_sum.shape[1]

    def by_request(k, length_ref):
        return (r, 0)

    def whole(k, length_ref):
        return (0, 0)

    return pl.pallas_call(
        functools.partial(attend_kernel, r, model_width),
        grid_spec=pltpu.PrefetchScalarGridSpec(
            num_scalar_prefetch=1,
            grid=(1,),
            in_specs=[
                pl.BlockSpec((suffix_len, width), by_request),
                pl.BlockSpec((suffix_len, kv_sum.shape[1]), by_request),
                pl.BlockSpec((suffix_len, LANES), by_request),
                pl.BlockSpec((suffix_len, head_size), whole),
                pl.BlockSpec((suffix_len, head_size), whole),
                pl.BlockSpec((2, prefix_len, head_size), lambda k, length_ref: (0, 0, 0)),
            ],
            out_specs=[
                pl.BlockSpec((suffix_len, width), whole),
                pl.BlockSpec((suffix_len, kv_sum.shape[1]), whole),
            ],
        ),
        out_shape=[
            jax.ShapeDtypeStruct((suffix_len, width), jnp.bfloat16),
            jax.ShapeDtypeStruct((suffix_len, kv_sum.shape[1]), jnp.bfloat16),
        ],
        compiler_params=pltpu.CompilerParams(vmem_limit_bytes=VMEM_BYTES),
        cost_estimate=pl.CostEstimate(
            flops=4 * suffix_len * width * (prefix_len + suffix_len),
            bytes_accessed=4 * prefix_len * head_size + 4 * suffix_len * (width + 2 * head_size),
            transcendentals=suffix_len * width // head_size * prefix_len,
        ),
    )(lengths, q_sum, kv_sum, square_sum, *tables, pair)


def stage_kernel(from_ref, to_ref, arrived):
    copy = pltpu.make_async_copy(from_ref, to_ref, arrived)
    copy.start()
    copy.wait()


def stage_in(array):
    return pl.pallas_call(
        stage_kernel,
        in_specs=[pl.BlockSpec(memory_space=pltpu.HBM)],
        out_specs=pl.BlockSpec(memory_space=pltpu.VMEM),
        out_shape=jax.ShapeDtypeStruct(array.shape, array.dtype),
        scratch_shapes=[pltpu.SemaphoreType.DMA],
        compiler_params=pltpu.CompilerParams(vmem_limit_bytes=VMEM_BYTES),
        cost_estimate=pl.CostEstimate(flops=0, bytes_accessed=2 * array.size * 2, transcendentals=0),
    )(array)


def output_kernel(n_tp, length_ref, *refs):
    own_ref, others_ref, hidden_ref, out_ref = refs[-4:]
    req_count, suffix_len, features = hidden_ref.shape
    chunk = 2 * LANES if features % (2 * LANES) == 0 else LANES
    position = lax.broadcasted_iota(jnp.int32, (suffix_len, chunk), 0)
    attention = [
        jnp.concatenate([refs[r * n_tp + j][...] for r in range(req_count)]) for j in range(n_tp)
    ]
    for begin in range(0, features, chunk):
        columns = slice(begin, begin + chunk)
        mixed = jnp.dot(attention[0], own_ref[:, columns], preferred_element_type=jnp.float32)
        for j in range(1, n_tp):
            weights = others_ref[:, j - 1, :, columns].reshape(own_ref.shape[0], chunk)
            mixed = mixed + jnp.dot(attention[j], weights, preferred_element_type=jnp.float32)
        for r in range(req_count):
            part = mixed[r * suffix_len : (r + 1) * suffix_len]
            part = part + hidden_ref[r, :, columns].astype(jnp.float32)
            part = jnp.where(position < length_ref[r], part, 0.0)
            out_ref[r, :, columns] = part.astype(jnp.bfloat16)


def project_out(lengths, attention, w_own, w_others, hidden):
    req_count, suffix_len, features = hidden.shape
    n_tp = len(attention[0])
    vmem = pl.BlockSpec(memory_space=pltpu.VMEM)
    return pl.pallas_call(
        functools.partial(output_kernel, n_tp),
        in_specs=[pl.BlockSpec(memory_space=pltpu.SMEM)] + [vmem] * (req_count * n_tp + 3),
        out_specs=vmem,
        out_shape=jax.ShapeDtypeStruct(hidden.shape, jnp.bfloat16),
        compiler_params=pltpu.CompilerParams(vmem_limit_bytes=VMEM_BYTES),
        cost_estimate=pl.CostEstimate(
            flops=2 * req_count * suffix_len * features * w_own.shape[0] * n_tp,
            bytes_accessed=2 * features * (w_own.shape[0] * n_tp + 2 * req_count * suffix_len),
            transcendentals=0,
        ),
    )(lengths, *[block for slots in attention for block in slots], w_own, w_others, hidden)


def shards(hidden, norm_gain, w_query, w_kv, w_out, prefix_cache, lengths, groups, owners):
    n_tp = lax.axis_size("tp")
    n_owners = lax.axis_size("req")
    my_index = lax.axis_index("req")
    place = lax.axis_index("tp")
    req_count, suffix_len, features = hidden.shape
    head_size = w_kv.shape[2]
    model_width = w_query.shape[0]

    flat_kv = w_kv.reshape(model_width, 2 * head_size)
    tables = rope_tables(suffix_len, head_size)

    share = w_out.shape[0] // n_owners
    my_rows = lax.dynamic_slice_in_dim(w_out, my_index * share, share, axis=0)
    moved = []
    for j in range(1, n_tp):
        piece = lax.dynamic_slice_in_dim(my_rows, ring_place(place, j) * features, features, axis=1)
        moved.append(shift(piece, j))
    w_own = lax.dynamic_slice_in_dim(w_out, place * features, features, axis=1)

    _, prefix_len, _, head_size = prefix_cache.shape
    prefixes = lax.all_gather(prefix_cache.reshape(prefix_len * 2, head_size), "req", axis=0)
    local_groups = lax.dynamic_slice_in_dim(groups, my_index * req_count, req_count)
    owner_of = jnp.sum(
        jnp.where(local_groups[:, None] == jnp.arange(n_owners)[None, :], owners[None, :], 0), axis=-1
    ).astype(jnp.int32)

    def weights_of(begin):
        return (
            lax.dynamic_slice_in_dim(norm_gain, begin, features).reshape(1, features),
            lax.dynamic_slice_in_dim(w_query, begin, features, axis=0),
            lax.dynamic_slice_in_dim(flat_kv, begin, features, axis=0),
        )

    block = hidden.reshape(req_count * suffix_len, features)
    begins = [ring_place(place, -step) * features for step in range(n_tp)]
    weights = weights_of(begins[0])
    sums = []
    for step in range(n_tp - 1):
        coming = shift(block, 1)
        sums = project(block, weights, sums)
        early = (tables, w_own, begins, owner_of)
        state = [coming, sums, weights_of(begins[step + 1]), moved, early]
        if step == n_tp - 2:
            state.append(
                [
                    lax.dynamic_index_in_dim(prefixes, owner_of[r], 0, keepdims=False)
                    .reshape(prefix_len, 2, head_size)
                    .transpose(1, 0, 2)
                    for r in range(req_count)
                ]
            )
        state = lax.optimization_barrier(state)
        block, sums, weights, moved, early = state[:5]
        tables, w_own, begins, owner_of = early
        if step == 0:
            moved = jnp.stack(moved)
        elif step == 1:
            w_others, moved = lax.all_gather(moved, "req", axis=0), []
    sums = project(block, weights, sums)
    pairs = state[5]

    caches, gathered = [], []
    for r in range(req_count):
        attention, cache = attend(r, suffix_len, model_width, lengths, sums, tables, pairs[r])
        caches.append(cache)
        gathered.append([attention] + [shift(attention, j) for j in range(1, n_tp)])

    suffix_cache = jnp.stack(caches).reshape(req_count, suffix_len, 2, head_size)
    out_hidden = project_out(lengths, gathered, w_own, stage_in(w_others), hidden)
    return (out_hidden, suffix_cache)


def solution(mesh):
    return jax.shard_map(
        shards,
        mesh=mesh,
        in_specs=(
            P("req", None, "tp"),
            P(),
            P(None, "tp"),
            P(None, None, "tp"),
            P("tp", None),
            P("req", None, None, "tp"),
            P("req"),
            P(),
            P(),
        ),
        out_specs=(P("req", None, "tp"), P("req", None, None, "tp")),
        check_vma=False,
    )
```

```python
import functools

import jax
import jax.numpy as jnp
from jax import lax
from jax.experimental import pallas as pl
from jax.experimental.pallas import tpu as pltpu
from jax.sharding import PartitionSpec as P

PREFIX = 2048


EPSILON = 1e-05
ROPE_BASE = 5000000.0
VMEM_BYTES = 12 * 1024 * 1024
LANES = 128
ROW_TILE = 16


def rope_tables(suffix_len, head_size):
    positions = (PREFIX + jnp.arange(suffix_len)).astype(jnp.float32)
    inverse = ROPE_BASE ** (-(2.0 * jnp.arange(head_size // 2).astype(jnp.float32)) / head_size)
    angles = positions[:, None] * inverse[None, :]
    cosine_table = jnp.concatenate([jnp.cos(angles), jnp.cos(angles)], axis=-1)
    sine_table = jnp.concatenate([-jnp.sin(angles), jnp.sin(angles)], axis=-1)
    return (cosine_table, sine_table)


def ring_order(n):
    return [0] + list(range(1, n, 2)) + list(range(n - 2 if n % 2 == 0 else n - 1, 0, -2))


def ring_place(place, distance):
    n = lax.axis_size("tp")
    ring = ring_order(n)
    return sum(jnp.where(place == ring[p], ring[(p + distance) % n], 0) for p in range(n))


def shift(block, distance):
    n = lax.axis_size("tp")
    ring = ring_order(n)
    return lax.ppermute(block, "tp", [(ring[p], ring[(p + distance) % n]) for p in range(n)])


def project_kernel(block_ref, gain_ref, wq_ref, wkv_ref, *refs):
    sums_in, sums = refs[:-3], refs[-3:]
    rows = block_ref.shape[0]
    block_f = block_ref[...].astype(jnp.float32)
    scaled = (block_f * gain_ref[...]).astype(jnp.bfloat16)
    squares = block_f * block_f
    square = squares[:, :LANES]
    for i in range(1, squares.shape[1] // LANES):
        square = square + squares[:, i * LANES : (i + 1) * LANES]
    parts = (
        jnp.dot(scaled, wq_ref[...], preferred_element_type=jnp.float32),
        jnp.dot(scaled, wkv_ref[...], preferred_element_type=jnp.float32),
        square,
    )
    for i in range(3):
        sums[i][:rows] = sums_in[i][:rows] + parts[i] if sums_in else parts[i]


def project(block, weights, sums, total_rows):
    rows, features = block.shape
    gain, w_query, flat_kv = weights
    widths = (w_query.shape[1], flat_kv.shape[1], LANES)
    vmem = pl.BlockSpec(memory_space=pltpu.VMEM)
    return pl.pallas_call(
        project_kernel,
        in_specs=[vmem] * (4 + len(sums)),
        out_specs=[vmem] * 3,
        out_shape=[jax.ShapeDtypeStruct((total_rows, width), jnp.float32) for width in widths],
        compiler_params=pltpu.CompilerParams(vmem_limit_bytes=VMEM_BYTES),
        cost_estimate=pl.CostEstimate(
            flops=2 * rows * features * (widths[0] + widths[1]),
            bytes_accessed=2 * features * (widths[0] + widths[1] + rows),
            transcendentals=0,
        ),
    )(block, gain, w_query, flat_kv, *sums)


def attend_kernel(
    r, model_width, length_ref, offset_ref, q_ref, kv_ref, square_ref, cos_ref, sin_ref, pair_ref, att_ref, cache_ref
):
    rows = att_ref.shape[0]
    packed = pl.ds(pl.multiple_of(offset_ref[r], ROW_TILE), rows)
    head_size = pair_ref.shape[-1]
    heads = q_ref.shape[1] // head_size
    per_dot = 2 if heads % 2 == 0 else 1
    scale = head_size ** (-0.5)
    length = length_ref[r]
    cosine, sine = cos_ref[...], sin_ref[...]
    mean = jnp.sum(square_ref[packed, :], axis=-1, keepdims=True) / model_width
    row_scale = lax.rsqrt(mean + EPSILON)

    def turn(vector):
        vector = vector * row_scale
        return vector * cosine + pltpu.roll(vector, head_size // 2, 1) * sine

    keys_f = turn(kv_ref[packed, :head_size])
    values_f = kv_ref[packed, head_size:] * row_scale
    live = lax.broadcasted_iota(jnp.int32, (rows, head_size), 0) < length
    own_keys = jnp.where(live, keys_f, 0.0).astype(jnp.bfloat16)
    own_values = jnp.where(live, values_f, 0.0).astype(jnp.bfloat16)
    cache_ref[:, :head_size] = own_keys
    cache_ref[:, head_size:] = own_values

    position = lax.broadcasted_iota(jnp.int32, (per_dot * rows, rows), 0) % rows
    other = lax.broadcasted_iota(jnp.int32, (per_dot * rows, rows), 1)
    causal = (other <= position) & (other < length)
    against = (((1,), (1,)), ((), ()))
    for g in range(0, heads, per_dot):
        query = jnp.concatenate(
            [turn(q_ref[packed, (g + i) * head_size : (g + i + 1) * head_size]) for i in range(per_dot)]
        ).astype(jnp.bfloat16)
        scores = lax.dot_general(query, pair_ref[0], against, preferred_element_type=jnp.float32)
        own_scores = lax.dot_general(query, own_keys, against, preferred_element_type=jnp.float32)
        own_scores = jnp.where(causal, own_scores, -jnp.inf)
        highest = jnp.maximum(
            jnp.max(scores, axis=-1, keepdims=True), jnp.max(own_scores, axis=-1, keepdims=True)
        )
        weights = jnp.exp((scores - highest) * scale)
        own_weights = jnp.exp((own_scores - highest) * scale)
        total = jnp.sum(weights, axis=-1, keepdims=True) + jnp.sum(own_weights, axis=-1, keepdims=True)
        mixed = jnp.dot(weights.astype(jnp.bfloat16), pair_ref[1], preferred_element_type=jnp.float32)
        mixed = mixed + jnp.dot(
            own_weights.astype(jnp.bfloat16), own_values, preferred_element_type=jnp.float32
        )
        mixed = (mixed / total).astype(jnp.bfloat16)
        for i in range(per_dot):
            att_ref[:, (g + i) * head_size : (g + i + 1) * head_size] = mixed[i * rows : (i + 1) * rows]


def attend(r, suffix_len, model_width, lengths, offsets, sums, tables, pair):
    width = sums[0].shape[1]
    _, prefix_len, head_size = pair.shape
    vmem = pl.BlockSpec(memory_space=pltpu.VMEM)
    smem = pl.BlockSpec(memory_space=pltpu.SMEM)
    return pl.pallas_call(
        functools.partial(attend_kernel, r, model_width),
        in_specs=[smem] * 2 + [vmem] * 6,
        out_specs=[vmem] * 2,
        out_shape=[
            jax.ShapeDtypeStruct((suffix_len, width), jnp.bfloat16),
            jax.ShapeDtypeStruct((suffix_len, 2 * head_size), jnp.bfloat16),
        ],
        compiler_params=pltpu.CompilerParams(vmem_limit_bytes=VMEM_BYTES),
        cost_estimate=pl.CostEstimate(
            flops=4 * suffix_len * width * (prefix_len + suffix_len),
            bytes_accessed=4 * prefix_len * head_size + 4 * suffix_len * (width + 2 * head_size),
            transcendentals=suffix_len * width // head_size * prefix_len,
        ),
    )(lengths, offsets, *sums, *tables, pair)


def stage_kernel(from_ref, to_ref, arrived):
    copy = pltpu.make_async_copy(from_ref, to_ref, arrived)
    copy.start()
    copy.wait()


def stage_in(array):
    return pl.pallas_call(
        stage_kernel,
        in_specs=[pl.BlockSpec(memory_space=pltpu.HBM)],
        out_specs=pl.BlockSpec(memory_space=pltpu.VMEM),
        out_shape=jax.ShapeDtypeStruct(array.shape, array.dtype),
        scratch_shapes=[pltpu.SemaphoreType.DMA],
        compiler_params=pltpu.CompilerParams(vmem_limit_bytes=VMEM_BYTES),
        cost_estimate=pl.CostEstimate(flops=0, bytes_accessed=2 * array.size * 2, transcendentals=0),
    )(array)


def output_kernel(n_tp, length_ref, *refs):
    own_ref, others_ref, hidden_ref, out_ref = refs[-4:]
    req_count, suffix_len, features = hidden_ref.shape
    chunk = 2 * LANES if features % (2 * LANES) == 0 else LANES
    position = lax.broadcasted_iota(jnp.int32, (suffix_len, chunk), 0)
    attention = [
        jnp.concatenate([refs[r * n_tp + j][...] for r in range(req_count)]) for j in range(n_tp)
    ]
    for begin in range(0, features, chunk):
        columns = slice(begin, begin + chunk)
        mixed = jnp.dot(attention[0], own_ref[:, columns], preferred_element_type=jnp.float32)
        for j in range(1, n_tp):
            weights = others_ref[:, j - 1, :, columns].reshape(own_ref.shape[0], chunk)
            mixed = mixed + jnp.dot(attention[j], weights, preferred_element_type=jnp.float32)
        for r in range(req_count):
            part = mixed[r * suffix_len : (r + 1) * suffix_len]
            part = part + hidden_ref[r, :, columns].astype(jnp.float32)
            part = jnp.where(position < length_ref[r], part, 0.0)
            out_ref[r, :, columns] = part.astype(jnp.bfloat16)


def project_out(lengths, attention, w_own, w_others, hidden):
    req_count, suffix_len, features = hidden.shape
    n_tp = len(attention[0])
    vmem = pl.BlockSpec(memory_space=pltpu.VMEM)
    return pl.pallas_call(
        functools.partial(output_kernel, n_tp),
        in_specs=[pl.BlockSpec(memory_space=pltpu.SMEM)] + [vmem] * (req_count * n_tp + 3),
        out_specs=vmem,
        out_shape=jax.ShapeDtypeStruct(hidden.shape, jnp.bfloat16),
        compiler_params=pltpu.CompilerParams(vmem_limit_bytes=VMEM_BYTES),
        cost_estimate=pl.CostEstimate(
            flops=2 * req_count * suffix_len * features * w_own.shape[0] * n_tp,
            bytes_accessed=2 * features * (w_own.shape[0] * n_tp + 2 * req_count * suffix_len),
            transcendentals=0,
        ),
    )(lengths, *[block for slots in attention for block in slots], w_own, w_others, hidden)


def shards(hidden, norm_gain, w_query, w_kv, w_out, prefix_cache, lengths, groups, owners):
    n_tp = lax.axis_size("tp")
    n_owners = lax.axis_size("req")
    my_index = lax.axis_index("req")
    place = lax.axis_index("tp")
    req_count, suffix_len, features = hidden.shape
    head_size = w_kv.shape[2]
    model_width = w_query.shape[0]

    flat_kv = w_kv.reshape(model_width, 2 * head_size)
    tables = rope_tables(suffix_len, head_size)

    share = w_out.shape[0] // n_owners
    my_rows = lax.dynamic_slice_in_dim(w_out, my_index * share, share, axis=0)
    moved = []
    for j in range(1, n_tp):
        piece = lax.dynamic_slice_in_dim(my_rows, ring_place(place, j) * features, features, axis=1)
        moved.append(shift(piece, j))
    w_own = lax.dynamic_slice_in_dim(w_out, place * features, features, axis=1)

    _, prefix_len, _, head_size = prefix_cache.shape
    prefixes = lax.all_gather(prefix_cache.reshape(prefix_len * 2, head_size), "req", axis=0)
    local_groups = lax.dynamic_slice_in_dim(groups, my_index * req_count, req_count)
    owner_of = jnp.sum(
        jnp.where(local_groups[:, None] == jnp.arange(n_owners)[None, :], owners[None, :], 0), axis=-1
    ).astype(jnp.int32)

    def weights_of(begin):
        return (
            lax.dynamic_slice_in_dim(norm_gain, begin, features).reshape(1, features),
            lax.dynamic_slice_in_dim(w_query, begin, features, axis=0),
            lax.dynamic_slice_in_dim(flat_kv, begin, features, axis=0),
        )

    total_rows = req_count * suffix_len
    packed = hidden.reshape(total_rows, features)
    offsets = [jnp.int32(0)]
    for r in range(1, req_count):
        offsets.append(offsets[-1] + (lengths[r - 1] + ROW_TILE - 1) // ROW_TILE * ROW_TILE)
        packed = lax.dynamic_update_slice(packed, hidden[r], (offsets[r], 0))
    live_rows = offsets[-1] + lengths[-1]
    offsets = jnp.stack(offsets)
    capacities = [total_rows * k // 8 for k in range(3, 9)]
    branch = sum((live_rows > capacity).astype(jnp.int32) for capacity in capacities[:-1])

    begins = [ring_place(place, -step) * features for step in range(n_tp)]
    own_sums = project(packed, weights_of(begins[0]), [], total_rows)
    state = (packed, own_sums, weights_of(begins[1]), moved, tables, w_own, begins, owner_of, offsets, branch)
    state = lax.optimization_barrier(state)
    packed, own_sums, next_weights, moved, tables, w_own, begins, owner_of, offsets, branch = state
    w_others = lax.all_gather(jnp.stack(moved), "req", axis=0)

    def ring_of(capacity):
        def run(packed, sums, weights):
            block = shift(packed[:capacity], 1)
            for step in range(1, n_tp - 1):
                coming = shift(block, 1)
                sums = project(block, weights, sums, total_rows)
                state = (coming, sums, weights_of(begins[step + 1]))
                block, sums, weights = lax.optimization_barrier(state)
            return project(block, weights, sums, total_rows)

        return run

    sums = lax.switch(branch, [ring_of(c) for c in capacities], packed, own_sums, next_weights)

    caches, gathered = [], []
    for r in range(req_count):
        pair = lax.dynamic_index_in_dim(prefixes, owner_of[r], 0, keepdims=False)
        pair = pair.reshape(prefix_len, 2, head_size).transpose(1, 0, 2)
        attention, cache = attend(r, suffix_len, model_width, lengths, offsets, sums, tables, pair)
        caches.append(cache)
        gathered.append([attention] + [shift(attention, j) for j in range(1, n_tp)])

    suffix_cache = jnp.stack(caches).reshape(req_count, suffix_len, 2, head_size)
    w_others, suffix_cache = lax.optimization_barrier((w_others, suffix_cache))
    out_hidden = project_out(lengths, gathered, w_own, stage_in(w_others), hidden)
    return (out_hidden, suffix_cache)


def solution(mesh):
    return jax.shard_map(
        shards,
        mesh=mesh,
        in_specs=(
            P("req", None, "tp"),
            P(),
            P(None, "tp"),
            P(None, None, "tp"),
            P("tp", None),
            P("req", None, None, "tp"),
            P("req"),
            P(),
            P(),
        ),
        out_specs=(P("req", None, "tp"), P("req", None, None, "tp")),
        check_vma=False,
    )
```

```python
import functools

import jax
import jax.numpy as jnp
from jax import lax
from jax.experimental import pallas as pl
from jax.experimental.pallas import tpu as pltpu
from jax.sharding import PartitionSpec as P

PREFIX = 2048


EPSILON = 1e-05
ROPE_BASE = 5000000.0
VMEM_BYTES = 12 * 1024 * 1024
LANES = 128
ROW_TILE = 16


def rope_tables(suffix_len, head_size):
    positions = (PREFIX + jnp.arange(suffix_len)).astype(jnp.float32)
    inverse = ROPE_BASE ** (-(2.0 * jnp.arange(head_size // 2).astype(jnp.float32)) / head_size)
    angles = positions[:, None] * inverse[None, :]
    cosine_table = jnp.concatenate([jnp.cos(angles), jnp.cos(angles)], axis=-1)
    sine_table = jnp.concatenate([-jnp.sin(angles), jnp.sin(angles)], axis=-1)
    return (cosine_table, sine_table)


def ring_order(n):
    return [0] + list(range(1, n, 2)) + list(range(n - 2 if n % 2 == 0 else n - 1, 0, -2))


def ring_place(place, distance):
    n = lax.axis_size("tp")
    ring = ring_order(n)
    return sum(jnp.where(place == ring[p], ring[(p + distance) % n], 0) for p in range(n))


def shift(block, distance):
    n = lax.axis_size("tp")
    ring = ring_order(n)
    return lax.ppermute(block, "tp", [(ring[p], ring[(p + distance) % n]) for p in range(n)])


def project_kernel(block_ref, gain_ref, wq_ref, wkv_ref, *refs):
    sums_in, sums = refs[:-3], refs[-3:]
    rows = block_ref.shape[0]
    block_f = block_ref[...].astype(jnp.float32)
    scaled = (block_f * gain_ref[...]).astype(jnp.bfloat16)
    squares = block_f * block_f
    square = squares[:, :LANES]
    for i in range(1, squares.shape[1] // LANES):
        square = square + squares[:, i * LANES : (i + 1) * LANES]
    parts = (
        jnp.dot(scaled, wq_ref[...], preferred_element_type=jnp.float32),
        jnp.dot(scaled, wkv_ref[...], preferred_element_type=jnp.float32),
        square,
    )
    for i in range(3):
        sums[i][:rows] = sums_in[i][:rows] + parts[i] if sums_in else parts[i]


def project(block, weights, sums, total_rows):
    rows, features = block.shape
    gain, w_query, flat_kv = weights
    widths = (w_query.shape[1], flat_kv.shape[1], LANES)
    vmem = pl.BlockSpec(memory_space=pltpu.VMEM)
    return pl.pallas_call(
        project_kernel,
        in_specs=[vmem] * (4 + len(sums)),
        out_specs=[vmem] * 3,
        out_shape=[jax.ShapeDtypeStruct((total_rows, width), jnp.float32) for width in widths],
        compiler_params=pltpu.CompilerParams(vmem_limit_bytes=VMEM_BYTES),
        cost_estimate=pl.CostEstimate(
            flops=2 * rows * features * (widths[0] + widths[1]),
            bytes_accessed=2 * features * (widths[0] + widths[1] + rows),
            transcendentals=0,
        ),
    )(block, gain, w_query, flat_kv, *sums)


def attend_kernel(
    r, model_width, length_ref, offset_ref, q_ref, kv_ref, square_ref, cos_ref, sin_ref, pair_ref, att_ref, cache_ref
):
    rows = att_ref.shape[0]
    packed = pl.ds(pl.multiple_of(offset_ref[r], ROW_TILE), rows)
    head_size = pair_ref.shape[-1]
    heads = q_ref.shape[1] // head_size
    per_dot = 2 if heads % 2 == 0 else 1
    scale = head_size ** (-0.5)
    length = length_ref[r]
    cosine, sine = cos_ref[...], sin_ref[...]
    mean = jnp.sum(square_ref[packed, :], axis=-1, keepdims=True) / model_width
    row_scale = lax.rsqrt(mean + EPSILON)

    def turn(vector):
        vector = vector * row_scale
        return vector * cosine + pltpu.roll(vector, head_size // 2, 1) * sine

    keys_f = turn(kv_ref[packed, :head_size])
    values_f = kv_ref[packed, head_size:] * row_scale
    live = lax.broadcasted_iota(jnp.int32, (rows, head_size), 0) < length
    own_keys = jnp.where(live, keys_f, 0.0).astype(jnp.bfloat16)
    own_values = jnp.where(live, values_f, 0.0).astype(jnp.bfloat16)
    cache_ref[:, :head_size] = own_keys
    cache_ref[:, head_size:] = own_values

    position = lax.broadcasted_iota(jnp.int32, (per_dot * rows, rows), 0) % rows
    other = lax.broadcasted_iota(jnp.int32, (per_dot * rows, rows), 1)
    causal = (other <= position) & (other < length)
    against = (((1,), (1,)), ((), ()))
    for g in range(0, heads, per_dot):
        query = jnp.concatenate(
            [turn(q_ref[packed, (g + i) * head_size : (g + i + 1) * head_size]) for i in range(per_dot)]
        ).astype(jnp.bfloat16)
        scores = lax.dot_general(query, pair_ref[0], against, preferred_element_type=jnp.float32)
        own_scores = lax.dot_general(query, own_keys, against, preferred_element_type=jnp.float32)
        own_scores = jnp.where(causal, own_scores, -jnp.inf)
        highest = jnp.maximum(
            jnp.max(scores, axis=-1, keepdims=True), jnp.max(own_scores, axis=-1, keepdims=True)
        )
        weights = jnp.exp((scores - highest) * scale)
        own_weights = jnp.exp((own_scores - highest) * scale)
        total = jnp.sum(weights, axis=-1, keepdims=True) + jnp.sum(own_weights, axis=-1, keepdims=True)
        mixed = jnp.dot(weights.astype(jnp.bfloat16), pair_ref[1], preferred_element_type=jnp.float32)
        mixed = mixed + jnp.dot(
            own_weights.astype(jnp.bfloat16), own_values, preferred_element_type=jnp.float32
        )
        mixed = (mixed / total).astype(jnp.bfloat16)
        for i in range(per_dot):
            att_ref[:, (g + i) * head_size : (g + i + 1) * head_size] = mixed[i * rows : (i + 1) * rows]


def attend(r, suffix_len, model_width, lengths, offsets, sums, tables, pair):
    width = sums[0].shape[1]
    _, prefix_len, head_size = pair.shape
    vmem = pl.BlockSpec(memory_space=pltpu.VMEM)
    smem = pl.BlockSpec(memory_space=pltpu.SMEM)
    return pl.pallas_call(
        functools.partial(attend_kernel, r, model_width),
        in_specs=[smem] * 2 + [vmem] * 6,
        out_specs=[vmem] * 2,
        out_shape=[
            jax.ShapeDtypeStruct((suffix_len, width), jnp.bfloat16),
            jax.ShapeDtypeStruct((suffix_len, 2 * head_size), jnp.bfloat16),
        ],
        compiler_params=pltpu.CompilerParams(vmem_limit_bytes=VMEM_BYTES),
        cost_estimate=pl.CostEstimate(
            flops=4 * suffix_len * width * (prefix_len + suffix_len),
            bytes_accessed=4 * prefix_len * head_size + 4 * suffix_len * (width + 2 * head_size),
            transcendentals=suffix_len * width // head_size * prefix_len,
        ),
    )(lengths, offsets, *sums, *tables, pair)


def copies_kernel(plan, *refs):
    arrived = refs[-1]
    copies = [
        pltpu.make_async_copy(source, target, arrived.at[i])
        for i, (source, target) in enumerate(plan(refs[:-1]))
    ]
    for copy in copies:
        copy.start()
    for copy in copies:
        copy.wait()


def copied(plan, n_copies, scalars, arrays, outs, out_space=pltpu.HBM, vmem_bytes=VMEM_BYTES):
    size = sum(out.size for out in outs)
    return pl.pallas_call(
        functools.partial(copies_kernel, plan),
        in_specs=[pl.BlockSpec(memory_space=pltpu.SMEM)] * len(scalars)
        + [pl.BlockSpec(memory_space=pltpu.HBM)] * len(arrays),
        out_specs=[pl.BlockSpec(memory_space=out_space)] * len(outs),
        out_shape=outs,
        scratch_shapes=[pltpu.SemaphoreType.DMA((n_copies,))],
        compiler_params=pltpu.CompilerParams(vmem_limit_bytes=vmem_bytes),
        cost_estimate=pl.CostEstimate(flops=0, bytes_accessed=4 * size, transcendentals=0),
    )(*scalars, *arrays)


def stage_in(array):
    out = jax.ShapeDtypeStruct(array.shape, array.dtype)
    return copied(lambda refs: [(refs[0], refs[1])], 1, [], [array], [out], pltpu.VMEM)[0]


def first_rows(array, count):
    out = jax.ShapeDtypeStruct((count, array.shape[1]), array.dtype)
    return copied(lambda refs: [(refs[0].at[pl.ds(0, count)], refs[1])], 1, [], [array], [out])[0]


def stacked(arrays):
    n = len(arrays)
    out = jax.ShapeDtypeStruct((n,) + arrays[0].shape, arrays[0].dtype)
    return copied(lambda refs: [(refs[i], refs[n].at[i]) for i in range(n)], n, [], arrays, [out])[0]


def cut(array, row, columns, shape):
    n = len(columns)

    def plan(refs):
        begins, whole, outs = refs[0], refs[1], refs[2:]
        rows = pl.ds(pl.multiple_of(begins[0], ROW_TILE), shape[0])
        return [
            (whole.at[rows, pl.ds(pl.multiple_of(begins[i + 1], LANES), shape[1])], outs[i])
            for i in range(n)
        ]

    outs = [jax.ShapeDtypeStruct(shape, array.dtype)] * n
    begins = jnp.stack([row] + columns).astype(jnp.int32)
    return copied(plan, n, [begins], [array], outs, vmem_bytes=58 * 1024 * 1024)


def output_kernel(n_tp, length_ref, *refs):
    own_ref, others_ref, hidden_ref, out_ref = refs[-4:]
    req_count, suffix_len, features = hidden_ref.shape
    chunk = 2 * LANES if features % (2 * LANES) == 0 else LANES
    position = lax.broadcasted_iota(jnp.int32, (suffix_len, chunk), 0)
    attention = [
        jnp.concatenate([refs[r * n_tp + j][...] for r in range(req_count)]) for j in range(n_tp)
    ]
    for begin in range(0, features, chunk):
        columns = slice(begin, begin + chunk)
        mixed = jnp.dot(attention[0], own_ref[:, columns], preferred_element_type=jnp.float32)
        for j in range(1, n_tp):
            weights = others_ref[:, j - 1, :, columns].reshape(own_ref.shape[0], chunk)
            mixed = mixed + jnp.dot(attention[j], weights, preferred_element_type=jnp.float32)
        for r in range(req_count):
            part = mixed[r * suffix_len : (r + 1) * suffix_len]
            part = part + hidden_ref[r, :, columns].astype(jnp.float32)
            part = jnp.where(position < length_ref[r], part, 0.0)
            out_ref[r, :, columns] = part.astype(jnp.bfloat16)


def project_out(lengths, attention, w_own, w_others, hidden):
    req_count, suffix_len, features = hidden.shape
    n_tp = len(attention[0])
    vmem = pl.BlockSpec(memory_space=pltpu.VMEM)
    return pl.pallas_call(
        functools.partial(output_kernel, n_tp),
        in_specs=[pl.BlockSpec(memory_space=pltpu.SMEM)] + [vmem] * (req_count * n_tp + 3),
        out_specs=vmem,
        out_shape=jax.ShapeDtypeStruct(hidden.shape, jnp.bfloat16),
        compiler_params=pltpu.CompilerParams(vmem_limit_bytes=VMEM_BYTES),
        cost_estimate=pl.CostEstimate(
            flops=2 * req_count * suffix_len * features * w_own.shape[0] * n_tp,
            bytes_accessed=2 * features * (w_own.shape[0] * n_tp + 2 * req_count * suffix_len),
            transcendentals=0,
        ),
    )(lengths, *[block for slots in attention for block in slots], w_own, w_others, hidden)


def shards(hidden, norm_gain, w_query, w_kv, w_out, prefix_cache, lengths, groups, owners):
    n_tp = lax.axis_size("tp")
    n_owners = lax.axis_size("req")
    my_index = lax.axis_index("req")
    place = lax.axis_index("tp")
    req_count, suffix_len, features = hidden.shape
    head_size = w_kv.shape[2]
    model_width = w_query.shape[0]

    flat_kv = w_kv.reshape(model_width, 2 * head_size)
    tables = rope_tables(suffix_len, head_size)

    share = w_out.shape[0] // n_owners
    columns = [ring_place(place, j) * features for j in range(1, n_tp)]
    pieces = cut(w_out, my_index * share, columns, (share, features))
    moved = [shift(piece, j) for j, piece in enumerate(pieces, 1)]

    _, prefix_len, _, head_size = prefix_cache.shape
    prefixes = lax.all_gather(prefix_cache.reshape(prefix_len * 2, head_size), "req", axis=0)
    local_groups = lax.dynamic_slice_in_dim(groups, my_index * req_count, req_count)
    owner_of = jnp.sum(
        jnp.where(local_groups[:, None] == jnp.arange(n_owners)[None, :], owners[None, :], 0), axis=-1
    ).astype(jnp.int32)

    def weights_of(begin):
        return (
            lax.dynamic_slice_in_dim(norm_gain, begin, features).reshape(1, features),
            lax.dynamic_slice_in_dim(w_query, begin, features, axis=0),
            lax.dynamic_slice_in_dim(flat_kv, begin, features, axis=0),
        )

    total_rows = req_count * suffix_len
    packed = hidden.reshape(total_rows, features)
    offsets = [jnp.int32(0)]
    for r in range(1, req_count):
        offsets.append(offsets[-1] + (lengths[r - 1] + ROW_TILE - 1) // ROW_TILE * ROW_TILE)
        packed = lax.dynamic_update_slice(packed, hidden[r], (offsets[r], 0))
    live_rows = offsets[-1] + lengths[-1]
    offsets = jnp.stack(offsets)
    capacities = [total_rows * k // 8 for k in range(3, 9)]
    branch = sum((live_rows > capacity).astype(jnp.int32) for capacity in capacities[:-1])

    begins = [ring_place(place, -step) * features for step in range(n_tp)]
    own_sums = project(packed, weights_of(begins[0]), [], total_rows)
    state = (packed, own_sums, moved, tables, begins, owner_of, offsets, branch)
    state = lax.optimization_barrier(state)
    packed, own_sums, moved, tables, begins, owner_of, offsets, branch = state
    w_others = lax.all_gather(stacked(moved), "req", axis=0)

    def ring_of(capacity):
        def run(packed, sums):
            block = first_rows(packed, capacity) if capacity < total_rows else packed
            for step in range(n_tp - 1):
                coming = shift(block, 1)
                if step > 0:
                    sums = project(block, weights, sums, total_rows)
                state = (coming, sums, weights_of(begins[step + 1]))
                block, sums, weights = lax.optimization_barrier(state)
            return project(block, weights, sums, total_rows)

        return run

    sums = lax.switch(branch, [ring_of(c) for c in capacities], packed, own_sums)

    caches, gathered = [], []
    for r in range(req_count):
        pair = lax.dynamic_index_in_dim(prefixes, owner_of[r], 0, keepdims=False)
        pair = pair.reshape(prefix_len, 2, head_size).transpose(1, 0, 2)
        attention, cache = attend(r, suffix_len, model_width, lengths, offsets, sums, tables, pair)
        caches.append(cache)
        gathered.append([attention] + [shift(attention, j) for j in range(1, n_tp)])
    place, _ = lax.optimization_barrier((place, caches[-1]))
    w_own = lax.dynamic_slice_in_dim(w_out, place * features, features, axis=1)

    suffix_cache = jnp.stack(caches).reshape(req_count, suffix_len, 2, head_size)
    w_others, suffix_cache = lax.optimization_barrier((w_others, suffix_cache))
    out_hidden = project_out(lengths, gathered, w_own, stage_in(w_others), hidden)
    return (out_hidden, suffix_cache)


def solution(mesh):
    return jax.shard_map(
        shards,
        mesh=mesh,
        in_specs=(
            P("req", None, "tp"),
            P(),
            P(None, "tp"),
            P(None, None, "tp"),
            P("tp", None),
            P("req", None, None, "tp"),
            P("req"),
            P(),
            P(),
        ),
        out_specs=(P("req", None, "tp"), P("req", None, None, "tp")),
        check_vma=False,
    )
```

```python
import functools

import jax
import jax.numpy as jnp
from jax import lax
from jax.experimental import pallas as pl
from jax.experimental.pallas import tpu as pltpu
from jax.sharding import PartitionSpec as P

PREFIX = 2048


EPSILON = 1e-05
ROPE_BASE = 5000000.0
VMEM_BYTES = 12 * 1024 * 1024
LANES = 128
ROW_TILE = 16


def rope_tables(suffix_len, head_size):
    positions = (PREFIX + jnp.arange(suffix_len)).astype(jnp.float32)
    inverse = ROPE_BASE ** (-(2.0 * jnp.arange(head_size // 2).astype(jnp.float32)) / head_size)
    angles = positions[:, None] * inverse[None, :]
    cosine_table = jnp.concatenate([jnp.cos(angles), jnp.cos(angles)], axis=-1)
    sine_table = jnp.concatenate([-jnp.sin(angles), jnp.sin(angles)], axis=-1)
    return (cosine_table, sine_table)


def ring_order(n):
    return [0] + list(range(1, n, 2)) + list(range(n - 2 if n % 2 == 0 else n - 1, 0, -2))


def ring_place(place, distance):
    n = lax.axis_size("tp")
    ring = ring_order(n)
    return sum(jnp.where(place == ring[p], ring[(p + distance) % n], 0) for p in range(n))


def shift(block, distance):
    n = lax.axis_size("tp")
    ring = ring_order(n)
    return lax.ppermute(block, "tp", [(ring[p], ring[(p + distance) % n]) for p in range(n)])


def project_kernel(block_ref, gain_ref, wq_ref, wkv_ref, *refs):
    sums_in, sums = refs[:-3], refs[-3:]
    rows = block_ref.shape[0]
    block_f = block_ref[...].astype(jnp.float32)
    scaled = (block_f * gain_ref[...]).astype(jnp.bfloat16)
    squares = block_f * block_f
    square = squares[:, :LANES]
    for i in range(1, squares.shape[1] // LANES):
        square = square + squares[:, i * LANES : (i + 1) * LANES]
    parts = (
        jnp.dot(scaled, wq_ref[...], preferred_element_type=jnp.float32),
        jnp.dot(scaled, wkv_ref[...], preferred_element_type=jnp.float32),
        square,
    )
    for i in range(3):
        sums[i][:rows] = sums_in[i][:rows] + parts[i] if sums_in else parts[i]


def project(block, weights, sums, total_rows):
    rows, features = block.shape
    gain, w_query, flat_kv = weights
    widths = (w_query.shape[1], flat_kv.shape[1], LANES)
    vmem = pl.BlockSpec(memory_space=pltpu.VMEM)
    return pl.pallas_call(
        project_kernel,
        in_specs=[vmem] * (4 + len(sums)),
        out_specs=[vmem] * 3,
        out_shape=[jax.ShapeDtypeStruct((total_rows, width), jnp.float32) for width in widths],
        compiler_params=pltpu.CompilerParams(vmem_limit_bytes=VMEM_BYTES),
        cost_estimate=pl.CostEstimate(
            flops=2 * rows * features * (widths[0] + widths[1]),
            bytes_accessed=2 * features * (widths[0] + widths[1] + rows),
            transcendentals=0,
        ),
    )(block, gain, w_query, flat_kv, *sums)


def attend_kernel(
    r, model_width, length_ref, offset_ref, q_ref, kv_ref, square_ref, cos_ref, sin_ref, pair_ref, att_ref, cache_ref
):
    rows = att_ref.shape[0]
    packed = pl.ds(pl.multiple_of(offset_ref[r], ROW_TILE), rows)
    head_size = pair_ref.shape[-1]
    heads = q_ref.shape[1] // head_size
    per_dot = 2 if heads % 2 == 0 else 1
    scale = head_size ** (-0.5)
    length = length_ref[r]
    cosine, sine = cos_ref[...], sin_ref[...]
    mean = jnp.sum(square_ref[packed, :], axis=-1, keepdims=True) / model_width
    row_scale = lax.rsqrt(mean + EPSILON)

    def turn(vector):
        vector = vector * row_scale
        return vector * cosine + pltpu.roll(vector, head_size // 2, 1) * sine

    keys_f = turn(kv_ref[packed, :head_size])
    values_f = kv_ref[packed, head_size:] * row_scale
    live = lax.broadcasted_iota(jnp.int32, (rows, head_size), 0) < length
    own_keys = jnp.where(live, keys_f, 0.0).astype(jnp.bfloat16)
    own_values = jnp.where(live, values_f, 0.0).astype(jnp.bfloat16)
    cache_ref[:, :head_size] = own_keys
    cache_ref[:, head_size:] = own_values

    position = lax.broadcasted_iota(jnp.int32, (per_dot * rows, rows), 0) % rows
    other = lax.broadcasted_iota(jnp.int32, (per_dot * rows, rows), 1)
    causal = (other <= position) & (other < length)
    against = (((1,), (1,)), ((), ()))
    for g in range(0, heads, per_dot):
        query = jnp.concatenate(
            [turn(q_ref[packed, (g + i) * head_size : (g + i + 1) * head_size]) for i in range(per_dot)]
        ).astype(jnp.bfloat16)
        scores = lax.dot_general(query, pair_ref[0], against, preferred_element_type=jnp.float32)
        own_scores = lax.dot_general(query, own_keys, against, preferred_element_type=jnp.float32)
        own_scores = jnp.where(causal, own_scores, -jnp.inf)
        highest = jnp.maximum(
            jnp.max(scores, axis=-1, keepdims=True), jnp.max(own_scores, axis=-1, keepdims=True)
        )
        weights = jnp.exp((scores - highest) * scale)
        own_weights = jnp.exp((own_scores - highest) * scale)
        total = jnp.sum(weights, axis=-1, keepdims=True) + jnp.sum(own_weights, axis=-1, keepdims=True)
        mixed = jnp.dot(weights.astype(jnp.bfloat16), pair_ref[1], preferred_element_type=jnp.float32)
        mixed = mixed + jnp.dot(
            own_weights.astype(jnp.bfloat16), own_values, preferred_element_type=jnp.float32
        )
        mixed = (mixed / total).astype(jnp.bfloat16)
        for i in range(per_dot):
            att_ref[:, (g + i) * head_size : (g + i + 1) * head_size] = mixed[i * rows : (i + 1) * rows]


def attend(r, suffix_len, model_width, lengths, offsets, sums, tables, pair):
    width = sums[0].shape[1]
    _, prefix_len, head_size = pair.shape
    vmem = pl.BlockSpec(memory_space=pltpu.VMEM)
    smem = pl.BlockSpec(memory_space=pltpu.SMEM)
    return pl.pallas_call(
        functools.partial(attend_kernel, r, model_width),
        in_specs=[smem] * 2 + [vmem] * 6,
        out_specs=[vmem] * 2,
        out_shape=[
            jax.ShapeDtypeStruct((suffix_len, width), jnp.bfloat16),
            jax.ShapeDtypeStruct((suffix_len, 2 * head_size), jnp.bfloat16),
        ],
        compiler_params=pltpu.CompilerParams(vmem_limit_bytes=VMEM_BYTES),
        cost_estimate=pl.CostEstimate(
            flops=4 * suffix_len * width * (prefix_len + suffix_len),
            bytes_accessed=4 * prefix_len * head_size + 4 * suffix_len * (width + 2 * head_size),
            transcendentals=suffix_len * width // head_size * prefix_len,
        ),
    )(lengths, offsets, *sums, *tables, pair)


def copies_kernel(plan, *refs):
    arrived = refs[-1]
    copies = [
        pltpu.make_async_copy(source, target, arrived.at[i])
        for i, (source, target) in enumerate(plan(refs[:-1]))
    ]
    for copy in copies:
        copy.start()
    for copy in copies:
        copy.wait()


def copied(plan, n_copies, scalars, arrays, outs, out_space=pltpu.HBM, vmem_bytes=VMEM_BYTES):
    size = sum(out.size for out in outs)
    return pl.pallas_call(
        functools.partial(copies_kernel, plan),
        in_specs=[pl.BlockSpec(memory_space=pltpu.SMEM)] * len(scalars)
        + [pl.BlockSpec(memory_space=pltpu.HBM)] * len(arrays),
        out_specs=[pl.BlockSpec(memory_space=out_space)] * len(outs),
        out_shape=outs,
        scratch_shapes=[pltpu.SemaphoreType.DMA((n_copies,))],
        compiler_params=pltpu.CompilerParams(vmem_limit_bytes=vmem_bytes),
        cost_estimate=pl.CostEstimate(flops=0, bytes_accessed=4 * size, transcendentals=0),
    )(*scalars, *arrays)


def stage_in(array):
    out = jax.ShapeDtypeStruct(array.shape, array.dtype)
    return copied(lambda refs: [(refs[0], refs[1])], 1, [], [array], [out], pltpu.VMEM)[0]


def first_rows(array, count):
    out = jax.ShapeDtypeStruct((count, array.shape[1]), array.dtype)
    return copied(
        lambda refs: [(refs[0].at[pl.ds(0, count)], refs[1])], 1, [], [array], [out], pltpu.VMEM
    )[0]


def stacked(arrays):
    n = len(arrays)
    out = jax.ShapeDtypeStruct((n,) + arrays[0].shape, arrays[0].dtype)
    return copied(lambda refs: [(refs[i], refs[n].at[i]) for i in range(n)], n, [], arrays, [out])[0]


def cut(array, row, columns, shape):
    n = len(columns)

    def plan(refs):
        begins, whole, outs = refs[0], refs[1], refs[2:]
        rows = pl.ds(pl.multiple_of(begins[0], ROW_TILE), shape[0])
        return [
            (whole.at[rows, pl.ds(pl.multiple_of(begins[i + 1], LANES), shape[1])], outs[i])
            for i in range(n)
        ]

    outs = [jax.ShapeDtypeStruct(shape, array.dtype)] * n
    begins = jnp.stack([row] + columns).astype(jnp.int32)
    return copied(plan, n, [begins], [array], outs, pltpu.VMEM, 58 * 1024 * 1024)


def output_kernel(n_tp, length_ref, *refs):
    own_ref, others_ref, hidden_ref, out_ref = refs[-4:]
    req_count, suffix_len, features = hidden_ref.shape
    chunk = 2 * LANES if features % (2 * LANES) == 0 else LANES
    position = lax.broadcasted_iota(jnp.int32, (suffix_len, chunk), 0)
    attention = [
        jnp.concatenate([refs[r * n_tp + j][...] for r in range(req_count)]) for j in range(n_tp)
    ]
    for begin in range(0, features, chunk):
        columns = slice(begin, begin + chunk)
        mixed = jnp.dot(attention[0], own_ref[:, columns], preferred_element_type=jnp.float32)
        for j in range(1, n_tp):
            weights = others_ref[:, j - 1, :, columns].reshape(own_ref.shape[0], chunk)
            mixed = mixed + jnp.dot(attention[j], weights, preferred_element_type=jnp.float32)
        for r in range(req_count):
            part = mixed[r * suffix_len : (r + 1) * suffix_len]
            part = part + hidden_ref[r, :, columns].astype(jnp.float32)
            part = jnp.where(position < length_ref[r], part, 0.0)
            out_ref[r, :, columns] = part.astype(jnp.bfloat16)


def project_out(lengths, attention, w_own, w_others, hidden):
    req_count, suffix_len, features = hidden.shape
    n_tp = len(attention[0])
    vmem = pl.BlockSpec(memory_space=pltpu.VMEM)
    return pl.pallas_call(
        functools.partial(output_kernel, n_tp),
        in_specs=[pl.BlockSpec(memory_space=pltpu.SMEM)] + [vmem] * (req_count * n_tp + 3),
        out_specs=vmem,
        out_shape=jax.ShapeDtypeStruct(hidden.shape, jnp.bfloat16),
        compiler_params=pltpu.CompilerParams(vmem_limit_bytes=VMEM_BYTES),
        cost_estimate=pl.CostEstimate(
            flops=2 * req_count * suffix_len * features * w_own.shape[0] * n_tp,
            bytes_accessed=2 * features * (w_own.shape[0] * n_tp + 2 * req_count * suffix_len),
            transcendentals=0,
        ),
    )(lengths, *[block for slots in attention for block in slots], w_own, w_others, hidden)


def shards(hidden, norm_gain, w_query, w_kv, w_out, prefix_cache, lengths, groups, owners):
    n_tp = lax.axis_size("tp")
    n_owners = lax.axis_size("req")
    my_index = lax.axis_index("req")
    place = lax.axis_index("tp")
    req_count, suffix_len, features = hidden.shape
    head_size = w_kv.shape[2]
    model_width = w_query.shape[0]

    flat_kv = w_kv.reshape(model_width, 2 * head_size)
    tables = rope_tables(suffix_len, head_size)

    share = w_out.shape[0] // n_owners
    columns = [ring_place(place, j) * features for j in range(1, n_tp)]
    pieces = cut(w_out, my_index * share, columns, (share, features))
    moved = [shift(piece, j) for j, piece in enumerate(pieces, 1)]

    _, prefix_len, _, head_size = prefix_cache.shape
    prefixes = lax.all_gather(prefix_cache.reshape(prefix_len * 2, head_size), "req", axis=0)
    local_groups = lax.dynamic_slice_in_dim(groups, my_index * req_count, req_count)
    owner_of = jnp.sum(
        jnp.where(local_groups[:, None] == jnp.arange(n_owners)[None, :], owners[None, :], 0), axis=-1
    ).astype(jnp.int32)

    def weights_of(begin):
        return (
            lax.dynamic_slice_in_dim(norm_gain, begin, features).reshape(1, features),
            lax.dynamic_slice_in_dim(w_query, begin, features, axis=0),
            lax.dynamic_slice_in_dim(flat_kv, begin, features, axis=0),
        )

    total_rows = req_count * suffix_len
    packed = hidden.reshape(total_rows, features)
    offsets = [jnp.int32(0)]
    for r in range(1, req_count):
        offsets.append(offsets[-1] + (lengths[r - 1] + ROW_TILE - 1) // ROW_TILE * ROW_TILE)
        packed = lax.dynamic_update_slice(packed, hidden[r], (offsets[r], 0))
    live_rows = offsets[-1] + lengths[-1]
    offsets = jnp.stack(offsets)
    capacities = [total_rows * k // 8 for k in range(3, 9)]
    branch = sum((live_rows > capacity).astype(jnp.int32) for capacity in capacities[:-1])

    begins = [ring_place(place, -step) * features for step in range(n_tp)]
    own_sums = project(packed, weights_of(begins[0]), [], total_rows)
    state = (packed, own_sums, moved, tables, begins, owner_of, offsets, branch)
    state = lax.optimization_barrier(state)
    packed, own_sums, moved, tables, begins, owner_of, offsets, branch = state
    w_others = lax.all_gather(stacked(moved), "req", axis=0)

    def ring_of(capacity):
        def run(packed, sums):
            block = first_rows(packed, capacity) if capacity < total_rows else packed
            for step in range(n_tp - 1):
                coming = shift(block, 1)
                if step > 0:
                    sums = project(block, weights, sums, total_rows)
                state = (coming, sums, weights_of(begins[step + 1]))
                block, sums, weights = lax.optimization_barrier(state)
            return project(block, weights, sums, total_rows)

        return run

    sums = lax.switch(branch, [ring_of(c) for c in capacities], packed, own_sums)

    caches, gathered = [], []
    for r in range(req_count):
        pair = lax.dynamic_index_in_dim(prefixes, owner_of[r], 0, keepdims=False)
        pair = pair.reshape(prefix_len, 2, head_size).transpose(1, 0, 2)
        attention, cache = attend(r, suffix_len, model_width, lengths, offsets, sums, tables, pair)
        caches.append(cache)
        gathered.append([attention] + [shift(attention, j) for j in range(1, n_tp)])
    place, _ = lax.optimization_barrier((place, caches[-1]))
    w_own = lax.dynamic_slice_in_dim(w_out, place * features, features, axis=1)

    suffix_cache = jnp.stack(caches).reshape(req_count, suffix_len, 2, head_size)
    w_others, suffix_cache = lax.optimization_barrier((w_others, suffix_cache))
    out_hidden = project_out(lengths, gathered, w_own, stage_in(w_others), hidden)
    return (out_hidden, suffix_cache)


def solution(mesh):
    return jax.shard_map(
        shards,
        mesh=mesh,
        in_specs=(
            P("req", None, "tp"),
            P(),
            P(None, "tp"),
            P(None, None, "tp"),
            P("tp", None),
            P("req", None, None, "tp"),
            P("req"),
            P(),
            P(),
        ),
        out_specs=(P("req", None, "tp"), P("req", None, None, "tp")),
        check_vma=False,
    )
```

```python
import functools

import jax
import jax.numpy as jnp
from jax import lax
from jax.experimental import pallas as pl
from jax.experimental.pallas import tpu as pltpu
from jax.sharding import PartitionSpec as P

PREFIX = 2048


EPSILON = 1e-05
ROPE_BASE = 5000000.0
VMEM_BYTES = 12 * 1024 * 1024
LANES = 128
ROW_TILE = 16


def rope_tables(suffix_len, head_size):
    positions = (PREFIX + jnp.arange(suffix_len)).astype(jnp.float32)
    inverse = ROPE_BASE ** (-(2.0 * jnp.arange(head_size // 2).astype(jnp.float32)) / head_size)
    angles = positions[:, None] * inverse[None, :]
    cosine_table = jnp.concatenate([jnp.cos(angles), jnp.cos(angles)], axis=-1)
    sine_table = jnp.concatenate([-jnp.sin(angles), jnp.sin(angles)], axis=-1)
    return (cosine_table, sine_table)


def ring_order(n):
    return [0] + list(range(1, n, 2)) + list(range(n - 2 if n % 2 == 0 else n - 1, 0, -2))


def ring_place(place, distance):
    n = lax.axis_size("tp")
    ring = ring_order(n)
    return sum(jnp.where(place == ring[p], ring[(p + distance) % n], 0) for p in range(n))


def shift(block, distance):
    n = lax.axis_size("tp")
    ring = ring_order(n)
    return lax.ppermute(block, "tp", [(ring[p], ring[(p + distance) % n]) for p in range(n)])


def chunk_of(size):
    return 2 * LANES if size % (2 * LANES) == 0 else LANES


def project_kernel(block_ref, gain_ref, wq_ref, wkv_ref, *refs):
    sums_in, (q_ref, kv_ref, square_ref) = refs[:-3], refs[-3:]
    rows, features = block_ref.shape
    chunk = chunk_of(features)
    for i, ref in enumerate(refs[-3:]):
        ref[:rows] = sums_in[i][:rows] if sums_in else jnp.zeros((rows, ref.shape[1]), jnp.float32)

    def step(k, _):
        part = pl.ds(pl.multiple_of(k * chunk, chunk), chunk)
        block_f = block_ref[:, part].astype(jnp.float32)
        scaled = (block_f * gain_ref[:, part]).astype(jnp.bfloat16)
        squares = block_f * block_f
        for i in range(chunk // LANES):
            square_ref[:rows] += squares[:, i * LANES : (i + 1) * LANES]
        q_ref[:rows] += jnp.dot(scaled, wq_ref[part, :], preferred_element_type=jnp.float32)
        kv_ref[:rows] += jnp.dot(scaled, wkv_ref[part, :], preferred_element_type=jnp.float32)
        return 0

    lax.fori_loop(0, features // chunk, step, 0)


def project(block, weights, sums, total_rows):
    rows, features = block.shape
    gain, w_query, flat_kv = weights
    widths = (w_query.shape[1], flat_kv.shape[1], LANES)
    vmem = pl.BlockSpec(memory_space=pltpu.VMEM)
    return pl.pallas_call(
        project_kernel,
        in_specs=[vmem] * (4 + len(sums)),
        out_specs=[vmem] * 3,
        out_shape=[jax.ShapeDtypeStruct((total_rows, width), jnp.float32) for width in widths],
        compiler_params=pltpu.CompilerParams(vmem_limit_bytes=VMEM_BYTES),
        cost_estimate=pl.CostEstimate(
            flops=2 * rows * features * (widths[0] + widths[1]),
            bytes_accessed=2 * features * (widths[0] + widths[1] + rows),
            transcendentals=0,
        ),
    )(block, gain, w_query, flat_kv, *sums)


def attend_kernel(
    r, model_width, length_ref, offset_ref, q_ref, kv_ref, square_ref, cos_ref, sin_ref, pair_ref, att_ref, cache_ref
):
    rows = att_ref.shape[0]
    packed = pl.ds(pl.multiple_of(offset_ref[r], ROW_TILE), rows)
    head_size = pair_ref.shape[-1]
    heads = q_ref.shape[1] // head_size
    per_dot = 2 if heads % 2 == 0 else 1
    scale = head_size ** (-0.5)
    length = length_ref[r]
    cosine, sine = cos_ref[...], sin_ref[...]
    mean = jnp.sum(square_ref[packed, :], axis=-1, keepdims=True) / model_width
    row_scale = lax.rsqrt(mean + EPSILON)

    def turn(vector):
        vector = vector * row_scale
        return vector * cosine + pltpu.roll(vector, head_size // 2, 1) * sine

    keys_f = turn(kv_ref[packed, :head_size])
    values_f = kv_ref[packed, head_size:] * row_scale
    live = lax.broadcasted_iota(jnp.int32, (rows, head_size), 0) < length
    own_keys = jnp.where(live, keys_f, 0.0).astype(jnp.bfloat16)
    own_values = jnp.where(live, values_f, 0.0).astype(jnp.bfloat16)
    cache_ref[:, :head_size] = own_keys
    cache_ref[:, head_size:] = own_values

    position = lax.broadcasted_iota(jnp.int32, (per_dot * rows, rows), 0) % rows
    other = lax.broadcasted_iota(jnp.int32, (per_dot * rows, rows), 1)
    causal = (other <= position) & (other < length)
    against = (((1,), (1,)), ((), ()))
    def step(g, _):
        width = per_dot * head_size
        part = pl.ds(pl.multiple_of(g * width, width), width)
        vectors = q_ref[packed, part]
        query = jnp.concatenate(
            [turn(vectors[:, i * head_size : (i + 1) * head_size]) for i in range(per_dot)]
        ).astype(jnp.bfloat16)
        scores = lax.dot_general(query, pair_ref[0], against, preferred_element_type=jnp.float32)
        own_scores = lax.dot_general(query, own_keys, against, preferred_element_type=jnp.float32)
        own_scores = jnp.where(causal, own_scores, -jnp.inf)
        highest = jnp.maximum(
            jnp.max(scores, axis=-1, keepdims=True), jnp.max(own_scores, axis=-1, keepdims=True)
        )
        weights = jnp.exp((scores - highest) * scale)
        own_weights = jnp.exp((own_scores - highest) * scale)
        total = jnp.sum(weights, axis=-1, keepdims=True) + jnp.sum(own_weights, axis=-1, keepdims=True)
        mixed = jnp.dot(weights.astype(jnp.bfloat16), pair_ref[1], preferred_element_type=jnp.float32)
        mixed = mixed + jnp.dot(
            own_weights.astype(jnp.bfloat16), own_values, preferred_element_type=jnp.float32
        )
        mixed = (mixed / total).astype(jnp.bfloat16)
        att_ref[:, part] = jnp.concatenate(
            [mixed[i * rows : (i + 1) * rows] for i in range(per_dot)], axis=1
        )
        return 0

    lax.fori_loop(0, heads // per_dot, step, 0)


def attend(r, suffix_len, model_width, lengths, offsets, sums, tables, pair):
    width = sums[0].shape[1]
    _, prefix_len, head_size = pair.shape
    vmem = pl.BlockSpec(memory_space=pltpu.VMEM)
    smem = pl.BlockSpec(memory_space=pltpu.SMEM)
    return pl.pallas_call(
        functools.partial(attend_kernel, r, model_width),
        in_specs=[smem] * 2 + [vmem] * 6,
        out_specs=[vmem] * 2,
        out_shape=[
            jax.ShapeDtypeStruct((suffix_len, width), jnp.bfloat16),
            jax.ShapeDtypeStruct((suffix_len, 2 * head_size), jnp.bfloat16),
        ],
        compiler_params=pltpu.CompilerParams(vmem_limit_bytes=VMEM_BYTES),
        cost_estimate=pl.CostEstimate(
            flops=4 * suffix_len * width * (prefix_len + suffix_len),
            bytes_accessed=4 * prefix_len * head_size + 4 * suffix_len * (width + 2 * head_size),
            transcendentals=suffix_len * width // head_size * prefix_len,
        ),
    )(lengths, offsets, *sums, *tables, pair)


def copies_kernel(plan, *refs):
    arrived = refs[-1]
    copies = [
        pltpu.make_async_copy(source, target, arrived.at[i])
        for i, (source, target) in enumerate(plan(refs[:-1]))
    ]
    for copy in copies:
        copy.start()
    for copy in copies:
        copy.wait()


def copied(plan, n_copies, scalars, arrays, outs, out_space=pltpu.HBM, vmem_bytes=VMEM_BYTES):
    size = sum(out.size for out in outs)
    return pl.pallas_call(
        functools.partial(copies_kernel, plan),
        in_specs=[pl.BlockSpec(memory_space=pltpu.SMEM)] * len(scalars)
        + [pl.BlockSpec(memory_space=pltpu.HBM)] * len(arrays),
        out_specs=[pl.BlockSpec(memory_space=out_space)] * len(outs),
        out_shape=outs,
        scratch_shapes=[pltpu.SemaphoreType.DMA((n_copies,))],
        compiler_params=pltpu.CompilerParams(vmem_limit_bytes=vmem_bytes),
        cost_estimate=pl.CostEstimate(flops=0, bytes_accessed=4 * size, transcendentals=0),
    )(*scalars, *arrays)


def stage_in(array):
    out = jax.ShapeDtypeStruct(array.shape, array.dtype)
    return copied(lambda refs: [(refs[0], refs[1])], 1, [], [array], [out], pltpu.VMEM)[0]


def first_rows(array, count):
    out = jax.ShapeDtypeStruct((count, array.shape[1]), array.dtype)
    return copied(
        lambda refs: [(refs[0].at[pl.ds(0, count)], refs[1])], 1, [], [array], [out], pltpu.VMEM
    )[0]


def stacked(arrays):
    n = len(arrays)
    out = jax.ShapeDtypeStruct((n,) + arrays[0].shape, arrays[0].dtype)
    return copied(lambda refs: [(refs[i], refs[n].at[i]) for i in range(n)], n, [], arrays, [out])[0]


def cut(array, row, columns, shape):
    n = len(columns)

    def plan(refs):
        begins, whole, outs = refs[0], refs[1], refs[2:]
        rows = pl.ds(pl.multiple_of(begins[0], ROW_TILE), shape[0])
        return [
            (whole.at[rows, pl.ds(pl.multiple_of(begins[i + 1], LANES), shape[1])], outs[i])
            for i in range(n)
        ]

    outs = [jax.ShapeDtypeStruct(shape, array.dtype)] * n
    begins = jnp.stack([row] + columns).astype(jnp.int32)
    return copied(plan, n, [begins], [array], outs, pltpu.VMEM, 58 * 1024 * 1024)


def output_kernel(n_tp, length_ref, *refs):
    own_ref, others_ref, hidden_ref, out_ref, attention = refs[-5:]
    req_count, suffix_len, features = hidden_ref.shape
    chunk = chunk_of(features)
    position = lax.broadcasted_iota(jnp.int32, (suffix_len, chunk), 0)
    for j in range(n_tp):
        for r in range(req_count):
            attention[j, r * suffix_len : (r + 1) * suffix_len] = refs[r * n_tp + j][...]

    def step(c, _):
        columns = pl.ds(pl.multiple_of(c * chunk, chunk), chunk)
        mixed = jnp.dot(attention[0], own_ref[:, columns], preferred_element_type=jnp.float32)
        for j in range(1, n_tp):
            weights = others_ref[:, j - 1, :, columns].reshape(own_ref.shape[0], chunk)
            mixed = mixed + jnp.dot(attention[j], weights, preferred_element_type=jnp.float32)
        for r in range(req_count):
            part = mixed[r * suffix_len : (r + 1) * suffix_len]
            part = part + hidden_ref[r, :, columns].astype(jnp.float32)
            part = jnp.where(position < length_ref[r], part, 0.0)
            out_ref[r, :, columns] = part.astype(jnp.bfloat16)
        return 0

    lax.fori_loop(0, features // chunk, step, 0)


def project_out(lengths, attention, w_own, w_others, hidden):
    req_count, suffix_len, features = hidden.shape
    n_tp = len(attention[0])
    vmem = pl.BlockSpec(memory_space=pltpu.VMEM)
    return pl.pallas_call(
        functools.partial(output_kernel, n_tp),
        in_specs=[pl.BlockSpec(memory_space=pltpu.SMEM)] + [vmem] * (req_count * n_tp + 3),
        out_specs=vmem,
        out_shape=jax.ShapeDtypeStruct(hidden.shape, jnp.bfloat16),
        scratch_shapes=[
            pltpu.VMEM((n_tp, req_count * suffix_len, w_own.shape[0]), jnp.bfloat16)
        ],
        compiler_params=pltpu.CompilerParams(vmem_limit_bytes=VMEM_BYTES),
        cost_estimate=pl.CostEstimate(
            flops=2 * req_count * suffix_len * features * w_own.shape[0] * n_tp,
            bytes_accessed=2 * features * (w_own.shape[0] * n_tp + 2 * req_count * suffix_len),
            transcendentals=0,
        ),
    )(lengths, *[block for slots in attention for block in slots], w_own, w_others, hidden)


def shards(hidden, norm_gain, w_query, w_kv, w_out, prefix_cache, lengths, groups, owners):
    n_tp = lax.axis_size("tp")
    n_owners = lax.axis_size("req")
    my_index = lax.axis_index("req")
    place = lax.axis_index("tp")
    req_count, suffix_len, features = hidden.shape
    head_size = w_kv.shape[2]
    model_width = w_query.shape[0]

    flat_kv = w_kv.reshape(model_width, 2 * head_size)
    tables = rope_tables(suffix_len, head_size)

    share = w_out.shape[0] // n_owners
    columns = [ring_place(place, j) * features for j in range(1, n_tp)]
    pieces = cut(w_out, my_index * share, columns, (share, features))
    moved = [shift(piece, j) for j, piece in enumerate(pieces, 1)]

    _, prefix_len, _, head_size = prefix_cache.shape
    prefixes = lax.all_gather(prefix_cache.reshape(prefix_len * 2, head_size), "req", axis=0)
    local_groups = lax.dynamic_slice_in_dim(groups, my_index * req_count, req_count)
    owner_of = jnp.sum(
        jnp.where(local_groups[:, None] == jnp.arange(n_owners)[None, :], owners[None, :], 0), axis=-1
    ).astype(jnp.int32)

    def weights_of(begin):
        return (
            lax.dynamic_slice_in_dim(norm_gain, begin, features).reshape(1, features),
            lax.dynamic_slice_in_dim(w_query, begin, features, axis=0),
            lax.dynamic_slice_in_dim(flat_kv, begin, features, axis=0),
        )

    total_rows = req_count * suffix_len
    packed = hidden.reshape(total_rows, features)
    offsets = [jnp.int32(0)]
    for r in range(1, req_count):
        offsets.append(offsets[-1] + (lengths[r - 1] + ROW_TILE - 1) // ROW_TILE * ROW_TILE)
        packed = lax.dynamic_update_slice(packed, hidden[r], (offsets[r], 0))
    live_rows = offsets[-1] + lengths[-1]
    offsets = jnp.stack(offsets)
    capacities = [total_rows * k // 8 for k in range(3, 9)]
    branch = sum((live_rows > capacity).astype(jnp.int32) for capacity in capacities[:-1])

    begins = [ring_place(place, -step) * features for step in range(n_tp)]
    own_sums = project(packed, weights_of(begins[0]), [], total_rows)
    state = (packed, own_sums, moved, tables, begins, owner_of, offsets, branch)
    state = lax.optimization_barrier(state)
    packed, own_sums, moved, tables, begins, owner_of, offsets, branch = state
    w_others = lax.all_gather(stacked(moved), "req", axis=0)

    def ring_of(capacity):
        def run(packed, sums):
            block = first_rows(packed, capacity) if capacity < total_rows else packed
            for step in range(n_tp - 1):
                coming = shift(block, 1)
                if step > 0:
                    sums = project(block, weights, sums, total_rows)
                state = (coming, sums, weights_of(begins[step + 1]))
                block, sums, weights = lax.optimization_barrier(state)
            return project(block, weights, sums, total_rows)

        return run

    sums = lax.switch(branch, [ring_of(c) for c in capacities], packed, own_sums)

    caches, gathered = [], []
    for r in range(req_count):
        pair = lax.dynamic_index_in_dim(prefixes, owner_of[r], 0, keepdims=False)
        pair = pair.reshape(prefix_len, 2, head_size).transpose(1, 0, 2)
        attention, cache = attend(r, suffix_len, model_width, lengths, offsets, sums, tables, pair)
        caches.append(cache)
        gathered.append([attention] + [shift(attention, j) for j in range(1, n_tp)])
    place, _ = lax.optimization_barrier((place, caches[-1]))
    w_own = lax.dynamic_slice_in_dim(w_out, place * features, features, axis=1)

    suffix_cache = jnp.stack(caches).reshape(req_count, suffix_len, 2, head_size)
    w_others, suffix_cache = lax.optimization_barrier((w_others, suffix_cache))
    out_hidden = project_out(lengths, gathered, w_own, stage_in(w_others), hidden)
    return (out_hidden, suffix_cache)


def solution(mesh):
    return jax.shard_map(
        shards,
        mesh=mesh,
        in_specs=(
            P("req", None, "tp"),
            P(),
            P(None, "tp"),
            P(None, None, "tp"),
            P("tp", None),
            P("req", None, None, "tp"),
            P("req"),
            P(),
            P(),
        ),
        out_specs=(P("req", None, "tp"), P("req", None, None, "tp")),
        check_vma=False,
    )
```

```python
import functools

import jax
import jax.numpy as jnp
from jax import lax
from jax.experimental import pallas as pl
from jax.experimental.pallas import tpu as pltpu
from jax.sharding import PartitionSpec as P

PREFIX = 2048


EPSILON = 1e-05
ROPE_BASE = 5000000.0
VMEM_BYTES = 12 * 1024 * 1024
LANES = 128
ROW_TILE = 16


def rope_tables(suffix_len, head_size):
    positions = (PREFIX + jnp.arange(suffix_len)).astype(jnp.float32)
    inverse = ROPE_BASE ** (-(2.0 * jnp.arange(head_size // 2).astype(jnp.float32)) / head_size)
    angles = positions[:, None] * inverse[None, :]
    cosine_table = jnp.concatenate([jnp.cos(angles), jnp.cos(angles)], axis=-1)
    sine_table = jnp.concatenate([-jnp.sin(angles), jnp.sin(angles)], axis=-1)
    return (cosine_table, sine_table)


def ring_order(n):
    return [0] + list(range(1, n, 2)) + list(range(n - 2 if n % 2 == 0 else n - 1, 0, -2))


def ring_place(place, distance):
    n = lax.axis_size("tp")
    ring = ring_order(n)
    return sum(jnp.where(place == ring[p], ring[(p + distance) % n], 0) for p in range(n))


def shift(block, distance):
    n = lax.axis_size("tp")
    ring = ring_order(n)
    return lax.ppermute(block, "tp", [(ring[p], ring[(p + distance) % n]) for p in range(n)])


def chunk_of(size):
    return 2 * LANES if size % (2 * LANES) == 0 else LANES


def project_kernel(chunk, block_ref, gain_ref, wq_ref, wkv_ref, *refs):
    sums_in, (q_ref, kv_ref, square_ref) = refs[:-3], refs[-3:]
    rows, features = block_ref.shape

    def parts_of(part):
        block_f = block_ref[:, part].astype(jnp.float32)
        scaled = (block_f * gain_ref[:, part]).astype(jnp.bfloat16)
        squares = block_f * block_f
        square = squares[:, :LANES]
        for i in range(1, chunk // LANES):
            square = square + squares[:, i * LANES : (i + 1) * LANES]
        return (
            jnp.dot(scaled, wq_ref[part, :], preferred_element_type=jnp.float32),
            jnp.dot(scaled, wkv_ref[part, :], preferred_element_type=jnp.float32),
            square,
        )

    parts = parts_of(pl.ds(0, chunk))
    for i, ref in enumerate(refs[-3:]):
        ref[:rows] = sums_in[i][:rows] + parts[i] if sums_in else parts[i]

    def step(k, _):
        parts = parts_of(pl.ds(pl.multiple_of(k * chunk, chunk), chunk))
        for i, ref in enumerate(refs[-3:]):
            ref[:rows] += parts[i]
        return 0

    if chunk < features:
        lax.fori_loop(1, features // chunk, step, 0)


def project(block, weights, sums, total_rows, in_loop=True):
    rows, features = block.shape
    gain, w_query, flat_kv = weights
    widths = (w_query.shape[1], flat_kv.shape[1], LANES)
    vmem = pl.BlockSpec(memory_space=pltpu.VMEM)
    return pl.pallas_call(
        functools.partial(project_kernel, chunk_of(features) if in_loop else features),
        in_specs=[vmem] * (4 + len(sums)),
        out_specs=[vmem] * 3,
        out_shape=[jax.ShapeDtypeStruct((total_rows, width), jnp.float32) for width in widths],
        compiler_params=pltpu.CompilerParams(vmem_limit_bytes=VMEM_BYTES),
        cost_estimate=pl.CostEstimate(
            flops=2 * rows * features * (widths[0] + widths[1]),
            bytes_accessed=2 * features * (widths[0] + widths[1] + rows),
            transcendentals=0,
        ),
    )(block, gain, w_query, flat_kv, *sums)


def attend_kernel(
    r, model_width, length_ref, offset_ref, q_ref, kv_ref, square_ref, cos_ref, sin_ref, pair_ref, att_ref, cache_ref
):
    rows = att_ref.shape[0]
    packed = pl.ds(pl.multiple_of(offset_ref[r], ROW_TILE), rows)
    head_size = pair_ref.shape[-1]
    heads = q_ref.shape[1] // head_size
    per_dot = 2 if heads % 2 == 0 else 1
    scale = head_size ** (-0.5)
    length = length_ref[r]
    cosine, sine = cos_ref[...], sin_ref[...]
    mean = jnp.sum(square_ref[packed, :], axis=-1, keepdims=True) / model_width
    row_scale = lax.rsqrt(mean + EPSILON)

    def turn(vector):
        vector = vector * row_scale
        return vector * cosine + pltpu.roll(vector, head_size // 2, 1) * sine

    keys_f = turn(kv_ref[packed, :head_size])
    values_f = kv_ref[packed, head_size:] * row_scale
    live = lax.broadcasted_iota(jnp.int32, (rows, head_size), 0) < length
    own_keys = jnp.where(live, keys_f, 0.0).astype(jnp.bfloat16)
    own_values = jnp.where(live, values_f, 0.0).astype(jnp.bfloat16)
    cache_ref[:, :head_size] = own_keys
    cache_ref[:, head_size:] = own_values

    position = lax.broadcasted_iota(jnp.int32, (per_dot * rows, rows), 0) % rows
    other = lax.broadcasted_iota(jnp.int32, (per_dot * rows, rows), 1)
    causal = (other <= position) & (other < length)
    against = (((1,), (1,)), ((), ()))
    for g in range(heads // per_dot):
        part = slice(g * per_dot * head_size, (g + 1) * per_dot * head_size)
        vectors = q_ref[packed, part]
        query = jnp.concatenate(
            [turn(vectors[:, i * head_size : (i + 1) * head_size]) for i in range(per_dot)]
        ).astype(jnp.bfloat16)
        scores = lax.dot_general(query, pair_ref[0], against, preferred_element_type=jnp.float32)
        own_scores = lax.dot_general(query, own_keys, against, preferred_element_type=jnp.float32)
        own_scores = jnp.where(causal, own_scores, -jnp.inf)
        highest = jnp.maximum(
            jnp.max(scores, axis=-1, keepdims=True), jnp.max(own_scores, axis=-1, keepdims=True)
        )
        weights = jnp.exp((scores - highest) * scale)
        own_weights = jnp.exp((own_scores - highest) * scale)
        total = jnp.sum(weights, axis=-1, keepdims=True) + jnp.sum(own_weights, axis=-1, keepdims=True)
        mixed = jnp.dot(weights.astype(jnp.bfloat16), pair_ref[1], preferred_element_type=jnp.float32)
        mixed = mixed + jnp.dot(
            own_weights.astype(jnp.bfloat16), own_values, preferred_element_type=jnp.float32
        )
        mixed = (mixed / total).astype(jnp.bfloat16)
        att_ref[:, part] = jnp.concatenate(
            [mixed[i * rows : (i + 1) * rows] for i in range(per_dot)], axis=1
        )


def attend(r, suffix_len, model_width, lengths, offsets, sums, tables, pair):
    width = sums[0].shape[1]
    _, prefix_len, head_size = pair.shape
    vmem = pl.BlockSpec(memory_space=pltpu.VMEM)
    smem = pl.BlockSpec(memory_space=pltpu.SMEM)
    return pl.pallas_call(
        functools.partial(attend_kernel, r, model_width),
        in_specs=[smem] * 2 + [vmem] * 6,
        out_specs=[vmem] * 2,
        out_shape=[
            jax.ShapeDtypeStruct((suffix_len, width), jnp.bfloat16),
            jax.ShapeDtypeStruct((suffix_len, 2 * head_size), jnp.bfloat16),
        ],
        compiler_params=pltpu.CompilerParams(vmem_limit_bytes=VMEM_BYTES),
        cost_estimate=pl.CostEstimate(
            flops=4 * suffix_len * width * (prefix_len + suffix_len),
            bytes_accessed=4 * prefix_len * head_size + 4 * suffix_len * (width + 2 * head_size),
            transcendentals=suffix_len * width // head_size * prefix_len,
        ),
    )(lengths, offsets, *sums, *tables, pair)


def copies_kernel(plan, *refs):
    arrived = refs[-1]
    copies = [
        pltpu.make_async_copy(source, target, arrived.at[i])
        for i, (source, target) in enumerate(plan(refs[:-1]))
    ]
    for copy in copies:
        copy.start()
    for copy in copies:
        copy.wait()


def copied(plan, n_copies, scalars, arrays, outs, out_space=pltpu.HBM, vmem_bytes=VMEM_BYTES):
    size = sum(out.size for out in outs)
    return pl.pallas_call(
        functools.partial(copies_kernel, plan),
        in_specs=[pl.BlockSpec(memory_space=pltpu.SMEM)] * len(scalars)
        + [pl.BlockSpec(memory_space=pltpu.HBM)] * len(arrays),
        out_specs=[pl.BlockSpec(memory_space=out_space)] * len(outs),
        out_shape=outs,
        scratch_shapes=[pltpu.SemaphoreType.DMA((n_copies,))],
        compiler_params=pltpu.CompilerParams(vmem_limit_bytes=vmem_bytes),
        cost_estimate=pl.CostEstimate(flops=0, bytes_accessed=4 * size, transcendentals=0),
    )(*scalars, *arrays)


def stage_in(array):
    out = jax.ShapeDtypeStruct(array.shape, array.dtype)
    return copied(lambda refs: [(refs[0], refs[1])], 1, [], [array], [out], pltpu.VMEM)[0]


def first_rows(array, count):
    out = jax.ShapeDtypeStruct((count, array.shape[1]), array.dtype)
    return copied(
        lambda refs: [(refs[0].at[pl.ds(0, count)], refs[1])], 1, [], [array], [out], pltpu.VMEM
    )[0]


def stacked(arrays):
    n = len(arrays)
    out = jax.ShapeDtypeStruct((n,) + arrays[0].shape, arrays[0].dtype)
    return copied(lambda refs: [(refs[i], refs[n].at[i]) for i in range(n)], n, [], arrays, [out])[0]


def cut(array, row, columns, shape):
    n = len(columns)

    def plan(refs):
        begins, whole, outs = refs[0], refs[1], refs[2:]
        rows = pl.ds(pl.multiple_of(begins[0], ROW_TILE), shape[0])
        return [
            (whole.at[rows, pl.ds(pl.multiple_of(begins[i + 1], LANES), shape[1])], outs[i])
            for i in range(n)
        ]

    outs = [jax.ShapeDtypeStruct(shape, array.dtype)] * n
    begins = jnp.stack([row] + columns).astype(jnp.int32)
    return copied(plan, n, [begins], [array], outs, pltpu.VMEM, 58 * 1024 * 1024)


def most_kernel(n_slots, *refs):
    own_ref, others_ref, hidden_ref, most_ref = refs[-4:]
    req_count, suffix_len, features = hidden_ref.shape
    chunk = chunk_of(features)
    attention = [
        jnp.concatenate([refs[r * n_slots + j][...] for r in range(req_count)]) for j in range(n_slots)
    ]
    for begin in range(0, features, chunk):
        columns = slice(begin, begin + chunk)
        mixed = jnp.dot(attention[0], own_ref[:, columns], preferred_element_type=jnp.float32)
        for j in range(1, n_slots):
            weights = others_ref[:, j - 1, :, columns].reshape(own_ref.shape[0], chunk)
            mixed = mixed + jnp.dot(attention[j], weights, preferred_element_type=jnp.float32)
        for r in range(req_count):
            rows = slice(r * suffix_len, (r + 1) * suffix_len)
            most_ref[rows, columns] = mixed[rows] + hidden_ref[r, :, columns].astype(jnp.float32)


def last_kernel(length_ref, attention_ref, others_ref, most_ref, out_ref):
    req_count, suffix_len, features = out_ref.shape
    chunk = chunk_of(features)
    position = lax.broadcasted_iota(jnp.int32, (suffix_len, chunk), 0)
    for begin in range(0, features, chunk):
        columns = slice(begin, begin + chunk)
        weights = others_ref[:, others_ref.shape[1] - 1, :, columns]
        weights = weights.reshape(attention_ref.shape[1], chunk)
        mixed = jnp.dot(attention_ref[...], weights, preferred_element_type=jnp.float32)
        mixed = mixed + most_ref[:, columns]
        for r in range(req_count):
            part = mixed[r * suffix_len : (r + 1) * suffix_len]
            part = jnp.where(position < length_ref[r], part, 0.0)
            out_ref[r, :, columns] = part.astype(jnp.bfloat16)


def project_out(lengths, attention, last_slot, w_own, w_others, hidden):
    req_count, suffix_len, features = hidden.shape
    n_slots = len(attention[0])
    rows = req_count * suffix_len
    vmem = pl.BlockSpec(memory_space=pltpu.VMEM)
    params = pltpu.CompilerParams(vmem_limit_bytes=VMEM_BYTES)
    flops = 2 * rows * features * w_own.shape[0]
    most = pl.pallas_call(
        functools.partial(most_kernel, n_slots),
        in_specs=[vmem] * (req_count * n_slots + 3),
        out_specs=vmem,
        out_shape=jax.ShapeDtypeStruct((rows, features), jnp.float32),
        compiler_params=params,
        cost_estimate=pl.CostEstimate(
            flops=flops * n_slots,
            bytes_accessed=2 * features * (w_own.shape[0] * n_slots + 3 * rows),
            transcendentals=0,
        ),
    )(*[block for slots in attention for block in slots], w_own, w_others, hidden)
    return pl.pallas_call(
        last_kernel,
        in_specs=[pl.BlockSpec(memory_space=pltpu.SMEM)] + [vmem] * 3,
        out_specs=vmem,
        out_shape=jax.ShapeDtypeStruct(hidden.shape, jnp.bfloat16),
        compiler_params=params,
        cost_estimate=pl.CostEstimate(
            flops=flops,
            bytes_accessed=2 * features * (w_own.shape[0] + 3 * rows),
            transcendentals=0,
        ),
    )(lengths, last_slot, w_others, most)


def shards(hidden, norm_gain, w_query, w_kv, w_out, prefix_cache, lengths, groups, owners):
    n_tp = lax.axis_size("tp")
    n_owners = lax.axis_size("req")
    my_index = lax.axis_index("req")
    place = lax.axis_index("tp")
    req_count, suffix_len, features = hidden.shape
    head_size = w_kv.shape[2]
    model_width = w_query.shape[0]

    flat_kv = w_kv.reshape(model_width, 2 * head_size)
    tables = rope_tables(suffix_len, head_size)

    share = w_out.shape[0] // n_owners
    columns = [ring_place(place, j) * features for j in range(1, n_tp)]
    pieces = cut(w_out, my_index * share, columns, (share, features))
    moved = [shift(piece, j) for j, piece in enumerate(pieces, 1)]

    _, prefix_len, _, head_size = prefix_cache.shape
    prefixes = lax.all_gather(prefix_cache.reshape(prefix_len * 2, head_size), "req", axis=0)
    local_groups = lax.dynamic_slice_in_dim(groups, my_index * req_count, req_count)
    owner_of = jnp.sum(
        jnp.where(local_groups[:, None] == jnp.arange(n_owners)[None, :], owners[None, :], 0), axis=-1
    ).astype(jnp.int32)

    def weights_of(begin):
        return (
            lax.dynamic_slice_in_dim(norm_gain, begin, features).reshape(1, features),
            lax.dynamic_slice_in_dim(w_query, begin, features, axis=0),
            lax.dynamic_slice_in_dim(flat_kv, begin, features, axis=0),
        )

    total_rows = req_count * suffix_len
    packed = hidden.reshape(total_rows, features)
    offsets = [jnp.int32(0)]
    for r in range(1, req_count):
        offsets.append(offsets[-1] + (lengths[r - 1] + ROW_TILE - 1) // ROW_TILE * ROW_TILE)
        packed = lax.dynamic_update_slice(packed, hidden[r], (offsets[r], 0))
    live_rows = offsets[-1] + lengths[-1]
    offsets = jnp.stack(offsets)
    capacities = [total_rows * k // 8 for k in range(4, 9)]
    branch = sum((live_rows > capacity).astype(jnp.int32) for capacity in capacities[:-1])

    begins = [ring_place(place, -step) * features for step in range(n_tp)]
    own_sums = project(packed, weights_of(begins[0]), [], total_rows)
    state = (packed, own_sums, moved, tables, begins, owner_of, offsets, branch)
    state = lax.optimization_barrier(state)
    packed, own_sums, moved, tables, begins, owner_of, offsets, branch = state
    w_others = lax.all_gather(stacked(moved), "req", axis=0)

    def ring_of(capacity):
        def run(packed, sums):
            block = first_rows(packed, capacity) if capacity < total_rows else packed
            for step in range(n_tp - 1):
                coming = shift(block, 1)
                if step > 0:
                    sums = project(block, weights, sums, total_rows)
                state = (coming, sums, weights_of(begins[step + 1]))
                block, sums, weights = lax.optimization_barrier(state)
            return project(block, weights, sums, total_rows, in_loop=False)

        return run

    sums = lax.switch(branch, [ring_of(c) for c in capacities], packed, own_sums)

    caches, gathered, own = [], [], []
    for r in range(req_count):
        pair = lax.dynamic_index_in_dim(prefixes, owner_of[r], 0, keepdims=False)
        pair = pair.reshape(prefix_len, 2, head_size).transpose(1, 0, 2)
        attention, cache = attend(r, suffix_len, model_width, lengths, offsets, sums, tables, pair)
        caches.append(cache)
        own.append(attention)
        gathered.append([attention] + [shift(attention, j) for j in range(1, n_tp - 1)])
        prefixes = lax.optimization_barrier(prefixes)
    last_slot = shift(jnp.concatenate(own), n_tp - 1)
    place, _ = lax.optimization_barrier((place, caches[-1]))
    w_own = lax.dynamic_slice_in_dim(w_out, place * features, features, axis=1)

    suffix_cache = jnp.stack(caches).reshape(req_count, suffix_len, 2, head_size)
    w_others, suffix_cache = lax.optimization_barrier((w_others, suffix_cache))
    out_hidden = project_out(lengths, gathered, last_slot, w_own, stage_in(w_others), hidden)
    return (out_hidden, suffix_cache)


def solution(mesh):
    return jax.shard_map(
        shards,
        mesh=mesh,
        in_specs=(
            P("req", None, "tp"),
            P(),
            P(None, "tp"),
            P(None, None, "tp"),
            P("tp", None),
            P("req", None, None, "tp"),
            P("req"),
            P(),
            P(),
        ),
        out_specs=(P("req", None, "tp"), P("req", None, None, "tp")),
        check_vma=False,
    )
```

```python
import functools

import jax
import jax.numpy as jnp
from jax import lax
from jax.experimental import pallas as pl
from jax.experimental.pallas import tpu as pltpu
from jax.sharding import PartitionSpec as P

PREFIX = 2048


EPSILON = 1e-05
ROPE_BASE = 5000000.0
VMEM_BYTES = 12 * 1024 * 1024
LANES = 128
ROW_TILE = 16


def rope_tables(suffix_len, head_size):
    positions = (PREFIX + jnp.arange(suffix_len)).astype(jnp.float32)
    inverse = ROPE_BASE ** (-(2.0 * jnp.arange(head_size // 2).astype(jnp.float32)) / head_size)
    angles = positions[:, None] * inverse[None, :]
    cosine_table = jnp.concatenate([jnp.cos(angles), jnp.cos(angles)], axis=-1)
    sine_table = jnp.concatenate([-jnp.sin(angles), jnp.sin(angles)], axis=-1)
    return (cosine_table, sine_table)


def ring_order(n):
    return [0] + list(range(1, n, 2)) + list(range(n - 2 if n % 2 == 0 else n - 1, 0, -2))


def ring_place(place, distance):
    n = lax.axis_size("tp")
    ring = ring_order(n)
    return sum(jnp.where(place == ring[p], ring[(p + distance) % n], 0) for p in range(n))


def shift(block, distance):
    n = lax.axis_size("tp")
    ring = ring_order(n)
    return lax.ppermute(block, "tp", [(ring[p], ring[(p + distance) % n]) for p in range(n)])


def chunk_of(size):
    return 2 * LANES if size % (2 * LANES) == 0 else LANES


def project_kernel(chunk, n_blocks, *refs):
    blocks, (gain_ref, wq_ref, wkv_ref) = refs[:n_blocks], refs[n_blocks : n_blocks + 3]
    sums_in = refs[n_blocks + 3 : -3]
    rows, features = sum(block.shape[0] for block in blocks), blocks[0].shape[1]

    def parts_of(part):
        block = jnp.concatenate([block[:, part] for block in blocks])
        block_f = block.astype(jnp.float32)
        scaled = (block_f * gain_ref[:, part]).astype(jnp.bfloat16)
        squares = block_f * block_f
        square = squares[:, :LANES]
        for i in range(1, chunk // LANES):
            square = square + squares[:, i * LANES : (i + 1) * LANES]
        return (
            jnp.dot(scaled, wq_ref[part, :], preferred_element_type=jnp.float32),
            jnp.dot(scaled, wkv_ref[part, :], preferred_element_type=jnp.float32),
            square,
        )

    parts = parts_of(pl.ds(0, chunk))
    for i, ref in enumerate(refs[-3:]):
        ref[:rows] = sums_in[i][:rows] + parts[i] if sums_in else parts[i]

    def step(k, _):
        parts = parts_of(pl.ds(pl.multiple_of(k * chunk, chunk), chunk))
        for i, ref in enumerate(refs[-3:]):
            ref[:rows] += parts[i]
        return 0

    if chunk < features:
        lax.fori_loop(1, features // chunk, step, 0)


def project(blocks, weights, sums, total_rows, in_loop=True):
    rows, features = sum(block.shape[0] for block in blocks), blocks[0].shape[1]
    gain, w_query, flat_kv = weights
    widths = (w_query.shape[1], flat_kv.shape[1], LANES)
    vmem = pl.BlockSpec(memory_space=pltpu.VMEM)
    return pl.pallas_call(
        functools.partial(project_kernel, chunk_of(features) if in_loop else features, len(blocks)),
        in_specs=[vmem] * (len(blocks) + 3 + len(sums)),
        out_specs=[vmem] * 3,
        out_shape=[jax.ShapeDtypeStruct((total_rows, width), jnp.float32) for width in widths],
        compiler_params=pltpu.CompilerParams(vmem_limit_bytes=VMEM_BYTES),
        cost_estimate=pl.CostEstimate(
            flops=2 * rows * features * (widths[0] + widths[1]),
            bytes_accessed=2 * features * (widths[0] + widths[1] + rows),
            transcendentals=0,
        ),
    )(*blocks, gain, w_query, flat_kv, *sums)


def attend_kernel(
    r, model_width, length_ref, offset_ref, q_ref, kv_ref, square_ref, cos_ref, sin_ref, pair_ref, att_ref, cache_ref
):
    rows = att_ref.shape[0]
    packed = pl.ds(pl.multiple_of(offset_ref[r], ROW_TILE), rows)
    head_size = pair_ref.shape[-1]
    heads = q_ref.shape[1] // head_size
    per_dot = 2 if heads % 2 == 0 else 1
    scale = head_size ** (-0.5)
    length = length_ref[r]
    cosine, sine = cos_ref[...], sin_ref[...]
    mean = jnp.sum(square_ref[packed, :], axis=-1, keepdims=True) / model_width
    row_scale = lax.rsqrt(mean + EPSILON)

    def turn(vector):
        vector = vector * row_scale
        return vector * cosine + pltpu.roll(vector, head_size // 2, 1) * sine

    keys_f = turn(kv_ref[packed, :head_size])
    values_f = kv_ref[packed, head_size:] * row_scale
    live = lax.broadcasted_iota(jnp.int32, (rows, head_size), 0) < length
    own_keys = jnp.where(live, keys_f, 0.0).astype(jnp.bfloat16)
    own_values = jnp.where(live, values_f, 0.0).astype(jnp.bfloat16)
    cache_ref[:, :head_size] = own_keys
    cache_ref[:, head_size:] = own_values

    position = lax.broadcasted_iota(jnp.int32, (per_dot * rows, rows), 0) % rows
    other = lax.broadcasted_iota(jnp.int32, (per_dot * rows, rows), 1)
    causal = (other <= position) & (other < length)
    against = (((1,), (1,)), ((), ()))
    for g in range(heads // per_dot):
        part = slice(g * per_dot * head_size, (g + 1) * per_dot * head_size)
        vectors = q_ref[packed, part]
        query = jnp.concatenate(
            [turn(vectors[:, i * head_size : (i + 1) * head_size]) for i in range(per_dot)]
        ).astype(jnp.bfloat16)
        scores = lax.dot_general(query, pair_ref[0], against, preferred_element_type=jnp.float32)
        own_scores = lax.dot_general(query, own_keys, against, preferred_element_type=jnp.float32)
        own_scores = jnp.where(causal, own_scores, -jnp.inf)
        highest = jnp.maximum(
            jnp.max(scores, axis=-1, keepdims=True), jnp.max(own_scores, axis=-1, keepdims=True)
        )
        weights = jnp.exp((scores - highest) * scale)
        own_weights = jnp.exp((own_scores - highest) * scale)
        total = jnp.sum(weights, axis=-1, keepdims=True) + jnp.sum(own_weights, axis=-1, keepdims=True)
        mixed = jnp.dot(weights.astype(jnp.bfloat16), pair_ref[1], preferred_element_type=jnp.float32)
        mixed = mixed + jnp.dot(
            own_weights.astype(jnp.bfloat16), own_values, preferred_element_type=jnp.float32
        )
        mixed = (mixed / total).astype(jnp.bfloat16)
        att_ref[:, part] = jnp.concatenate(
            [mixed[i * rows : (i + 1) * rows] for i in range(per_dot)], axis=1
        )


def attend(r, suffix_len, model_width, lengths, offsets, sums, tables, pair):
    width = sums[0].shape[1]
    _, prefix_len, head_size = pair.shape
    vmem = pl.BlockSpec(memory_space=pltpu.VMEM)
    smem = pl.BlockSpec(memory_space=pltpu.SMEM)
    return pl.pallas_call(
        functools.partial(attend_kernel, r, model_width),
        in_specs=[smem] * 2 + [vmem] * 6,
        out_specs=[vmem] * 2,
        out_shape=[
            jax.ShapeDtypeStruct((suffix_len, width), jnp.bfloat16),
            jax.ShapeDtypeStruct((suffix_len, 2 * head_size), jnp.bfloat16),
        ],
        compiler_params=pltpu.CompilerParams(vmem_limit_bytes=VMEM_BYTES),
        cost_estimate=pl.CostEstimate(
            flops=4 * suffix_len * width * (prefix_len + suffix_len),
            bytes_accessed=4 * prefix_len * head_size + 4 * suffix_len * (width + 2 * head_size),
            transcendentals=suffix_len * width // head_size * prefix_len,
        ),
    )(lengths, offsets, *sums, *tables, pair)


def copies_kernel(plan, *refs):
    arrived = refs[-1]
    copies = [
        pltpu.make_async_copy(source, target, arrived.at[i])
        for i, (source, target) in enumerate(plan(refs[:-1]))
    ]
    for copy in copies:
        copy.start()
    for copy in copies:
        copy.wait()


def copied(plan, n_copies, scalars, arrays, outs, out_space=pltpu.HBM, vmem_bytes=VMEM_BYTES):
    size = sum(out.size for out in outs)
    return pl.pallas_call(
        functools.partial(copies_kernel, plan),
        in_specs=[pl.BlockSpec(memory_space=pltpu.SMEM)] * len(scalars)
        + [pl.BlockSpec(memory_space=pltpu.HBM)] * len(arrays),
        out_specs=[pl.BlockSpec(memory_space=out_space)] * len(outs),
        out_shape=outs,
        scratch_shapes=[pltpu.SemaphoreType.DMA((n_copies,))],
        compiler_params=pltpu.CompilerParams(vmem_limit_bytes=vmem_bytes),
        cost_estimate=pl.CostEstimate(flops=0, bytes_accessed=4 * size, transcendentals=0),
    )(*scalars, *arrays)


def stage_in(array):
    out = jax.ShapeDtypeStruct(array.shape, array.dtype)
    return copied(lambda refs: [(refs[0], refs[1])], 1, [], [array], [out], pltpu.VMEM)[0]


def first_rows(array, count, parts):
    size = count // parts
    outs = [jax.ShapeDtypeStruct((size, array.shape[1]), array.dtype)] * parts

    def plan(refs):
        return [(refs[0].at[pl.ds(i * size, size)], refs[i + 1]) for i in range(parts)]

    return copied(plan, parts, [], [array], outs, pltpu.VMEM)


def stacked(arrays):
    n = len(arrays)
    out = jax.ShapeDtypeStruct((n,) + arrays[0].shape, arrays[0].dtype)
    return copied(lambda refs: [(refs[i], refs[n].at[i]) for i in range(n)], n, [], arrays, [out])[0]


def cut(array, row, columns, shape):
    n = len(columns)

    def plan(refs):
        begins, whole, outs = refs[0], refs[1], refs[2:]
        rows = pl.ds(pl.multiple_of(begins[0], ROW_TILE), shape[0])
        return [
            (whole.at[rows, pl.ds(pl.multiple_of(begins[i + 1], LANES), shape[1])], outs[i])
            for i in range(n)
        ]

    outs = [jax.ShapeDtypeStruct(shape, array.dtype)] * n
    begins = jnp.stack([row] + columns).astype(jnp.int32)
    return copied(plan, n, [begins], [array], outs, pltpu.VMEM, 58 * 1024 * 1024)


def most_kernel(n_slots, *refs):
    own_ref, others_ref, hidden_ref, most_ref = refs[-4:]
    req_count, suffix_len, features = hidden_ref.shape
    chunk = chunk_of(features)
    attention = [
        jnp.concatenate([refs[r * n_slots + j][...] for r in range(req_count)]) for j in range(n_slots)
    ]
    for begin in range(0, features, chunk):
        columns = slice(begin, begin + chunk)
        mixed = jnp.dot(attention[0], own_ref[:, columns], preferred_element_type=jnp.float32)
        for j in range(1, n_slots):
            weights = others_ref[:, j - 1, :, columns].reshape(own_ref.shape[0], chunk)
            mixed = mixed + jnp.dot(attention[j], weights, preferred_element_type=jnp.float32)
        for r in range(req_count):
            rows = slice(r * suffix_len, (r + 1) * suffix_len)
            most_ref[rows, columns] = mixed[rows] + hidden_ref[r, :, columns].astype(jnp.float32)


def last_kernel(length_ref, attention_ref, others_ref, most_ref, out_ref):
    req_count, suffix_len, features = out_ref.shape
    chunk = chunk_of(features)
    position = lax.broadcasted_iota(jnp.int32, (suffix_len, chunk), 0)
    for begin in range(0, features, chunk):
        columns = slice(begin, begin + chunk)
        weights = others_ref[:, others_ref.shape[1] - 1, :, columns]
        weights = weights.reshape(attention_ref.shape[1], chunk)
        mixed = jnp.dot(attention_ref[...], weights, preferred_element_type=jnp.float32)
        mixed = mixed + most_ref[:, columns]
        for r in range(req_count):
            part = mixed[r * suffix_len : (r + 1) * suffix_len]
            part = jnp.where(position < length_ref[r], part, 0.0)
            out_ref[r, :, columns] = part.astype(jnp.bfloat16)


def project_out(lengths, attention, last_slot, w_own, w_others, hidden):
    req_count, suffix_len, features = hidden.shape
    n_slots = len(attention[0])
    rows = req_count * suffix_len
    vmem = pl.BlockSpec(memory_space=pltpu.VMEM)
    params = pltpu.CompilerParams(vmem_limit_bytes=VMEM_BYTES)
    flops = 2 * rows * features * w_own.shape[0]
    most = pl.pallas_call(
        functools.partial(most_kernel, n_slots),
        in_specs=[vmem] * (req_count * n_slots + 3),
        out_specs=vmem,
        out_shape=jax.ShapeDtypeStruct((rows, features), jnp.float32),
        compiler_params=params,
        cost_estimate=pl.CostEstimate(
            flops=flops * n_slots,
            bytes_accessed=2 * features * (w_own.shape[0] * n_slots + 3 * rows),
            transcendentals=0,
        ),
    )(*[block for slots in attention for block in slots], w_own, w_others, hidden)
    return pl.pallas_call(
        last_kernel,
        in_specs=[pl.BlockSpec(memory_space=pltpu.SMEM)] + [vmem] * 3,
        out_specs=vmem,
        out_shape=jax.ShapeDtypeStruct(hidden.shape, jnp.bfloat16),
        compiler_params=params,
        cost_estimate=pl.CostEstimate(
            flops=flops,
            bytes_accessed=2 * features * (w_own.shape[0] + 3 * rows),
            transcendentals=0,
        ),
    )(lengths, last_slot, w_others, most)


def shards(hidden, norm_gain, w_query, w_kv, w_out, prefix_cache, lengths, groups, owners):
    n_tp = lax.axis_size("tp")
    n_owners = lax.axis_size("req")
    my_index = lax.axis_index("req")
    place = lax.axis_index("tp")
    req_count, suffix_len, features = hidden.shape
    head_size = w_kv.shape[2]
    model_width = w_query.shape[0]

    flat_kv = w_kv.reshape(model_width, 2 * head_size)
    tables = rope_tables(suffix_len, head_size)

    share = w_out.shape[0] // n_owners
    columns = [ring_place(place, j) * features for j in range(1, n_tp)]
    pieces = cut(w_out, my_index * share, columns, (share, features))
    moved = [shift(piece, j) for j, piece in enumerate(pieces, 1)]

    _, prefix_len, _, head_size = prefix_cache.shape
    prefixes = lax.all_gather(prefix_cache.reshape(prefix_len * 2, head_size), "req", axis=0)
    local_groups = lax.dynamic_slice_in_dim(groups, my_index * req_count, req_count)
    owner_of = jnp.sum(
        jnp.where(local_groups[:, None] == jnp.arange(n_owners)[None, :], owners[None, :], 0), axis=-1
    ).astype(jnp.int32)

    def weights_of(begin):
        return (
            lax.dynamic_slice_in_dim(norm_gain, begin, features).reshape(1, features),
            lax.dynamic_slice_in_dim(w_query, begin, features, axis=0),
            lax.dynamic_slice_in_dim(flat_kv, begin, features, axis=0),
        )

    total_rows = req_count * suffix_len
    packed = hidden.reshape(total_rows, features)
    offsets = [jnp.int32(0)]
    for r in range(1, req_count):
        offsets.append(offsets[-1] + (lengths[r - 1] + ROW_TILE - 1) // ROW_TILE * ROW_TILE)
        packed = lax.dynamic_update_slice(packed, hidden[r], (offsets[r], 0))
    live_rows = offsets[-1] + lengths[-1]
    offsets = jnp.stack(offsets)
    capacities = [total_rows * k // 8 for k in range(4, 9)]
    branch = sum((live_rows > capacity).astype(jnp.int32) for capacity in capacities[:-1])

    begins = [ring_place(place, -step) * features for step in range(n_tp)]
    own_sums = project([packed], weights_of(begins[0]), [], total_rows)
    state = (packed, own_sums, moved, tables, begins, owner_of, offsets, branch)
    state = lax.optimization_barrier(state)
    packed, own_sums, moved, tables, begins, owner_of, offsets, branch = state
    w_others = lax.all_gather(stacked(moved), "req", axis=0)

    def ring_of(capacity):
        def run(packed, sums):
            blocks = first_rows(packed, capacity, 2)
            for step in range(n_tp - 1):
                coming = [shift(block, 1) for block in blocks]
                if step > 0:
                    sums = project(blocks, weights, sums, total_rows)
                state = (coming, sums, weights_of(begins[step + 1]))
                blocks, sums, weights = lax.optimization_barrier(state)
            return project(blocks, weights, sums, total_rows, in_loop=False)

        return run

    sums = lax.switch(branch, [ring_of(c) for c in capacities], packed, own_sums)

    caches, gathered, own = [], [], []
    for r in range(req_count):
        pair = lax.dynamic_index_in_dim(prefixes, owner_of[r], 0, keepdims=False)
        pair = pair.reshape(prefix_len, 2, head_size).transpose(1, 0, 2)
        attention, cache = attend(r, suffix_len, model_width, lengths, offsets, sums, tables, pair)
        caches.append(cache)
        own.append(attention)
        gathered.append([attention] + [shift(attention, j) for j in range(1, n_tp - 1)])
        prefixes = lax.optimization_barrier(prefixes)
    last_slot = shift(jnp.concatenate(own), n_tp - 1)
    place, _ = lax.optimization_barrier((place, caches[-1]))
    w_own = lax.dynamic_slice_in_dim(w_out, place * features, features, axis=1)

    suffix_cache = jnp.stack(caches).reshape(req_count, suffix_len, 2, head_size)
    w_others, suffix_cache = lax.optimization_barrier((w_others, suffix_cache))
    out_hidden = project_out(lengths, gathered, last_slot, w_own, stage_in(w_others), hidden)
    return (out_hidden, suffix_cache)


def solution(mesh):
    return jax.shard_map(
        shards,
        mesh=mesh,
        in_specs=(
            P("req", None, "tp"),
            P(),
            P(None, "tp"),
            P(None, None, "tp"),
            P("tp", None),
            P("req", None, None, "tp"),
            P("req"),
            P(),
            P(),
        ),
        out_specs=(P("req", None, "tp"), P("req", None, None, "tp")),
        check_vma=False,
    )
```

```python
import functools

import jax
import jax.numpy as jnp
from jax import lax
from jax.experimental import pallas as pl
from jax.experimental.pallas import tpu as pltpu
from jax.sharding import PartitionSpec as P

PREFIX = 2048


EPSILON = 1e-05
ROPE_BASE = 5000000.0
VMEM_BYTES = 12 * 1024 * 1024
LANES = 128
ROW_TILE = 16


def rope_tables(suffix_len, head_size):
    positions = (PREFIX + jnp.arange(suffix_len)).astype(jnp.float32)
    inverse = ROPE_BASE ** (-(2.0 * jnp.arange(head_size // 2).astype(jnp.float32)) / head_size)
    angles = positions[:, None] * inverse[None, :]
    cosine_table = jnp.concatenate([jnp.cos(angles), jnp.cos(angles)], axis=-1)
    sine_table = jnp.concatenate([-jnp.sin(angles), jnp.sin(angles)], axis=-1)
    return (cosine_table, sine_table)


def ring_order(n):
    return [0] + list(range(1, n, 2)) + list(range(n - 2 if n % 2 == 0 else n - 1, 0, -2))


def ring_place(place, distance):
    n = lax.axis_size("tp")
    ring = ring_order(n)
    return sum(jnp.where(place == ring[p], ring[(p + distance) % n], 0) for p in range(n))


def shift(block, distance):
    n = lax.axis_size("tp")
    ring = ring_order(n)
    return lax.ppermute(block, "tp", [(ring[p], ring[(p + distance) % n]) for p in range(n)])


def chunk_of(size):
    return 2 * LANES if size % (2 * LANES) == 0 else LANES


def project_kernel(chunk, block_ref, gain_ref, wq_ref, wkv_ref, *refs):
    sums_in, (q_ref, kv_ref, square_ref) = refs[:-3], refs[-3:]
    rows, features = block_ref.shape

    def parts_of(part):
        block_f = block_ref[:, part].astype(jnp.float32)
        scaled = (block_f * gain_ref[:, part]).astype(jnp.bfloat16)
        squares = block_f * block_f
        square = squares[:, :LANES]
        for i in range(1, chunk // LANES):
            square = square + squares[:, i * LANES : (i + 1) * LANES]
        return (
            jnp.dot(scaled, wq_ref[part, :], preferred_element_type=jnp.float32),
            jnp.dot(scaled, wkv_ref[part, :], preferred_element_type=jnp.float32),
            square,
        )

    parts = parts_of(pl.ds(0, chunk))
    for i, ref in enumerate(refs[-3:]):
        ref[:rows] = sums_in[i][:rows] + parts[i] if sums_in else parts[i]

    def step(k, _):
        parts = parts_of(pl.ds(pl.multiple_of(k * chunk, chunk), chunk))
        for i, ref in enumerate(refs[-3:]):
            ref[:rows] += parts[i]
        return 0

    if chunk < features:
        lax.fori_loop(1, features // chunk, step, 0)


def project(block, weights, sums, total_rows, in_loop=True):
    rows, features = block.shape
    gain, w_query, flat_kv = weights
    widths = (w_query.shape[1], flat_kv.shape[1], LANES)
    vmem = pl.BlockSpec(memory_space=pltpu.VMEM)
    return pl.pallas_call(
        functools.partial(project_kernel, chunk_of(features) if in_loop else features),
        in_specs=[vmem] * (4 + len(sums)),
        out_specs=[vmem] * 3,
        out_shape=[jax.ShapeDtypeStruct((total_rows, width), jnp.float32) for width in widths],
        compiler_params=pltpu.CompilerParams(vmem_limit_bytes=VMEM_BYTES),
        cost_estimate=pl.CostEstimate(
            flops=2 * rows * features * (widths[0] + widths[1]),
            bytes_accessed=2 * features * (widths[0] + widths[1] + rows),
            transcendentals=0,
        ),
    )(block, gain, w_query, flat_kv, *sums)


def attend_kernel(
    r, last, model_width, length_ref, offset_ref, q_ref, kv_ref, square_ref, cos_ref, sin_ref, pair_ref, *refs
):
    rows = cos_ref.shape[0]
    n_earlier = 2 * r if last else 0
    earlier, att_ref, outs = refs[:n_earlier], refs[n_earlier], refs[n_earlier + 1 :]
    for i in range(n_earlier):
        outs[i % 2][i // 2 * rows : (i // 2 + 1) * rows] = earlier[i][...]
    mine = slice(r * rows, (r + 1) * rows) if last else slice(0, rows)
    cache_ref = outs[1] if last else outs[0]
    packed = pl.ds(pl.multiple_of(offset_ref[r], ROW_TILE), rows)
    head_size = pair_ref.shape[-1]
    heads = q_ref.shape[1] // head_size
    per_dot = 2 if heads % 2 == 0 else 1
    scale = head_size ** (-0.5)
    length = length_ref[r]
    cosine, sine = cos_ref[...], sin_ref[...]
    mean = jnp.sum(square_ref[packed, :], axis=-1, keepdims=True) / model_width
    row_scale = lax.rsqrt(mean + EPSILON)

    def turn(vector):
        vector = vector * row_scale
        return vector * cosine + pltpu.roll(vector, head_size // 2, 1) * sine

    keys_f = turn(kv_ref[packed, :head_size])
    values_f = kv_ref[packed, head_size:] * row_scale
    live = lax.broadcasted_iota(jnp.int32, (rows, head_size), 0) < length
    own_keys = jnp.where(live, keys_f, 0.0).astype(jnp.bfloat16)
    own_values = jnp.where(live, values_f, 0.0).astype(jnp.bfloat16)
    cache_ref[mine, :head_size] = own_keys
    cache_ref[mine, head_size:] = own_values

    position = lax.broadcasted_iota(jnp.int32, (per_dot * rows, rows), 0) % rows
    other = lax.broadcasted_iota(jnp.int32, (per_dot * rows, rows), 1)
    causal = (other <= position) & (other < length)
    against = (((1,), (1,)), ((), ()))
    for g in range(heads // per_dot):
        part = slice(g * per_dot * head_size, (g + 1) * per_dot * head_size)
        vectors = q_ref[packed, part]
        query = jnp.concatenate(
            [turn(vectors[:, i * head_size : (i + 1) * head_size]) for i in range(per_dot)]
        ).astype(jnp.bfloat16)
        scores = lax.dot_general(query, pair_ref[0], against, preferred_element_type=jnp.float32)
        own_scores = lax.dot_general(query, own_keys, against, preferred_element_type=jnp.float32)
        own_scores = jnp.where(causal, own_scores, -jnp.inf)
        highest = jnp.maximum(
            jnp.max(scores, axis=-1, keepdims=True), jnp.max(own_scores, axis=-1, keepdims=True)
        )
        weights = jnp.exp((scores - highest) * scale)
        own_weights = jnp.exp((own_scores - highest) * scale)
        total = jnp.sum(weights, axis=-1, keepdims=True) + jnp.sum(own_weights, axis=-1, keepdims=True)
        mixed = jnp.dot(weights.astype(jnp.bfloat16), pair_ref[1], preferred_element_type=jnp.float32)
        mixed = mixed + jnp.dot(
            own_weights.astype(jnp.bfloat16), own_values, preferred_element_type=jnp.float32
        )
        mixed = (mixed / total).astype(jnp.bfloat16)
        mixed = jnp.concatenate([mixed[i * rows : (i + 1) * rows] for i in range(per_dot)], axis=1)
        att_ref[:, part] = mixed
        if last:
            outs[0][mine, part] = mixed


def attend(r, suffix_len, model_width, lengths, offsets, sums, tables, pair, earlier, last):
    width = sums[0].shape[1]
    _, prefix_len, head_size = pair.shape
    vmem = pl.BlockSpec(memory_space=pltpu.VMEM)
    smem = pl.BlockSpec(memory_space=pltpu.SMEM)
    widths = (width, 2 * head_size)
    all_rows = (r + 1) * suffix_len
    shapes = [(suffix_len, width)]
    shapes += [(all_rows, w) for w in widths] if last else [(suffix_len, widths[1])]
    earlier = earlier if last else []
    return pl.pallas_call(
        functools.partial(attend_kernel, r, last, model_width),
        in_specs=[smem] * 2 + [vmem] * (6 + len(earlier)),
        out_specs=[vmem] * len(shapes),
        out_shape=[jax.ShapeDtypeStruct(shape, jnp.bfloat16) for shape in shapes],
        compiler_params=pltpu.CompilerParams(vmem_limit_bytes=VMEM_BYTES),
        cost_estimate=pl.CostEstimate(
            flops=4 * suffix_len * width * (prefix_len + suffix_len),
            bytes_accessed=4 * prefix_len * head_size + 4 * suffix_len * (width + 2 * head_size),
            transcendentals=suffix_len * width // head_size * prefix_len,
        ),
    )(lengths, offsets, *sums, *tables, pair, *earlier)


def copies_kernel(plan, *refs):
    arrived = refs[-1]
    copies = [
        pltpu.make_async_copy(source, target, arrived.at[i])
        for i, (source, target) in enumerate(plan(refs[:-1]))
    ]
    for copy in copies:
        copy.start()
    for copy in copies:
        copy.wait()


def copied(plan, n_copies, scalars, arrays, outs, out_space=pltpu.HBM, vmem_bytes=VMEM_BYTES):
    size = sum(out.size for out in outs)
    return pl.pallas_call(
        functools.partial(copies_kernel, plan),
        in_specs=[pl.BlockSpec(memory_space=pltpu.SMEM)] * len(scalars)
        + [pl.BlockSpec(memory_space=pltpu.HBM)] * len(arrays),
        out_specs=[pl.BlockSpec(memory_space=out_space)] * len(outs),
        out_shape=outs,
        scratch_shapes=[pltpu.SemaphoreType.DMA((n_copies,))],
        compiler_params=pltpu.CompilerParams(vmem_limit_bytes=vmem_bytes),
        cost_estimate=pl.CostEstimate(flops=0, bytes_accessed=4 * size, transcendentals=0),
    )(*scalars, *arrays)


def stage_in(array):
    out = jax.ShapeDtypeStruct(array.shape, array.dtype)
    return copied(lambda refs: [(refs[0], refs[1])], 1, [], [array], [out], pltpu.VMEM)[0]


def first_rows(array, count):
    out = jax.ShapeDtypeStruct((count, array.shape[1]), array.dtype)
    return copied(
        lambda refs: [(refs[0].at[pl.ds(0, count)], refs[1])], 1, [], [array], [out], pltpu.VMEM
    )[0]


def stacked(arrays):
    n = len(arrays)
    out = jax.ShapeDtypeStruct((n,) + arrays[0].shape, arrays[0].dtype)
    return copied(lambda refs: [(refs[i], refs[n].at[i]) for i in range(n)], n, [], arrays, [out])[0]


def cut(array, row, columns, shape):
    n = len(columns)

    def plan(refs):
        begins, whole, outs = refs[0], refs[1], refs[2:]
        rows = pl.ds(pl.multiple_of(begins[0], ROW_TILE), shape[0])
        return [
            (whole.at[rows, pl.ds(pl.multiple_of(begins[i + 1], LANES), shape[1])], outs[i])
            for i in range(n)
        ]

    outs = [jax.ShapeDtypeStruct(shape, array.dtype)] * n
    begins = jnp.stack([row] + columns).astype(jnp.int32)
    return copied(plan, n, [begins], [array], outs, pltpu.VMEM, 58 * 1024 * 1024)


def most_kernel(n_slots, *refs):
    own_ref, others_ref, hidden_ref, most_ref = refs[-4:]
    req_count, suffix_len, features = hidden_ref.shape
    chunk = chunk_of(features)
    attention = [
        jnp.concatenate([refs[r * n_slots + j][...] for r in range(req_count)]) for j in range(n_slots)
    ]
    for begin in range(0, features, chunk):
        columns = slice(begin, begin + chunk)
        mixed = jnp.dot(attention[0], own_ref[:, columns], preferred_element_type=jnp.float32)
        for j in range(1, n_slots):
            weights = others_ref[:, j - 1, :, columns].reshape(own_ref.shape[0], chunk)
            mixed = mixed + jnp.dot(attention[j], weights, preferred_element_type=jnp.float32)
        for r in range(req_count):
            rows = slice(r * suffix_len, (r + 1) * suffix_len)
            most_ref[rows, columns] = mixed[rows] + hidden_ref[r, :, columns].astype(jnp.float32)


def last_kernel(length_ref, attention_ref, others_ref, most_ref, out_ref):
    req_count, suffix_len, features = out_ref.shape
    chunk = chunk_of(features)
    position = lax.broadcasted_iota(jnp.int32, (suffix_len, chunk), 0)
    for begin in range(0, features, chunk):
        columns = slice(begin, begin + chunk)
        weights = others_ref[:, others_ref.shape[1] - 1, :, columns]
        weights = weights.reshape(attention_ref.shape[1], chunk)
        mixed = jnp.dot(attention_ref[...], weights, preferred_element_type=jnp.float32)
        mixed = mixed + most_ref[:, columns]
        for r in range(req_count):
            part = mixed[r * suffix_len : (r + 1) * suffix_len]
            part = jnp.where(position < length_ref[r], part, 0.0)
            out_ref[r, :, columns] = part.astype(jnp.bfloat16)


def project_out(lengths, attention, last_slot, w_own, w_others, hidden):
    req_count, suffix_len, features = hidden.shape
    n_slots = len(attention[0])
    rows = req_count * suffix_len
    vmem = pl.BlockSpec(memory_space=pltpu.VMEM)
    params = pltpu.CompilerParams(vmem_limit_bytes=VMEM_BYTES)
    flops = 2 * rows * features * w_own.shape[0]
    most = pl.pallas_call(
        functools.partial(most_kernel, n_slots),
        in_specs=[vmem] * (req_count * n_slots + 3),
        out_specs=vmem,
        out_shape=jax.ShapeDtypeStruct((rows, features), jnp.float32),
        compiler_params=params,
        cost_estimate=pl.CostEstimate(
            flops=flops * n_slots,
            bytes_accessed=2 * features * (w_own.shape[0] * n_slots + 3 * rows),
            transcendentals=0,
        ),
    )(*[block for slots in attention for block in slots], w_own, w_others, hidden)
    return pl.pallas_call(
        last_kernel,
        in_specs=[pl.BlockSpec(memory_space=pltpu.SMEM)] + [vmem] * 3,
        out_specs=vmem,
        out_shape=jax.ShapeDtypeStruct(hidden.shape, jnp.bfloat16),
        compiler_params=params,
        cost_estimate=pl.CostEstimate(
            flops=flops,
            bytes_accessed=2 * features * (w_own.shape[0] + 3 * rows),
            transcendentals=0,
        ),
    )(lengths, last_slot, w_others, most)


def shards(hidden, norm_gain, w_query, w_kv, w_out, prefix_cache, lengths, groups, owners):
    n_tp = lax.axis_size("tp")
    n_owners = lax.axis_size("req")
    my_index = lax.axis_index("req")
    place = lax.axis_index("tp")
    req_count, suffix_len, features = hidden.shape
    head_size = w_kv.shape[2]
    model_width = w_query.shape[0]

    flat_kv = w_kv.reshape(model_width, 2 * head_size)
    tables = rope_tables(suffix_len, head_size)

    share = w_out.shape[0] // n_owners
    columns = [ring_place(place, j) * features for j in range(1, n_tp)]
    pieces = cut(w_out, my_index * share, columns, (share, features))
    moved = [shift(piece, j) for j, piece in enumerate(pieces, 1)]

    _, prefix_len, _, head_size = prefix_cache.shape
    prefixes = lax.all_gather(prefix_cache.reshape(prefix_len * 2, head_size), "req", axis=0)
    local_groups = lax.dynamic_slice_in_dim(groups, my_index * req_count, req_count)
    owner_of = jnp.sum(
        jnp.where(local_groups[:, None] == jnp.arange(n_owners)[None, :], owners[None, :], 0), axis=-1
    ).astype(jnp.int32)

    def weights_of(begin):
        return (
            lax.dynamic_slice_in_dim(norm_gain, begin, features).reshape(1, features),
            lax.dynamic_slice_in_dim(w_query, begin, features, axis=0),
            lax.dynamic_slice_in_dim(flat_kv, begin, features, axis=0),
        )

    total_rows = req_count * suffix_len
    packed = hidden.reshape(total_rows, features)
    offsets = [jnp.int32(0)]
    for r in range(1, req_count):
        offsets.append(offsets[-1] + (lengths[r - 1] + ROW_TILE - 1) // ROW_TILE * ROW_TILE)
        packed = lax.dynamic_update_slice(packed, hidden[r], (offsets[r], 0))
    live_rows = offsets[-1] + lengths[-1]
    offsets = jnp.stack(offsets)
    capacities = [total_rows * k // 8 for k in range(4, 9)]
    branch = sum((live_rows > capacity).astype(jnp.int32) for capacity in capacities[:-1])

    begins = [ring_place(place, -step) * features for step in range(n_tp)]
    own_sums = project(packed, weights_of(begins[0]), [], total_rows, in_loop=False)
    state = (packed, own_sums, moved, tables, begins, owner_of, offsets, branch)
    state = lax.optimization_barrier(state)
    packed, own_sums, moved, tables, begins, owner_of, offsets, branch = state
    w_others = lax.all_gather(stacked(moved), "req", axis=0)

    def ring_of(capacity):
        def run(packed, sums):
            block = first_rows(packed, capacity) if capacity < total_rows else packed
            for step in range(n_tp - 1):
                coming = shift(block, 1)
                if step > 0:
                    sums = project(block, weights, sums, total_rows)
                state = (coming, sums, weights_of(begins[step + 1]))
                block, sums, weights = lax.optimization_barrier(state)
            return project(block, weights, sums, total_rows, in_loop=False)

        return run

    sums = lax.switch(branch, [ring_of(c) for c in capacities], packed, own_sums)

    earlier, gathered = [], []
    for r in range(req_count):
        pair = lax.dynamic_index_in_dim(prefixes, owner_of[r], 0, keepdims=False)
        pair = pair.reshape(prefix_len, 2, head_size).transpose(1, 0, 2)
        results = attend(
            r, suffix_len, model_width, lengths, offsets, sums, tables, pair, earlier, r == req_count - 1
        )
        earlier = earlier + list(results[:2])
        gathered.append([results[0]] + [shift(results[0], j) for j in range(1, n_tp - 1)])
        prefixes = lax.optimization_barrier(prefixes)
    _, all_attention, all_caches = results
    last_slot = shift(all_attention, n_tp - 1)
    place, _ = lax.optimization_barrier((place, all_caches))
    w_own = lax.dynamic_slice_in_dim(w_out, place * features, features, axis=1)
    suffix_cache = all_caches.reshape(req_count, suffix_len, 2, head_size)
    w_others, suffix_cache = lax.optimization_barrier((w_others, suffix_cache))
    out_hidden = project_out(lengths, gathered, last_slot, w_own, stage_in(w_others), hidden)
    return (out_hidden, suffix_cache)


def solution(mesh):
    return jax.shard_map(
        shards,
        mesh=mesh,
        in_specs=(
            P("req", None, "tp"),
            P(),
            P(None, "tp"),
            P(None, None, "tp"),
            P("tp", None),
            P("req", None, None, "tp"),
            P("req"),
            P(),
            P(),
        ),
        out_specs=(P("req", None, "tp"), P("req", None, None, "tp")),
        check_vma=False,
    )
```

```python
import functools

import jax
import jax.numpy as jnp
from jax import lax
from jax.experimental import pallas as pl
from jax.experimental.pallas import tpu as pltpu
from jax.sharding import PartitionSpec as P

PREFIX = 2048


EPSILON = 1e-05
ROPE_BASE = 5000000.0
VMEM_BYTES = 12 * 1024 * 1024
LANES = 128
ROW_TILE = 16


def rope_tables(suffix_len, head_size):
    positions = (PREFIX + jnp.arange(suffix_len)).astype(jnp.float32)
    inverse = ROPE_BASE ** (-(2.0 * jnp.arange(head_size // 2).astype(jnp.float32)) / head_size)
    angles = positions[:, None] * inverse[None, :]
    cosine_table = jnp.concatenate([jnp.cos(angles), jnp.cos(angles)], axis=-1)
    sine_table = jnp.concatenate([-jnp.sin(angles), jnp.sin(angles)], axis=-1)
    return (cosine_table, sine_table)


def ring_order(n):
    return [0] + list(range(1, n, 2)) + list(range(n - 2 if n % 2 == 0 else n - 1, 0, -2))


def ring_place(place, distance):
    n = lax.axis_size("tp")
    ring = ring_order(n)
    return sum(jnp.where(place == ring[p], ring[(p + distance) % n], 0) for p in range(n))


def shift(block, distance):
    n = lax.axis_size("tp")
    ring = ring_order(n)
    return lax.ppermute(block, "tp", [(ring[p], ring[(p + distance) % n]) for p in range(n)])


def chunk_of(size):
    return 2 * LANES if size % (2 * LANES) == 0 else LANES


def project_kernel(chunk, block_ref, gain_ref, wq_ref, wkv_ref, *refs):
    sums_in, (q_ref, kv_ref, square_ref) = refs[:-3], refs[-3:]
    rows, features = block_ref.shape

    def parts_of(part):
        block_f = block_ref[:, part].astype(jnp.float32)
        scaled = (block_f * gain_ref[:, part]).astype(jnp.bfloat16)
        squares = block_f * block_f
        square = squares[:, :LANES]
        for i in range(1, chunk // LANES):
            square = square + squares[:, i * LANES : (i + 1) * LANES]
        return (
            jnp.dot(scaled, wq_ref[part, :], preferred_element_type=jnp.float32),
            jnp.dot(scaled, wkv_ref[part, :], preferred_element_type=jnp.float32),
            square,
        )

    parts = parts_of(pl.ds(0, chunk))
    for i, ref in enumerate(refs[-3:]):
        ref[:rows] = sums_in[i][:rows] + parts[i] if sums_in else parts[i]

    def step(k, _):
        parts = parts_of(pl.ds(pl.multiple_of(k * chunk, chunk), chunk))
        for i, ref in enumerate(refs[-3:]):
            ref[:rows] += parts[i]
        return 0

    if chunk < features:
        lax.fori_loop(1, features // chunk, step, 0)


def project(block, weights, sums, total_rows, in_loop=True):
    rows, features = block.shape
    gain, w_query, flat_kv = weights
    widths = (w_query.shape[1], flat_kv.shape[1], LANES)
    vmem = pl.BlockSpec(memory_space=pltpu.VMEM)
    return pl.pallas_call(
        functools.partial(project_kernel, chunk_of(features) if in_loop else features),
        in_specs=[vmem] * (4 + len(sums)),
        out_specs=[vmem] * 3,
        out_shape=[jax.ShapeDtypeStruct((total_rows, width), jnp.float32) for width in widths],
        compiler_params=pltpu.CompilerParams(vmem_limit_bytes=VMEM_BYTES),
        cost_estimate=pl.CostEstimate(
            flops=2 * rows * features * (widths[0] + widths[1]),
            bytes_accessed=2 * features * (widths[0] + widths[1] + rows),
            transcendentals=0,
        ),
    )(block, gain, w_query, flat_kv, *sums)


def attend_kernel(
    r, last, model_width, length_ref, offset_ref, q_ref, kv_ref, square_ref, cos_ref, sin_ref, pair_ref, *refs
):
    rows = cos_ref.shape[0]
    n_earlier = 2 * r if last else 0
    earlier, att_ref, outs = refs[:n_earlier], refs[n_earlier], refs[n_earlier + 1 :]
    for i in range(n_earlier):
        outs[i % 2][i // 2 * rows : (i // 2 + 1) * rows] = earlier[i][...]
    mine = slice(r * rows, (r + 1) * rows) if last else slice(0, rows)
    cache_ref = outs[1] if last else outs[0]
    packed = pl.ds(pl.multiple_of(offset_ref[r], ROW_TILE), rows)
    head_size = pair_ref.shape[-1]
    heads = q_ref.shape[1] // head_size
    per_dot = 2 if heads % 2 == 0 else 1
    scale = head_size ** (-0.5)
    length = length_ref[r]
    cosine, sine = cos_ref[...], sin_ref[...]
    mean = jnp.sum(square_ref[packed, :], axis=-1, keepdims=True) / model_width
    row_scale = lax.rsqrt(mean + EPSILON)

    def turn(vector):
        vector = vector * row_scale
        return vector * cosine + pltpu.roll(vector, head_size // 2, 1) * sine

    keys_f = turn(kv_ref[packed, :head_size])
    values_f = kv_ref[packed, head_size:] * row_scale
    live = lax.broadcasted_iota(jnp.int32, (rows, head_size), 0) < length
    own_keys = jnp.where(live, keys_f, 0.0).astype(jnp.bfloat16)
    own_values = jnp.where(live, values_f, 0.0).astype(jnp.bfloat16)
    cache_ref[mine, :head_size] = own_keys
    cache_ref[mine, head_size:] = own_values

    position = lax.broadcasted_iota(jnp.int32, (per_dot * rows, rows), 0) % rows
    other = lax.broadcasted_iota(jnp.int32, (per_dot * rows, rows), 1)
    causal = (other <= position) & (other < length)
    against = (((1,), (1,)), ((), ()))
    for g in range(heads // per_dot):
        part = slice(g * per_dot * head_size, (g + 1) * per_dot * head_size)
        vectors = q_ref[packed, part]
        query = jnp.concatenate(
            [turn(vectors[:, i * head_size : (i + 1) * head_size]) for i in range(per_dot)]
        ).astype(jnp.bfloat16)
        scores = lax.dot_general(query, pair_ref[0], against, preferred_element_type=jnp.float32)
        own_scores = lax.dot_general(query, own_keys, against, preferred_element_type=jnp.float32)
        own_scores = jnp.where(causal, own_scores, -jnp.inf)
        highest = jnp.maximum(
            jnp.max(scores, axis=-1, keepdims=True), jnp.max(own_scores, axis=-1, keepdims=True)
        )
        weights = jnp.exp((scores - highest) * scale)
        own_weights = jnp.exp((own_scores - highest) * scale)
        total = jnp.sum(weights, axis=-1, keepdims=True) + jnp.sum(own_weights, axis=-1, keepdims=True)
        mixed = jnp.dot(weights.astype(jnp.bfloat16), pair_ref[1], preferred_element_type=jnp.float32)
        mixed = mixed + jnp.dot(
            own_weights.astype(jnp.bfloat16), own_values, preferred_element_type=jnp.float32
        )
        mixed = (mixed / total).astype(jnp.bfloat16)
        mixed = jnp.concatenate([mixed[i * rows : (i + 1) * rows] for i in range(per_dot)], axis=1)
        att_ref[:, part] = mixed
        if last:
            outs[0][mine, part] = mixed


def attend(r, suffix_len, model_width, lengths, offsets, sums, tables, pair, earlier, last):
    width = sums[0].shape[1]
    _, prefix_len, head_size = pair.shape
    vmem = pl.BlockSpec(memory_space=pltpu.VMEM)
    smem = pl.BlockSpec(memory_space=pltpu.SMEM)
    widths = (width, 2 * head_size)
    all_rows = (r + 1) * suffix_len
    shapes = [(suffix_len, width)]
    shapes += [(all_rows, w) for w in widths] if last else [(suffix_len, widths[1])]
    earlier = earlier if last else []
    return pl.pallas_call(
        functools.partial(attend_kernel, r, last, model_width),
        in_specs=[smem] * 2 + [vmem] * (6 + len(earlier)),
        out_specs=[vmem] * len(shapes),
        out_shape=[jax.ShapeDtypeStruct(shape, jnp.bfloat16) for shape in shapes],
        compiler_params=pltpu.CompilerParams(vmem_limit_bytes=VMEM_BYTES),
        cost_estimate=pl.CostEstimate(
            flops=4 * suffix_len * width * (prefix_len + suffix_len),
            bytes_accessed=4 * prefix_len * head_size + 4 * suffix_len * (width + 2 * head_size),
            transcendentals=suffix_len * width // head_size * prefix_len,
        ),
    )(lengths, offsets, *sums, *tables, pair, *earlier)


def copies_kernel(plan, *refs):
    arrived = refs[-1]
    copies = [
        pltpu.make_async_copy(source, target, arrived.at[i])
        for i, (source, target) in enumerate(plan(refs[:-1]))
    ]
    for copy in copies:
        copy.start()
    for copy in copies:
        copy.wait()


def copied(plan, n_copies, arrays, outs, out_space=pltpu.HBM):
    size = sum(out.size for out in outs)
    return pl.pallas_call(
        functools.partial(copies_kernel, plan),
        in_specs=[pl.BlockSpec(memory_space=pltpu.HBM)] * len(arrays),
        out_specs=[pl.BlockSpec(memory_space=out_space)] * len(outs),
        out_shape=outs,
        scratch_shapes=[pltpu.SemaphoreType.DMA((n_copies,))],
        compiler_params=pltpu.CompilerParams(vmem_limit_bytes=VMEM_BYTES),
        cost_estimate=pl.CostEstimate(flops=0, bytes_accessed=4 * size, transcendentals=0),
    )(*arrays)


def stage_in(array):
    out = jax.ShapeDtypeStruct(array.shape, array.dtype)
    return copied(lambda refs: [(refs[0], refs[1])], 1, [array], [out], pltpu.VMEM)[0]


def first_rows(array, count):
    out = jax.ShapeDtypeStruct((count, array.shape[1]), array.dtype)
    return copied(
        lambda refs: [(refs[0].at[pl.ds(0, count)], refs[1])], 1, [array], [out], pltpu.VMEM
    )[0]


def stacked(arrays):
    n = len(arrays)
    out = jax.ShapeDtypeStruct((n,) + arrays[0].shape, arrays[0].dtype)
    return copied(lambda refs: [(refs[i], refs[n].at[i]) for i in range(n)], n, arrays, [out])[0]


def most_kernel(n_slots, *refs):
    own_ref, others_ref, hidden_ref, most_ref = refs[-4:]
    req_count, suffix_len, features = hidden_ref.shape
    chunk = chunk_of(features)
    attention = [
        jnp.concatenate([refs[r * n_slots + j][...] for r in range(req_count)]) for j in range(n_slots)
    ]
    for begin in range(0, features, chunk):
        columns = slice(begin, begin + chunk)
        mixed = jnp.dot(attention[0], own_ref[:, columns], preferred_element_type=jnp.float32)
        for j in range(1, n_slots):
            weights = others_ref[:, j - 1, :, columns].reshape(own_ref.shape[0], chunk)
            mixed = mixed + jnp.dot(attention[j], weights, preferred_element_type=jnp.float32)
        for r in range(req_count):
            rows = slice(r * suffix_len, (r + 1) * suffix_len)
            most_ref[rows, columns] = mixed[rows] + hidden_ref[r, :, columns].astype(jnp.float32)


def last_kernel(length_ref, attention_ref, others_ref, most_ref, out_ref):
    req_count, suffix_len, features = out_ref.shape
    chunk = chunk_of(features)
    position = lax.broadcasted_iota(jnp.int32, (suffix_len, chunk), 0)
    for begin in range(0, features, chunk):
        columns = slice(begin, begin + chunk)
        weights = others_ref[:, others_ref.shape[1] - 1, :, columns]
        weights = weights.reshape(attention_ref.shape[1], chunk)
        mixed = jnp.dot(attention_ref[...], weights, preferred_element_type=jnp.float32)
        mixed = mixed + most_ref[:, columns]
        for r in range(req_count):
            part = mixed[r * suffix_len : (r + 1) * suffix_len]
            part = jnp.where(position < length_ref[r], part, 0.0)
            out_ref[r, :, columns] = part.astype(jnp.bfloat16)


def project_out(lengths, attention, last_slot, w_own, w_others, hidden):
    req_count, suffix_len, features = hidden.shape
    n_slots = len(attention[0])
    rows = req_count * suffix_len
    vmem = pl.BlockSpec(memory_space=pltpu.VMEM)
    params = pltpu.CompilerParams(vmem_limit_bytes=VMEM_BYTES)
    flops = 2 * rows * features * w_own.shape[0]
    most = pl.pallas_call(
        functools.partial(most_kernel, n_slots),
        in_specs=[vmem] * (req_count * n_slots + 3),
        out_specs=vmem,
        out_shape=jax.ShapeDtypeStruct((rows, features), jnp.float32),
        compiler_params=params,
        cost_estimate=pl.CostEstimate(
            flops=flops * n_slots,
            bytes_accessed=2 * features * (w_own.shape[0] * n_slots + 3 * rows),
            transcendentals=0,
        ),
    )(*[block for slots in attention for block in slots], w_own, w_others, hidden)
    return pl.pallas_call(
        last_kernel,
        in_specs=[pl.BlockSpec(memory_space=pltpu.SMEM)] + [vmem] * 3,
        out_specs=vmem,
        out_shape=jax.ShapeDtypeStruct(hidden.shape, jnp.bfloat16),
        compiler_params=params,
        cost_estimate=pl.CostEstimate(
            flops=flops,
            bytes_accessed=2 * features * (w_own.shape[0] + 3 * rows),
            transcendentals=0,
        ),
    )(lengths, last_slot, w_others, most)


def shards(hidden, norm_gain, w_query, w_kv, w_out, prefix_cache, lengths, groups, owners):
    n_tp = lax.axis_size("tp")
    n_owners = lax.axis_size("req")
    my_index = lax.axis_index("req")
    place = lax.axis_index("tp")
    req_count, suffix_len, features = hidden.shape
    head_size = w_kv.shape[2]
    model_width = w_query.shape[0]

    flat_kv = w_kv.reshape(model_width, 2 * head_size)
    tables = rope_tables(suffix_len, head_size)

    share = w_out.shape[0] // n_owners
    my_rows = lax.dynamic_slice_in_dim(w_out, my_index * share, share, axis=0)
    moved = []
    for j in range(1, n_tp):
        begin = ring_place(place, j) * features
        moved.append(shift(lax.dynamic_slice_in_dim(my_rows, begin, features, axis=1), j))

    _, prefix_len, _, head_size = prefix_cache.shape
    prefixes = lax.all_gather(prefix_cache.reshape(prefix_len * 2, head_size), "req", axis=0)
    local_groups = lax.dynamic_slice_in_dim(groups, my_index * req_count, req_count)
    owner_of = jnp.sum(
        jnp.where(local_groups[:, None] == jnp.arange(n_owners)[None, :], owners[None, :], 0), axis=-1
    ).astype(jnp.int32)

    def weights_of(begin):
        return (
            lax.dynamic_slice_in_dim(norm_gain, begin, features).reshape(1, features),
            lax.dynamic_slice_in_dim(w_query, begin, features, axis=0),
            lax.dynamic_slice_in_dim(flat_kv, begin, features, axis=0),
        )

    total_rows = req_count * suffix_len
    packed = hidden.reshape(total_rows, features)
    offsets = [jnp.int32(0)]
    for r in range(1, req_count):
        offsets.append(offsets[-1] + (lengths[r - 1] + ROW_TILE - 1) // ROW_TILE * ROW_TILE)
        packed = lax.dynamic_update_slice(packed, hidden[r], (offsets[r], 0))
    live_rows = offsets[-1] + lengths[-1]
    offsets = jnp.stack(offsets)
    capacities = [total_rows * k // 16 for k in range(12, 17)]
    branch = sum((live_rows > capacity).astype(jnp.int32) for capacity in capacities[:-1])

    begins = [ring_place(place, -step) * features for step in range(n_tp)]
    own_sums = project(packed, weights_of(begins[0]), [], total_rows, in_loop=False)
    state = (packed, own_sums, moved, tables, begins, owner_of, offsets, branch)
    state = lax.optimization_barrier(state)
    packed, own_sums, moved, tables, begins, owner_of, offsets, branch = state
    w_others = lax.all_gather(stacked(moved), "req", axis=0)

    def ring_of(capacity):
        def run(packed, sums):
            block = first_rows(packed, capacity) if capacity < total_rows else packed
            for step in range(n_tp - 1):
                coming = shift(block, 1)
                if step > 0:
                    sums = project(block, weights, sums, total_rows)
                state = (coming, sums, weights_of(begins[step + 1]))
                block, sums, weights = lax.optimization_barrier(state)
            return project(block, weights, sums, total_rows, in_loop=False)

        return run

    sums = lax.switch(branch, [ring_of(c) for c in capacities], packed, own_sums)

    earlier, gathered = [], []
    for r in range(req_count):
        pair = lax.dynamic_index_in_dim(prefixes, owner_of[r], 0, keepdims=False)
        pair = pair.reshape(prefix_len, 2, head_size).transpose(1, 0, 2)
        results = attend(
            r, suffix_len, model_width, lengths, offsets, sums, tables, pair, earlier, r == req_count - 1
        )
        earlier = earlier + list(results[:2])
        gathered.append([results[0]] + [shift(results[0], j) for j in range(1, n_tp - 1)])
        prefixes = lax.optimization_barrier(prefixes)
    _, all_attention, all_caches = results
    last_slot = shift(all_attention, n_tp - 1)
    place, _ = lax.optimization_barrier((place, all_caches))
    w_own = lax.dynamic_slice_in_dim(w_out, place * features, features, axis=1)
    suffix_cache = all_caches.reshape(req_count, suffix_len, 2, head_size)
    w_others, suffix_cache = lax.optimization_barrier((w_others, suffix_cache))
    out_hidden = project_out(lengths, gathered, last_slot, w_own, stage_in(w_others), hidden)
    return (out_hidden, suffix_cache)


def solution(mesh):
    return jax.shard_map(
        shards,
        mesh=mesh,
        in_specs=(
            P("req", None, "tp"),
            P(),
            P(None, "tp"),
            P(None, None, "tp"),
            P("tp", None),
            P("req", None, None, "tp"),
            P("req"),
            P(),
            P(),
        ),
        out_specs=(P("req", None, "tp"), P("req", None, None, "tp")),
        check_vma=False,
    )
```

```python
import functools

import jax
import jax.numpy as jnp
from jax import lax
from jax.experimental import pallas as pl
from jax.experimental.pallas import tpu as pltpu
from jax.sharding import PartitionSpec as P

PREFIX = 2048


EPSILON = 1e-05
ROPE_BASE = 5000000.0
VMEM_BYTES = 12 * 1024 * 1024
LANES = 128
ROW_TILE = 16


def rope_tables(suffix_len, head_size):
    positions = (PREFIX + jnp.arange(suffix_len)).astype(jnp.float32)
    inverse = ROPE_BASE ** (-(2.0 * jnp.arange(head_size // 2).astype(jnp.float32)) / head_size)
    angles = positions[:, None] * inverse[None, :]
    cosine_table = jnp.concatenate([jnp.cos(angles), jnp.cos(angles)], axis=-1)
    sine_table = jnp.concatenate([-jnp.sin(angles), jnp.sin(angles)], axis=-1)
    return (cosine_table, sine_table)


def ring_order(n):
    return [0] + list(range(1, n, 2)) + list(range(n - 2 if n % 2 == 0 else n - 1, 0, -2))


def ring_place(place, distance):
    n = lax.axis_size("tp")
    ring = ring_order(n)
    return sum(jnp.where(place == ring[p], ring[(p + distance) % n], 0) for p in range(n))


def shift(block, distance):
    n = lax.axis_size("tp")
    ring = ring_order(n)
    return lax.ppermute(block, "tp", [(ring[p], ring[(p + distance) % n]) for p in range(n)])


def chunk_of(size):
    return 2 * LANES if size % (2 * LANES) == 0 else LANES


def project_kernel(chunk, block_ref, gain_ref, wq_ref, wkv_ref, *refs):
    sums_in, (q_ref, kv_ref, square_ref) = refs[:-3], refs[-3:]
    rows, features = block_ref.shape

    def parts_of(part):
        block_f = block_ref[:, part].astype(jnp.float32)
        scaled = (block_f * gain_ref[:, part]).astype(jnp.bfloat16)
        squares = block_f * block_f
        square = squares[:, :LANES]
        for i in range(1, chunk // LANES):
            square = square + squares[:, i * LANES : (i + 1) * LANES]
        return (
            jnp.dot(scaled, wq_ref[part, :], preferred_element_type=jnp.float32),
            jnp.dot(scaled, wkv_ref[part, :], preferred_element_type=jnp.float32),
            square,
        )

    parts = parts_of(pl.ds(0, chunk))
    for i, ref in enumerate(refs[-3:]):
        ref[:rows] = sums_in[i][:rows] + parts[i] if sums_in else parts[i]

    def step(k, _):
        parts = parts_of(pl.ds(pl.multiple_of(k * chunk, chunk), chunk))
        for i, ref in enumerate(refs[-3:]):
            ref[:rows] += parts[i]
        return 0

    if chunk < features:
        lax.fori_loop(1, features // chunk, step, 0)


def project(block, weights, sums, total_rows, in_loop=True):
    rows, features = block.shape
    gain, w_query, flat_kv = weights
    widths = (w_query.shape[1], flat_kv.shape[1], LANES)
    vmem = pl.BlockSpec(memory_space=pltpu.VMEM)
    return pl.pallas_call(
        functools.partial(project_kernel, chunk_of(features) if in_loop else features),
        in_specs=[vmem] * (4 + len(sums)),
        out_specs=[vmem] * 3,
        out_shape=[jax.ShapeDtypeStruct((total_rows, width), jnp.float32) for width in widths],
        compiler_params=pltpu.CompilerParams(vmem_limit_bytes=VMEM_BYTES),
        cost_estimate=pl.CostEstimate(
            flops=2 * rows * features * (widths[0] + widths[1]),
            bytes_accessed=2 * features * (widths[0] + widths[1] + rows),
            transcendentals=0,
        ),
    )(block, gain, w_query, flat_kv, *sums)


def attend_kernel(
    r, last, model_width, length_ref, offset_ref, q_ref, kv_ref, square_ref, cos_ref, sin_ref, pair_ref, *refs
):
    rows = cos_ref.shape[0]
    n_earlier = 2 * r if last else 0
    earlier, att_ref, outs = refs[:n_earlier], refs[n_earlier], refs[n_earlier + 1 :]
    for i in range(n_earlier):
        outs[i % 2][i // 2 * rows : (i // 2 + 1) * rows] = earlier[i][...]
    mine = slice(r * rows, (r + 1) * rows) if last else slice(0, rows)
    cache_ref = outs[1] if last else outs[0]
    packed = pl.ds(pl.multiple_of(offset_ref[r], ROW_TILE), rows)
    head_size = pair_ref.shape[-1]
    heads = q_ref.shape[1] // head_size
    per_dot = 2 if heads % 2 == 0 else 1
    scale = head_size ** (-0.5)
    length = length_ref[r]
    cosine, sine = cos_ref[...], sin_ref[...]
    mean = jnp.sum(square_ref[packed, :], axis=-1, keepdims=True) / model_width
    row_scale = lax.rsqrt(mean + EPSILON)

    def turn(vector):
        vector = vector * row_scale
        return vector * cosine + pltpu.roll(vector, head_size // 2, 1) * sine

    keys_f = turn(kv_ref[packed, :head_size])
    values_f = kv_ref[packed, head_size:] * row_scale
    live = lax.broadcasted_iota(jnp.int32, (rows, head_size), 0) < length
    own_keys = jnp.where(live, keys_f, 0.0).astype(jnp.bfloat16)
    own_values = jnp.where(live, values_f, 0.0).astype(jnp.bfloat16)
    cache_ref[mine, :head_size] = own_keys
    cache_ref[mine, head_size:] = own_values

    position = lax.broadcasted_iota(jnp.int32, (per_dot * rows, rows), 0) % rows
    other = lax.broadcasted_iota(jnp.int32, (per_dot * rows, rows), 1)
    causal = (other <= position) & (other < length)
    against = (((1,), (1,)), ((), ()))
    for g in range(heads // per_dot):
        part = slice(g * per_dot * head_size, (g + 1) * per_dot * head_size)
        vectors = q_ref[packed, part]
        query = jnp.concatenate(
            [turn(vectors[:, i * head_size : (i + 1) * head_size]) for i in range(per_dot)]
        ).astype(jnp.bfloat16)
        scores = lax.dot_general(query, pair_ref[0], against, preferred_element_type=jnp.float32)
        own_scores = lax.dot_general(query, own_keys, against, preferred_element_type=jnp.float32)
        own_scores = jnp.where(causal, own_scores, -jnp.inf)
        highest = jnp.maximum(
            jnp.max(scores, axis=-1, keepdims=True), jnp.max(own_scores, axis=-1, keepdims=True)
        )
        weights = jnp.exp((scores - highest) * scale)
        own_weights = jnp.exp((own_scores - highest) * scale)
        total = jnp.sum(weights, axis=-1, keepdims=True) + jnp.sum(own_weights, axis=-1, keepdims=True)
        mixed = jnp.dot(weights.astype(jnp.bfloat16), pair_ref[1], preferred_element_type=jnp.float32)
        mixed = mixed + jnp.dot(
            own_weights.astype(jnp.bfloat16), own_values, preferred_element_type=jnp.float32
        )
        mixed = (mixed / total).astype(jnp.bfloat16)
        mixed = jnp.concatenate([mixed[i * rows : (i + 1) * rows] for i in range(per_dot)], axis=1)
        att_ref[:, part] = mixed
        if last:
            outs[0][mine, part] = mixed


def attend(r, suffix_len, model_width, lengths, offsets, sums, tables, pair, earlier, last):
    width = sums[0].shape[1]
    _, prefix_len, head_size = pair.shape
    vmem = pl.BlockSpec(memory_space=pltpu.VMEM)
    smem = pl.BlockSpec(memory_space=pltpu.SMEM)
    widths = (width, 2 * head_size)
    all_rows = (r + 1) * suffix_len
    shapes = [(suffix_len, width)]
    shapes += [(all_rows, w) for w in widths] if last else [(suffix_len, widths[1])]
    earlier = earlier if last else []
    return pl.pallas_call(
        functools.partial(attend_kernel, r, last, model_width),
        in_specs=[smem] * 2 + [vmem] * (6 + len(earlier)),
        out_specs=[vmem] * len(shapes),
        out_shape=[jax.ShapeDtypeStruct(shape, jnp.bfloat16) for shape in shapes],
        compiler_params=pltpu.CompilerParams(vmem_limit_bytes=VMEM_BYTES),
        cost_estimate=pl.CostEstimate(
            flops=4 * suffix_len * width * (prefix_len + suffix_len),
            bytes_accessed=4 * prefix_len * head_size + 4 * suffix_len * (width + 2 * head_size),
            transcendentals=suffix_len * width // head_size * prefix_len,
        ),
    )(lengths, offsets, *sums, *tables, pair, *earlier)


def copies_kernel(plan, *refs):
    arrived = refs[-1]
    copies = [
        pltpu.make_async_copy(source, target, arrived.at[i])
        for i, (source, target) in enumerate(plan(refs[:-1]))
    ]
    for copy in copies:
        copy.start()
    for copy in copies:
        copy.wait()


def copied(plan, n_copies, arrays, outs, out_space=pltpu.HBM):
    size = sum(out.size for out in outs)
    return pl.pallas_call(
        functools.partial(copies_kernel, plan),
        in_specs=[pl.BlockSpec(memory_space=pltpu.HBM)] * len(arrays),
        out_specs=[pl.BlockSpec(memory_space=out_space)] * len(outs),
        out_shape=outs,
        scratch_shapes=[pltpu.SemaphoreType.DMA((n_copies,))],
        compiler_params=pltpu.CompilerParams(vmem_limit_bytes=VMEM_BYTES),
        cost_estimate=pl.CostEstimate(flops=0, bytes_accessed=4 * size, transcendentals=0),
    )(*arrays)


def stage_in(array):
    out = jax.ShapeDtypeStruct(array.shape, array.dtype)
    return copied(lambda refs: [(refs[0], refs[1])], 1, [array], [out], pltpu.VMEM)[0]


def first_rows(array, count):
    out = jax.ShapeDtypeStruct((count, array.shape[1]), array.dtype)
    return copied(
        lambda refs: [(refs[0].at[pl.ds(0, count)], refs[1])], 1, [array], [out], pltpu.VMEM
    )[0]


def stacked(arrays):
    n = len(arrays)
    out = jax.ShapeDtypeStruct((n,) + arrays[0].shape, arrays[0].dtype)
    return copied(lambda refs: [(refs[i], refs[n].at[i]) for i in range(n)], n, arrays, [out])[0]


def most_kernel(n_slots, *refs):
    own_ref, others_ref, hidden_ref, most_ref = refs[-4:]
    req_count, suffix_len, features = hidden_ref.shape
    chunk = chunk_of(features)
    attention = [
        jnp.concatenate([refs[r * n_slots + j][...] for r in range(req_count)]) for j in range(n_slots)
    ]
    for begin in range(0, features, chunk):
        columns = slice(begin, begin + chunk)
        mixed = jnp.dot(attention[0], own_ref[:, columns], preferred_element_type=jnp.float32)
        for j in range(1, n_slots):
            weights = others_ref[:, j - 1, :, columns].reshape(own_ref.shape[0], chunk)
            mixed = mixed + jnp.dot(attention[j], weights, preferred_element_type=jnp.float32)
        for r in range(req_count):
            rows = slice(r * suffix_len, (r + 1) * suffix_len)
            most_ref[rows, columns] = mixed[rows] + hidden_ref[r, :, columns].astype(jnp.float32)


def last_kernel(length_ref, attention_ref, others_ref, most_ref, out_ref):
    req_count, suffix_len, features = out_ref.shape
    chunk = chunk_of(features)
    position = lax.broadcasted_iota(jnp.int32, (suffix_len, chunk), 0)
    for begin in range(0, features, chunk):
        columns = slice(begin, begin + chunk)
        weights = others_ref[:, others_ref.shape[1] - 1, :, columns]
        weights = weights.reshape(attention_ref.shape[1], chunk)
        mixed = jnp.dot(attention_ref[...], weights, preferred_element_type=jnp.float32)
        mixed = mixed + most_ref[:, columns]
        for r in range(req_count):
            part = mixed[r * suffix_len : (r + 1) * suffix_len]
            part = jnp.where(position < length_ref[r], part, 0.0)
            out_ref[r, :, columns] = part.astype(jnp.bfloat16)


def project_out(lengths, attention, last_slot, w_own, w_others, hidden):
    req_count, suffix_len, features = hidden.shape
    n_slots = len(attention[0])
    rows = req_count * suffix_len
    vmem = pl.BlockSpec(memory_space=pltpu.VMEM)
    params = pltpu.CompilerParams(vmem_limit_bytes=VMEM_BYTES)
    flops = 2 * rows * features * w_own.shape[0]
    most = pl.pallas_call(
        functools.partial(most_kernel, n_slots),
        in_specs=[vmem] * (req_count * n_slots + 3),
        out_specs=vmem,
        out_shape=jax.ShapeDtypeStruct((rows, features), jnp.float32),
        compiler_params=params,
        cost_estimate=pl.CostEstimate(
            flops=flops * n_slots,
            bytes_accessed=2 * features * (w_own.shape[0] * n_slots + 3 * rows),
            transcendentals=0,
        ),
    )(*[block for slots in attention for block in slots], w_own, w_others, hidden)
    return pl.pallas_call(
        last_kernel,
        in_specs=[pl.BlockSpec(memory_space=pltpu.SMEM)] + [vmem] * 3,
        out_specs=vmem,
        out_shape=jax.ShapeDtypeStruct(hidden.shape, jnp.bfloat16),
        compiler_params=params,
        cost_estimate=pl.CostEstimate(
            flops=flops,
            bytes_accessed=2 * features * (w_own.shape[0] + 3 * rows),
            transcendentals=0,
        ),
    )(lengths, last_slot, w_others, most)


def shards(hidden, norm_gain, w_query, w_kv, w_out, prefix_cache, lengths, groups, owners):
    n_tp = lax.axis_size("tp")
    n_owners = lax.axis_size("req")
    my_index = lax.axis_index("req")
    place = lax.axis_index("tp")
    req_count, suffix_len, features = hidden.shape
    head_size = w_kv.shape[2]
    model_width = w_query.shape[0]

    flat_kv = w_kv.reshape(model_width, 2 * head_size)
    tables = rope_tables(suffix_len, head_size)

    share = w_out.shape[0] // n_owners
    my_rows = lax.dynamic_slice_in_dim(w_out, my_index * share, share, axis=0)
    moved = []
    for j in range(1, n_tp):
        begin = ring_place(place, j) * features
        moved.append(shift(lax.dynamic_slice_in_dim(my_rows, begin, features, axis=1), j))

    _, prefix_len, _, head_size = prefix_cache.shape
    prefixes = lax.all_gather(prefix_cache.reshape(prefix_len * 2, head_size), "req", axis=0)
    local_groups = lax.dynamic_slice_in_dim(groups, my_index * req_count, req_count)
    owner_of = jnp.sum(
        jnp.where(local_groups[:, None] == jnp.arange(n_owners)[None, :], owners[None, :], 0), axis=-1
    ).astype(jnp.int32)

    def weights_of(begin):
        return (
            lax.dynamic_slice_in_dim(norm_gain, begin, features).reshape(1, features),
            lax.dynamic_slice_in_dim(w_query, begin, features, axis=0),
            lax.dynamic_slice_in_dim(flat_kv, begin, features, axis=0),
        )

    total_rows = req_count * suffix_len
    packed = hidden.reshape(total_rows, features)
    offsets = [jnp.int32(0)]
    for r in range(1, req_count):
        offsets.append(offsets[-1] + (lengths[r - 1] + ROW_TILE - 1) // ROW_TILE * ROW_TILE)
        packed = lax.dynamic_update_slice(packed, hidden[r], (offsets[r], 0))
    live_rows = offsets[-1] + lengths[-1]
    offsets = jnp.stack(offsets)
    capacities = [total_rows * k // 16 for k in range(16, 12, -1)]
    branch = sum((live_rows <= capacity).astype(jnp.int32) for capacity in capacities[1:])

    begins = [ring_place(place, -step) * features for step in range(n_tp)]
    own_sums = project(packed, weights_of(begins[0]), [], total_rows, in_loop=False)
    state = (packed, own_sums, moved, tables, begins, owner_of, offsets, branch)
    state = lax.optimization_barrier(state)
    packed, own_sums, moved, tables, begins, owner_of, offsets, branch = state
    w_others = lax.all_gather(stacked(moved), "req", axis=0)

    def ring_of(capacity):
        def run(packed, sums):
            block = first_rows(packed, capacity) if capacity < total_rows else packed
            for step in range(n_tp - 1):
                coming = shift(block, 1)
                if step > 0:
                    sums = project(block, weights, sums, total_rows)
                state = (coming, sums, weights_of(begins[step + 1]))
                block, sums, weights = lax.optimization_barrier(state)
            return project(block, weights, sums, total_rows, in_loop=False)

        return run

    sums = lax.switch(branch, [ring_of(c) for c in capacities], packed, own_sums)

    earlier, gathered = [], []
    for r in range(req_count):
        pair = lax.dynamic_index_in_dim(prefixes, owner_of[r], 0, keepdims=False)
        pair = pair.reshape(prefix_len, 2, head_size).transpose(1, 0, 2)
        results = attend(
            r, suffix_len, model_width, lengths, offsets, sums, tables, pair, earlier, r == req_count - 1
        )
        earlier = earlier + list(results[:2])
        gathered.append([results[0]] + [shift(results[0], j) for j in range(1, n_tp - 1)])
        prefixes = lax.optimization_barrier(prefixes)
    _, all_attention, all_caches = results
    last_slot = shift(all_attention, n_tp - 1)
    place, _ = lax.optimization_barrier((place, all_caches))
    w_own = lax.dynamic_slice_in_dim(w_out, place * features, features, axis=1)
    suffix_cache = all_caches.reshape(req_count, suffix_len, 2, head_size)
    w_others, suffix_cache = lax.optimization_barrier((w_others, suffix_cache))
    out_hidden = project_out(lengths, gathered, last_slot, w_own, stage_in(w_others), hidden)
    return (out_hidden, suffix_cache)


def solution(mesh):
    return jax.shard_map(
        shards,
        mesh=mesh,
        in_specs=(
            P("req", None, "tp"),
            P(),
            P(None, "tp"),
            P(None, None, "tp"),
            P("tp", None),
            P("req", None, None, "tp"),
            P("req"),
            P(),
            P(),
        ),
        out_specs=(P("req", None, "tp"), P("req", None, None, "tp")),
        check_vma=False,
    )
```

```python
import functools

import jax
import jax.numpy as jnp
from jax import lax
from jax.experimental import pallas as pl
from jax.experimental.pallas import tpu as pltpu
from jax.sharding import PartitionSpec as P

PREFIX = 2048


EPSILON = 1e-05
ROPE_BASE = 5000000.0
VMEM_BYTES = 12 * 1024 * 1024
LANES = 128
ROW_TILE = 16


def rope_tables(suffix_len, head_size):
    positions = (PREFIX + jnp.arange(suffix_len)).astype(jnp.float32)
    inverse = ROPE_BASE ** (-(2.0 * jnp.arange(head_size // 2).astype(jnp.float32)) / head_size)
    angles = positions[:, None] * inverse[None, :]
    cosine_table = jnp.concatenate([jnp.cos(angles), jnp.cos(angles)], axis=-1)
    sine_table = jnp.concatenate([-jnp.sin(angles), jnp.sin(angles)], axis=-1)
    return (cosine_table, sine_table)


def ring_order(n):
    return [0] + list(range(1, n, 2)) + list(range(n - 2 if n % 2 == 0 else n - 1, 0, -2))


def ring_place(place, distance):
    n = lax.axis_size("tp")
    ring = ring_order(n)
    return sum(jnp.where(place == ring[p], ring[(p + distance) % n], 0) for p in range(n))


def shift(block, distance):
    n = lax.axis_size("tp")
    ring = ring_order(n)
    return lax.ppermute(block, "tp", [(ring[p], ring[(p + distance) % n]) for p in range(n)])


def chunk_of(size):
    return 2 * LANES if size % (2 * LANES) == 0 else LANES


def project_kernel(chunk, block_ref, gain_ref, wq_ref, wkv_ref, *refs):
    sums_in, (q_ref, kv_ref, square_ref) = refs[:-3], refs[-3:]
    rows, features = block_ref.shape

    def parts_of(part):
        block_f = block_ref[:, part].astype(jnp.float32)
        scaled = (block_f * gain_ref[:, part]).astype(jnp.bfloat16)
        squares = block_f * block_f
        square = squares[:, :LANES]
        for i in range(1, chunk // LANES):
            square = square + squares[:, i * LANES : (i + 1) * LANES]
        return (
            jnp.dot(scaled, wq_ref[part, :], preferred_element_type=jnp.float32),
            jnp.dot(scaled, wkv_ref[part, :], preferred_element_type=jnp.float32),
            square,
        )

    parts = parts_of(pl.ds(0, chunk))
    for i, ref in enumerate(refs[-3:]):
        ref[:rows] = sums_in[i][:rows] + parts[i] if sums_in else parts[i]

    def step(k, _):
        parts = parts_of(pl.ds(pl.multiple_of(k * chunk, chunk), chunk))
        for i, ref in enumerate(refs[-3:]):
            ref[:rows] += parts[i]
        return 0

    if chunk < features:
        lax.fori_loop(1, features // chunk, step, 0)


def project(block, weights, sums, total_rows, in_loop=True):
    rows, features = block.shape
    gain, w_query, flat_kv = weights
    widths = (w_query.shape[1], flat_kv.shape[1], LANES)
    vmem = pl.BlockSpec(memory_space=pltpu.VMEM)
    return pl.pallas_call(
        functools.partial(project_kernel, chunk_of(features) if in_loop else features),
        in_specs=[vmem] * (4 + len(sums)),
        out_specs=[vmem] * 3,
        out_shape=[jax.ShapeDtypeStruct((total_rows, width), jnp.float32) for width in widths],
        compiler_params=pltpu.CompilerParams(vmem_limit_bytes=VMEM_BYTES),
        cost_estimate=pl.CostEstimate(
            flops=2 * rows * features * (widths[0] + widths[1]),
            bytes_accessed=2 * features * (widths[0] + widths[1] + rows),
            transcendentals=0,
        ),
    )(block, gain, w_query, flat_kv, *sums)


def attend_kernel(
    r, last, model_width, length_ref, offset_ref, q_ref, kv_ref, square_ref, cos_ref, sin_ref, pair_ref, *refs
):
    rows = cos_ref.shape[0]
    n_earlier = 2 * r if last else 0
    earlier, att_ref, outs = refs[:n_earlier], refs[n_earlier], refs[n_earlier + 1 :]
    for i in range(n_earlier):
        outs[i % 2][i // 2 * rows : (i // 2 + 1) * rows] = earlier[i][...]
    mine = slice(r * rows, (r + 1) * rows) if last else slice(0, rows)
    cache_ref = outs[1] if last else outs[0]
    packed = pl.ds(pl.multiple_of(offset_ref[r], ROW_TILE), rows)
    head_size = pair_ref.shape[-1]
    heads = q_ref.shape[1] // head_size
    per_dot = 2 if heads % 2 == 0 else 1
    scale = head_size ** (-0.5)
    length = length_ref[r]
    cosine, sine = cos_ref[...], sin_ref[...]
    mean = jnp.sum(square_ref[packed, :], axis=-1, keepdims=True) / model_width
    row_scale = lax.rsqrt(mean + EPSILON)

    def turn(vector):
        vector = vector * row_scale
        return vector * cosine + pltpu.roll(vector, head_size // 2, 1) * sine

    keys_f = turn(kv_ref[packed, :head_size])
    values_f = kv_ref[packed, head_size:] * row_scale
    live = lax.broadcasted_iota(jnp.int32, (rows, head_size), 0) < length
    own_keys = jnp.where(live, keys_f, 0.0).astype(jnp.bfloat16)
    own_values = jnp.where(live, values_f, 0.0).astype(jnp.bfloat16)
    cache_ref[mine, :head_size] = own_keys
    cache_ref[mine, head_size:] = own_values

    position = lax.broadcasted_iota(jnp.int32, (per_dot * rows, rows), 0) % rows
    other = lax.broadcasted_iota(jnp.int32, (per_dot * rows, rows), 1)
    causal = (other <= position) & (other < length)
    against = (((1,), (1,)), ((), ()))
    for g in range(heads // per_dot):
        part = slice(g * per_dot * head_size, (g + 1) * per_dot * head_size)
        vectors = q_ref[packed, part]
        query = jnp.concatenate(
            [turn(vectors[:, i * head_size : (i + 1) * head_size]) for i in range(per_dot)]
        ).astype(jnp.bfloat16)
        scores = lax.dot_general(query, pair_ref[0], against, preferred_element_type=jnp.float32)
        own_scores = lax.dot_general(query, own_keys, against, preferred_element_type=jnp.float32)
        own_scores = jnp.where(causal, own_scores, -jnp.inf)
        highest = jnp.maximum(
            jnp.max(scores, axis=-1, keepdims=True), jnp.max(own_scores, axis=-1, keepdims=True)
        )
        weights = jnp.exp((scores - highest) * scale)
        own_weights = jnp.exp((own_scores - highest) * scale)
        total = jnp.sum(weights, axis=-1, keepdims=True) + jnp.sum(own_weights, axis=-1, keepdims=True)
        mixed = jnp.dot(weights.astype(jnp.bfloat16), pair_ref[1], preferred_element_type=jnp.float32)
        mixed = mixed + jnp.dot(
            own_weights.astype(jnp.bfloat16), own_values, preferred_element_type=jnp.float32
        )
        mixed = (mixed / total).astype(jnp.bfloat16)
        mixed = jnp.concatenate([mixed[i * rows : (i + 1) * rows] for i in range(per_dot)], axis=1)
        att_ref[:, part] = mixed
        if last:
            outs[0][mine, part] = mixed


def attend(r, suffix_len, model_width, lengths, offsets, sums, tables, pair, earlier, last):
    width = sums[0].shape[1]
    _, prefix_len, head_size = pair.shape
    vmem = pl.BlockSpec(memory_space=pltpu.VMEM)
    smem = pl.BlockSpec(memory_space=pltpu.SMEM)
    widths = (width, 2 * head_size)
    all_rows = (r + 1) * suffix_len
    shapes = [(suffix_len, width)]
    shapes += [(all_rows, w) for w in widths] if last else [(suffix_len, widths[1])]
    earlier = earlier if last else []
    return pl.pallas_call(
        functools.partial(attend_kernel, r, last, model_width),
        in_specs=[smem] * 2 + [vmem] * (6 + len(earlier)),
        out_specs=[vmem] * len(shapes),
        out_shape=[jax.ShapeDtypeStruct(shape, jnp.bfloat16) for shape in shapes],
        compiler_params=pltpu.CompilerParams(vmem_limit_bytes=VMEM_BYTES),
        cost_estimate=pl.CostEstimate(
            flops=4 * suffix_len * width * (prefix_len + suffix_len),
            bytes_accessed=4 * prefix_len * head_size + 4 * suffix_len * (width + 2 * head_size),
            transcendentals=suffix_len * width // head_size * prefix_len,
        ),
    )(lengths, offsets, *sums, *tables, pair, *earlier)


def copies_kernel(plan, *refs):
    arrived = refs[-1]
    copies = [
        pltpu.make_async_copy(source, target, arrived.at[i])
        for i, (source, target) in enumerate(plan(refs[:-1]))
    ]
    for copy in copies:
        copy.start()
    for copy in copies:
        copy.wait()


def copied(plan, n_copies, arrays, outs, out_space=pltpu.HBM):
    size = sum(out.size for out in outs)
    return pl.pallas_call(
        functools.partial(copies_kernel, plan),
        in_specs=[pl.BlockSpec(memory_space=pltpu.HBM)] * len(arrays),
        out_specs=[pl.BlockSpec(memory_space=out_space)] * len(outs),
        out_shape=outs,
        scratch_shapes=[pltpu.SemaphoreType.DMA((n_copies,))],
        compiler_params=pltpu.CompilerParams(vmem_limit_bytes=VMEM_BYTES),
        cost_estimate=pl.CostEstimate(flops=0, bytes_accessed=4 * size, transcendentals=0),
    )(*arrays)


def stage_in(array):
    out = jax.ShapeDtypeStruct(array.shape, array.dtype)
    return copied(lambda refs: [(refs[0], refs[1])], 1, [array], [out], pltpu.VMEM)[0]


def first_rows(array, count):
    out = jax.ShapeDtypeStruct((count, array.shape[1]), array.dtype)
    return copied(
        lambda refs: [(refs[0].at[pl.ds(0, count)], refs[1])], 1, [array], [out], pltpu.VMEM
    )[0]


def stacked(arrays):
    n = len(arrays)
    out = jax.ShapeDtypeStruct((n,) + arrays[0].shape, arrays[0].dtype)
    return copied(lambda refs: [(refs[i], refs[n].at[i]) for i in range(n)], n, arrays, [out])[0]


def most_kernel(n_slots, *refs):
    own_ref, others_ref, hidden_ref, most_ref = refs[-4:]
    req_count, suffix_len, features = hidden_ref.shape
    chunk = chunk_of(features)
    attention = [
        jnp.concatenate([refs[r * n_slots + j][...] for r in range(req_count)]) for j in range(n_slots)
    ]
    for begin in range(0, features, chunk):
        columns = slice(begin, begin + chunk)
        mixed = jnp.dot(attention[0], own_ref[:, columns], preferred_element_type=jnp.float32)
        for j in range(1, n_slots):
            weights = others_ref[:, j - 1, :, columns].reshape(own_ref.shape[0], chunk)
            mixed = mixed + jnp.dot(attention[j], weights, preferred_element_type=jnp.float32)
        for r in range(req_count):
            rows = slice(r * suffix_len, (r + 1) * suffix_len)
            most_ref[rows, columns] = mixed[rows] + hidden_ref[r, :, columns].astype(jnp.float32)


def last_kernel(length_ref, attention_ref, others_ref, most_ref, out_ref):
    req_count, suffix_len, features = out_ref.shape
    chunk = chunk_of(features)
    position = lax.broadcasted_iota(jnp.int32, (suffix_len, chunk), 0)
    for begin in range(0, features, chunk):
        columns = slice(begin, begin + chunk)
        weights = others_ref[:, others_ref.shape[1] - 1, :, columns]
        weights = weights.reshape(attention_ref.shape[1], chunk)
        mixed = jnp.dot(attention_ref[...], weights, preferred_element_type=jnp.float32)
        mixed = mixed + most_ref[:, columns]
        for r in range(req_count):
            part = mixed[r * suffix_len : (r + 1) * suffix_len]
            part = jnp.where(position < length_ref[r], part, 0.0)
            out_ref[r, :, columns] = part.astype(jnp.bfloat16)


def project_out(lengths, attention, last_slot, w_own, w_others, hidden):
    req_count, suffix_len, features = hidden.shape
    n_slots = len(attention[0])
    rows = req_count * suffix_len
    vmem = pl.BlockSpec(memory_space=pltpu.VMEM)
    params = pltpu.CompilerParams(vmem_limit_bytes=VMEM_BYTES)
    flops = 2 * rows * features * w_own.shape[0]
    most = pl.pallas_call(
        functools.partial(most_kernel, n_slots),
        in_specs=[vmem] * (req_count * n_slots + 3),
        out_specs=vmem,
        out_shape=jax.ShapeDtypeStruct((rows, features), jnp.float32),
        compiler_params=params,
        cost_estimate=pl.CostEstimate(
            flops=flops * n_slots,
            bytes_accessed=2 * features * (w_own.shape[0] * n_slots + 3 * rows),
            transcendentals=0,
        ),
    )(*[block for slots in attention for block in slots], w_own, w_others, hidden)
    return pl.pallas_call(
        last_kernel,
        in_specs=[pl.BlockSpec(memory_space=pltpu.SMEM)] + [vmem] * 3,
        out_specs=vmem,
        out_shape=jax.ShapeDtypeStruct(hidden.shape, jnp.bfloat16),
        compiler_params=params,
        cost_estimate=pl.CostEstimate(
            flops=flops,
            bytes_accessed=2 * features * (w_own.shape[0] + 3 * rows),
            transcendentals=0,
        ),
    )(lengths, last_slot, w_others, most)


def shards(hidden, norm_gain, w_query, w_kv, w_out, prefix_cache, lengths, groups, owners):
    n_tp = lax.axis_size("tp")
    n_owners = lax.axis_size("req")
    my_index = lax.axis_index("req")
    place = lax.axis_index("tp")
    req_count, suffix_len, features = hidden.shape
    head_size = w_kv.shape[2]
    model_width = w_query.shape[0]

    flat_kv = w_kv.reshape(model_width, 2 * head_size)
    tables = rope_tables(suffix_len, head_size)

    share = w_out.shape[0] // n_owners
    my_rows = lax.dynamic_slice_in_dim(w_out, my_index * share, share, axis=0)
    moved = []
    for j in range(1, n_tp):
        begin = ring_place(place, j) * features
        moved.append(shift(lax.dynamic_slice_in_dim(my_rows, begin, features, axis=1), j))

    _, prefix_len, _, head_size = prefix_cache.shape
    prefixes = lax.all_gather(prefix_cache.reshape(prefix_len * 2, head_size), "req", axis=0)
    local_groups = lax.dynamic_slice_in_dim(groups, my_index * req_count, req_count)
    owner_of = jnp.sum(
        jnp.where(local_groups[:, None] == jnp.arange(n_owners)[None, :], owners[None, :], 0), axis=-1
    ).astype(jnp.int32)

    def weights_of(begin):
        return (
            lax.dynamic_slice_in_dim(norm_gain, begin, features).reshape(1, features),
            lax.dynamic_slice_in_dim(w_query, begin, features, axis=0),
            lax.dynamic_slice_in_dim(flat_kv, begin, features, axis=0),
        )

    total_rows = req_count * suffix_len
    packed = hidden.reshape(total_rows, features)
    offsets = [jnp.int32(0)]
    for r in range(1, req_count):
        offsets.append(offsets[-1] + (lengths[r - 1] + ROW_TILE - 1) // ROW_TILE * ROW_TILE)
        packed = lax.dynamic_update_slice(packed, hidden[r], (offsets[r], 0))
    live_rows = offsets[-1] + lengths[-1]
    offsets = jnp.stack(offsets)
    capacities = [total_rows * k // 8 for k in range(8, 3, -1)]
    branch = sum((live_rows <= capacity).astype(jnp.int32) for capacity in capacities[1:])

    begins = [ring_place(place, -step) * features for step in range(n_tp)]
    own_sums = project(packed, weights_of(begins[0]), [], total_rows, in_loop=False)
    state = (packed, own_sums, moved, tables, begins, owner_of, offsets, branch)
    state = lax.optimization_barrier(state)
    packed, own_sums, moved, tables, begins, owner_of, offsets, branch = state
    w_others = lax.all_gather(stacked(moved), "req", axis=0)

    def ring_of(capacity):
        def run(packed, sums):
            block = first_rows(packed, capacity) if capacity < total_rows else packed
            for step in range(n_tp - 1):
                coming = shift(block, 1)
                if step > 0:
                    sums = project(block, weights, sums, total_rows)
                state = (coming, sums, weights_of(begins[step + 1]))
                block, sums, weights = lax.optimization_barrier(state)
            return project(block, weights, sums, total_rows, in_loop=False)

        return run

    sums = lax.switch(branch, [ring_of(c) for c in capacities], packed, own_sums)

    earlier, gathered = [], []
    for r in range(req_count):
        pair = lax.dynamic_index_in_dim(prefixes, owner_of[r], 0, keepdims=False)
        pair = pair.reshape(prefix_len, 2, head_size).transpose(1, 0, 2)
        results = attend(
            r, suffix_len, model_width, lengths, offsets, sums, tables, pair, earlier, r == req_count - 1
        )
        earlier = earlier + list(results[:2])
        gathered.append([results[0]] + [shift(results[0], j) for j in range(1, n_tp - 1)])
        prefixes = lax.optimization_barrier(prefixes)
    _, all_attention, all_caches = results
    last_slot = shift(all_attention, n_tp - 1)
    place, _ = lax.optimization_barrier((place, all_caches))
    w_own = lax.dynamic_slice_in_dim(w_out, place * features, features, axis=1)
    suffix_cache = all_caches.reshape(req_count, suffix_len, 2, head_size)
    w_others, suffix_cache = lax.optimization_barrier((w_others, suffix_cache))
    out_hidden = project_out(lengths, gathered, last_slot, w_own, stage_in(w_others), hidden)
    return (out_hidden, suffix_cache)


def solution(mesh):
    return jax.shard_map(
        shards,
        mesh=mesh,
        in_specs=(
            P("req", None, "tp"),
            P(),
            P(None, "tp"),
            P(None, None, "tp"),
            P("tp", None),
            P("req", None, None, "tp"),
            P("req"),
            P(),
            P(),
        ),
        out_specs=(P("req", None, "tp"), P("req", None, None, "tp")),
        check_vma=False,
    )
```

```python
import functools

import jax
import jax.numpy as jnp
from jax import lax
from jax.experimental import pallas as pl
from jax.experimental.pallas import tpu as pltpu
from jax.sharding import PartitionSpec as P

PREFIX = 2048


EPSILON = 1e-05
ROPE_BASE = 5000000.0
VMEM_BYTES = 12 * 1024 * 1024
LANES = 128
ROW_TILE = 16


def rope_tables(suffix_len, head_size):
    positions = (PREFIX + jnp.arange(suffix_len)).astype(jnp.float32)
    inverse = ROPE_BASE ** (-(2.0 * jnp.arange(head_size // 2).astype(jnp.float32)) / head_size)
    angles = positions[:, None] * inverse[None, :]
    cosine_table = jnp.concatenate([jnp.cos(angles), jnp.cos(angles)], axis=-1)
    sine_table = jnp.concatenate([-jnp.sin(angles), jnp.sin(angles)], axis=-1)
    return (cosine_table, sine_table)


def ring_order(n):
    return [0] + list(range(1, n, 2)) + list(range(n - 2 if n % 2 == 0 else n - 1, 0, -2))


def ring_place(place, distance):
    n = lax.axis_size("tp")
    ring = ring_order(n)
    return sum(jnp.where(place == ring[p], ring[(p + distance) % n], 0) for p in range(n))


def shift(block, distance):
    n = lax.axis_size("tp")
    ring = ring_order(n)
    return lax.ppermute(block, "tp", [(ring[p], ring[(p + distance) % n]) for p in range(n)])


def chunk_of(size):
    return 2 * LANES if size % (2 * LANES) == 0 else LANES


def project_kernel(chunk, block_ref, gain_ref, wq_ref, wkv_ref, *refs):
    sums_in, (q_ref, kv_ref, square_ref) = refs[:-3], refs[-3:]
    rows, features = block_ref.shape

    def parts_of(part):
        block_f = block_ref[:, part].astype(jnp.float32)
        scaled = (block_f * gain_ref[:, part]).astype(jnp.bfloat16)
        squares = block_f * block_f
        square = squares[:, :LANES]
        for i in range(1, chunk // LANES):
            square = square + squares[:, i * LANES : (i + 1) * LANES]
        return (
            jnp.dot(scaled, wq_ref[part, :], preferred_element_type=jnp.float32),
            jnp.dot(scaled, wkv_ref[part, :], preferred_element_type=jnp.float32),
            square,
        )

    parts = parts_of(pl.ds(0, chunk))
    for i, ref in enumerate(refs[-3:]):
        ref[:rows] = sums_in[i][:rows] + parts[i] if sums_in else parts[i]

    def step(k, _):
        parts = parts_of(pl.ds(pl.multiple_of(k * chunk, chunk), chunk))
        for i, ref in enumerate(refs[-3:]):
            ref[:rows] += parts[i]
        return 0

    if chunk < features:
        lax.fori_loop(1, features // chunk, step, 0)


def project(block, weights, sums, total_rows, in_loop=True):
    rows, features = block.shape
    gain, w_query, flat_kv = weights
    widths = (w_query.shape[1], flat_kv.shape[1], LANES)
    vmem = pl.BlockSpec(memory_space=pltpu.VMEM)
    return pl.pallas_call(
        functools.partial(project_kernel, chunk_of(features) if in_loop else features),
        in_specs=[vmem] * (4 + len(sums)),
        out_specs=[vmem] * 3,
        out_shape=[jax.ShapeDtypeStruct((total_rows, width), jnp.float32) for width in widths],
        compiler_params=pltpu.CompilerParams(vmem_limit_bytes=VMEM_BYTES),
        cost_estimate=pl.CostEstimate(
            flops=2 * rows * features * (widths[0] + widths[1]),
            bytes_accessed=2 * features * (widths[0] + widths[1] + rows),
            transcendentals=0,
        ),
    )(block, gain, w_query, flat_kv, *sums)


def attend_kernel(
    r, last, model_width, length_ref, offset_ref, q_ref, kv_ref, square_ref, cos_ref, sin_ref, pair_ref, *refs
):
    rows = cos_ref.shape[0]
    n_earlier = 2 * r if last else 0
    earlier, att_ref, outs = refs[:n_earlier], refs[n_earlier], refs[n_earlier + 1 :]
    for i in range(n_earlier):
        outs[i % 2][i // 2 * rows : (i // 2 + 1) * rows] = earlier[i][...]
    mine = slice(r * rows, (r + 1) * rows) if last else slice(0, rows)
    cache_ref = outs[1] if last else outs[0]
    packed = pl.ds(pl.multiple_of(offset_ref[r], ROW_TILE), rows)
    head_size = pair_ref.shape[-1]
    heads = q_ref.shape[1] // head_size
    per_dot = 2 if heads % 2 == 0 else 1
    scale = head_size ** (-0.5)
    length = length_ref[r]
    cosine, sine = cos_ref[...], sin_ref[...]
    mean = jnp.sum(square_ref[packed, :], axis=-1, keepdims=True) / model_width
    row_scale = lax.rsqrt(mean + EPSILON)

    def turn(vector):
        vector = vector * row_scale
        return vector * cosine + pltpu.roll(vector, head_size // 2, 1) * sine

    keys_f = turn(kv_ref[packed, :head_size])
    values_f = kv_ref[packed, head_size:] * row_scale
    live = lax.broadcasted_iota(jnp.int32, (rows, head_size), 0) < length
    own_keys = jnp.where(live, keys_f, 0.0).astype(jnp.bfloat16)
    own_values = jnp.where(live, values_f, 0.0).astype(jnp.bfloat16)
    cache_ref[mine, :head_size] = own_keys
    cache_ref[mine, head_size:] = own_values

    position = lax.broadcasted_iota(jnp.int32, (per_dot * rows, rows), 0) % rows
    other = lax.broadcasted_iota(jnp.int32, (per_dot * rows, rows), 1)
    causal = (other <= position) & (other < length)
    against = (((1,), (1,)), ((), ()))
    for g in range(heads // per_dot):
        part = slice(g * per_dot * head_size, (g + 1) * per_dot * head_size)
        vectors = q_ref[packed, part]
        query = jnp.concatenate(
            [turn(vectors[:, i * head_size : (i + 1) * head_size]) for i in range(per_dot)]
        ).astype(jnp.bfloat16)
        scores = lax.dot_general(query, pair_ref[0], against, preferred_element_type=jnp.float32)
        own_scores = lax.dot_general(query, own_keys, against, preferred_element_type=jnp.float32)
        own_scores = jnp.where(causal, own_scores, -jnp.inf)
        highest = jnp.maximum(
            jnp.max(scores, axis=-1, keepdims=True), jnp.max(own_scores, axis=-1, keepdims=True)
        )
        weights = jnp.exp((scores - highest) * scale)
        own_weights = jnp.exp((own_scores - highest) * scale)
        total = jnp.sum(weights, axis=-1, keepdims=True) + jnp.sum(own_weights, axis=-1, keepdims=True)
        mixed = jnp.dot(weights.astype(jnp.bfloat16), pair_ref[1], preferred_element_type=jnp.float32)
        mixed = mixed + jnp.dot(
            own_weights.astype(jnp.bfloat16), own_values, preferred_element_type=jnp.float32
        )
        mixed = (mixed / total).astype(jnp.bfloat16)
        mixed = jnp.concatenate([mixed[i * rows : (i + 1) * rows] for i in range(per_dot)], axis=1)
        att_ref[:, part] = mixed
        if last:
            outs[0][mine, part] = mixed


def attend(r, suffix_len, model_width, lengths, offsets, sums, tables, pair, earlier, last):
    width = sums[0].shape[1]
    _, prefix_len, head_size = pair.shape
    vmem = pl.BlockSpec(memory_space=pltpu.VMEM)
    smem = pl.BlockSpec(memory_space=pltpu.SMEM)
    widths = (width, 2 * head_size)
    all_rows = (r + 1) * suffix_len
    shapes = [(suffix_len, width)]
    shapes += [(all_rows, w) for w in widths] if last else [(suffix_len, widths[1])]
    earlier = earlier if last else []
    return pl.pallas_call(
        functools.partial(attend_kernel, r, last, model_width),
        in_specs=[smem] * 2 + [vmem] * (6 + len(earlier)),
        out_specs=[vmem] * len(shapes),
        out_shape=[jax.ShapeDtypeStruct(shape, jnp.bfloat16) for shape in shapes],
        compiler_params=pltpu.CompilerParams(vmem_limit_bytes=VMEM_BYTES),
        cost_estimate=pl.CostEstimate(
            flops=4 * suffix_len * width * (prefix_len + suffix_len),
            bytes_accessed=4 * prefix_len * head_size + 4 * suffix_len * (width + 2 * head_size),
            transcendentals=suffix_len * width // head_size * prefix_len,
        ),
    )(lengths, offsets, *sums, *tables, pair, *earlier)


def copies_kernel(plan, *refs):
    arrived = refs[-1]
    copies = [
        pltpu.make_async_copy(source, target, arrived.at[i])
        for i, (source, target) in enumerate(plan(refs[:-1]))
    ]
    for copy in copies:
        copy.start()
    for copy in copies:
        copy.wait()


def copied(plan, n_copies, arrays, outs, out_space=pltpu.HBM):
    size = sum(out.size for out in outs)
    return pl.pallas_call(
        functools.partial(copies_kernel, plan),
        in_specs=[pl.BlockSpec(memory_space=pltpu.HBM)] * len(arrays),
        out_specs=[pl.BlockSpec(memory_space=out_space)] * len(outs),
        out_shape=outs,
        scratch_shapes=[pltpu.SemaphoreType.DMA((n_copies,))],
        compiler_params=pltpu.CompilerParams(vmem_limit_bytes=VMEM_BYTES),
        cost_estimate=pl.CostEstimate(flops=0, bytes_accessed=4 * size, transcendentals=0),
    )(*arrays)


def stage_in(array):
    out = jax.ShapeDtypeStruct(array.shape, array.dtype)
    return copied(lambda refs: [(refs[0], refs[1])], 1, [array], [out], pltpu.VMEM)[0]


def first_rows(array, count):
    out = jax.ShapeDtypeStruct((count, array.shape[1]), array.dtype)
    return copied(
        lambda refs: [(refs[0].at[pl.ds(0, count)], refs[1])], 1, [array], [out], pltpu.VMEM
    )[0]


def stacked(arrays):
    n = len(arrays)
    out = jax.ShapeDtypeStruct((n,) + arrays[0].shape, arrays[0].dtype)
    return copied(lambda refs: [(refs[i], refs[n].at[i]) for i in range(n)], n, arrays, [out])[0]


def most_kernel(n_slots, *refs):
    own_ref, others_ref, hidden_ref, most_ref = refs[-4:]
    req_count, suffix_len, features = hidden_ref.shape
    chunk = chunk_of(features)
    attention = [
        jnp.concatenate([refs[r * n_slots + j][...] for r in range(req_count)]) for j in range(n_slots)
    ]
    for begin in range(0, features, chunk):
        columns = slice(begin, begin + chunk)
        mixed = jnp.dot(attention[0], own_ref[:, columns], preferred_element_type=jnp.float32)
        for j in range(1, n_slots):
            weights = others_ref[:, j - 1, :, columns].reshape(own_ref.shape[0], chunk)
            mixed = mixed + jnp.dot(attention[j], weights, preferred_element_type=jnp.float32)
        for r in range(req_count):
            rows = slice(r * suffix_len, (r + 1) * suffix_len)
            most_ref[rows, columns] = mixed[rows] + hidden_ref[r, :, columns].astype(jnp.float32)


def last_kernel(length_ref, attention_ref, others_ref, most_ref, out_ref):
    req_count, suffix_len, features = out_ref.shape
    chunk = chunk_of(features)
    position = lax.broadcasted_iota(jnp.int32, (suffix_len, chunk), 0)
    for begin in range(0, features, chunk):
        columns = slice(begin, begin + chunk)
        weights = others_ref[:, others_ref.shape[1] - 1, :, columns]
        weights = weights.reshape(attention_ref.shape[1], chunk)
        mixed = jnp.dot(attention_ref[...], weights, preferred_element_type=jnp.float32)
        mixed = mixed + most_ref[:, columns]
        for r in range(req_count):
            part = mixed[r * suffix_len : (r + 1) * suffix_len]
            part = jnp.where(position < length_ref[r], part, 0.0)
            out_ref[r, :, columns] = part.astype(jnp.bfloat16)


def project_out(lengths, attention, last_slot, w_own, w_others, hidden):
    req_count, suffix_len, features = hidden.shape
    n_slots = len(attention[0])
    rows = req_count * suffix_len
    vmem = pl.BlockSpec(memory_space=pltpu.VMEM)
    params = pltpu.CompilerParams(vmem_limit_bytes=VMEM_BYTES)
    flops = 2 * rows * features * w_own.shape[0]
    most = pl.pallas_call(
        functools.partial(most_kernel, n_slots),
        in_specs=[vmem] * (req_count * n_slots + 3),
        out_specs=vmem,
        out_shape=jax.ShapeDtypeStruct((rows, features), jnp.float32),
        compiler_params=params,
        cost_estimate=pl.CostEstimate(
            flops=flops * n_slots,
            bytes_accessed=2 * features * (w_own.shape[0] * n_slots + 3 * rows),
            transcendentals=0,
        ),
    )(*[block for slots in attention for block in slots], w_own, w_others, hidden)
    return pl.pallas_call(
        last_kernel,
        in_specs=[pl.BlockSpec(memory_space=pltpu.SMEM)] + [vmem] * 3,
        out_specs=vmem,
        out_shape=jax.ShapeDtypeStruct(hidden.shape, jnp.bfloat16),
        compiler_params=params,
        cost_estimate=pl.CostEstimate(
            flops=flops,
            bytes_accessed=2 * features * (w_own.shape[0] + 3 * rows),
            transcendentals=0,
        ),
    )(lengths, last_slot, w_others, most)


def shards(hidden, norm_gain, w_query, w_kv, w_out, prefix_cache, lengths, groups, owners):
    n_tp = lax.axis_size("tp")
    n_owners = lax.axis_size("req")
    my_index = lax.axis_index("req")
    place = lax.axis_index("tp")
    req_count, suffix_len, features = hidden.shape
    head_size = w_kv.shape[2]
    model_width = w_query.shape[0]

    flat_kv = w_kv.reshape(model_width, 2 * head_size)
    tables = rope_tables(suffix_len, head_size)

    share = w_out.shape[0] // n_owners
    my_rows = lax.dynamic_slice_in_dim(w_out, my_index * share, share, axis=0)
    moved = []
    for j in range(1, n_tp):
        begin = ring_place(place, j) * features
        moved.append(shift(lax.dynamic_slice_in_dim(my_rows, begin, features, axis=1), j))

    _, prefix_len, _, head_size = prefix_cache.shape
    prefixes = lax.all_gather(prefix_cache.reshape(prefix_len * 2, head_size), "req", axis=0)
    local_groups = lax.dynamic_slice_in_dim(groups, my_index * req_count, req_count)
    owner_of = jnp.sum(
        jnp.where(local_groups[:, None] == jnp.arange(n_owners)[None, :], owners[None, :], 0), axis=-1
    ).astype(jnp.int32)

    def weights_of(begin):
        return (
            lax.dynamic_slice_in_dim(norm_gain, begin, features).reshape(1, features),
            lax.dynamic_slice_in_dim(w_query, begin, features, axis=0),
            lax.dynamic_slice_in_dim(flat_kv, begin, features, axis=0),
        )

    total_rows = req_count * suffix_len
    packed = hidden.reshape(total_rows, features)
    offsets = [jnp.int32(0)]
    for r in range(1, req_count):
        offsets.append(offsets[-1] + (lengths[r - 1] + ROW_TILE - 1) // ROW_TILE * ROW_TILE)
        packed = lax.dynamic_update_slice(packed, hidden[r], (offsets[r], 0))
    live_rows = offsets[-1] + lengths[-1]
    offsets = jnp.stack(offsets)
    capacities = [total_rows * k // 8 for k in range(8, 3, -1)]
    branch = sum((live_rows <= capacity).astype(jnp.int32) for capacity in capacities[1:])

    begins = [ring_place(place, -step) * features for step in range(n_tp)]
    own_sums = project(packed, weights_of(begins[0]), [], total_rows, in_loop=False)
    w_own = lax.dynamic_slice_in_dim(w_out, begins[0], features, axis=1)
    state = (packed, own_sums, moved, tables, w_own, begins, owner_of, offsets, branch)
    state = lax.optimization_barrier(state)
    packed, own_sums, moved, tables, w_own, begins, owner_of, offsets, branch = state
    w_others = lax.all_gather(stacked(moved), "req", axis=0)

    def ring_of(capacity):
        def run(packed, sums):
            block = first_rows(packed, capacity) if capacity < total_rows else packed
            for step in range(n_tp - 1):
                coming = shift(block, 1)
                if step > 0:
                    sums = project(block, weights, sums, total_rows)
                state = (coming, sums, weights_of(begins[step + 1]))
                block, sums, weights = lax.optimization_barrier(state)
            return project(block, weights, sums, total_rows, in_loop=False)

        return run

    sums = lax.switch(branch, [ring_of(c) for c in capacities], packed, own_sums)

    earlier, gathered = [], []
    for r in range(req_count):
        pair = lax.dynamic_index_in_dim(prefixes, owner_of[r], 0, keepdims=False)
        pair = pair.reshape(prefix_len, 2, head_size).transpose(1, 0, 2)
        results = attend(
            r, suffix_len, model_width, lengths, offsets, sums, tables, pair, earlier, r == req_count - 1
        )
        earlier = earlier + list(results[:2])
        gathered.append([results[0]] + [shift(results[0], j) for j in range(1, n_tp - 1)])
        prefixes = lax.optimization_barrier(prefixes)
    _, all_attention, all_caches = results
    last_slot = shift(all_attention, n_tp - 1)
    suffix_cache = all_caches.reshape(req_count, suffix_len, 2, head_size)
    w_others, suffix_cache = lax.optimization_barrier((w_others, suffix_cache))
    out_hidden = project_out(lengths, gathered, last_slot, w_own, stage_in(w_others), hidden)
    return (out_hidden, suffix_cache)


def solution(mesh):
    return jax.shard_map(
        shards,
        mesh=mesh,
        in_specs=(
            P("req", None, "tp"),
            P(),
            P(None, "tp"),
            P(None, None, "tp"),
            P("tp", None),
            P("req", None, None, "tp"),
            P("req"),
            P(),
            P(),
        ),
        out_specs=(P("req", None, "tp"), P("req", None, None, "tp")),
        check_vma=False,
    )
```

```python
import functools

import jax
import jax.numpy as jnp
from jax import lax
from jax.experimental import pallas as pl
from jax.experimental.pallas import tpu as pltpu
from jax.sharding import PartitionSpec as P

PREFIX = 2048


EPSILON = 1e-05
ROPE_BASE = 5000000.0
VMEM_BYTES = 12 * 1024 * 1024
LANES = 128
ROW_TILE = 16


def rope_tables(suffix_len, head_size):
    positions = (PREFIX + jnp.arange(suffix_len)).astype(jnp.float32)
    inverse = ROPE_BASE ** (-(2.0 * jnp.arange(head_size // 2).astype(jnp.float32)) / head_size)
    angles = positions[:, None] * inverse[None, :]
    cosine_table = jnp.concatenate([jnp.cos(angles), jnp.cos(angles)], axis=-1)
    sine_table = jnp.concatenate([-jnp.sin(angles), jnp.sin(angles)], axis=-1)
    return (cosine_table, sine_table)


def ring_order(n):
    return [0] + list(range(1, n, 2)) + list(range(n - 2 if n % 2 == 0 else n - 1, 0, -2))


def ring_place(place, distance):
    n = lax.axis_size("tp")
    ring = ring_order(n)
    return sum(jnp.where(place == ring[p], ring[(p + distance) % n], 0) for p in range(n))


def shift(block, distance):
    n = lax.axis_size("tp")
    ring = ring_order(n)
    return lax.ppermute(block, "tp", [(ring[p], ring[(p + distance) % n]) for p in range(n)])


def chunk_of(size):
    return 2 * LANES if size % (2 * LANES) == 0 else LANES


def project_kernel(chunk, block_ref, gain_ref, wq_ref, wkv_ref, *refs):
    sums_in, (q_ref, kv_ref, square_ref) = refs[:-3], refs[-3:]
    rows, features = block_ref.shape

    def parts_of(part):
        block_f = block_ref[:, part].astype(jnp.float32)
        scaled = (block_f * gain_ref[:, part]).astype(jnp.bfloat16)
        squares = block_f * block_f
        square = squares[:, :LANES]
        for i in range(1, chunk // LANES):
            square = square + squares[:, i * LANES : (i + 1) * LANES]
        return (
            jnp.dot(scaled, wq_ref[part, :], preferred_element_type=jnp.float32),
            jnp.dot(scaled, wkv_ref[part, :], preferred_element_type=jnp.float32),
            square,
        )

    parts = parts_of(pl.ds(0, chunk))
    for i, ref in enumerate(refs[-3:]):
        ref[:rows] = sums_in[i][:rows] + parts[i] if sums_in else parts[i]

    def step(k, _):
        parts = parts_of(pl.ds(pl.multiple_of(k * chunk, chunk), chunk))
        for i, ref in enumerate(refs[-3:]):
            ref[:rows] += parts[i]
        return 0

    if chunk < features:
        lax.fori_loop(1, features // chunk, step, 0)


def project(block, weights, sums, total_rows, in_loop=True):
    rows, features = block.shape
    gain, w_query, flat_kv = weights
    widths = (w_query.shape[1], flat_kv.shape[1], LANES)
    vmem = pl.BlockSpec(memory_space=pltpu.VMEM)
    return pl.pallas_call(
        functools.partial(project_kernel, chunk_of(features) if in_loop else features),
        in_specs=[vmem] * (4 + len(sums)),
        out_specs=[vmem] * 3,
        out_shape=[jax.ShapeDtypeStruct((total_rows, width), jnp.float32) for width in widths],
        compiler_params=pltpu.CompilerParams(vmem_limit_bytes=VMEM_BYTES),
        cost_estimate=pl.CostEstimate(
            flops=2 * rows * features * (widths[0] + widths[1]),
            bytes_accessed=2 * features * (widths[0] + widths[1] + rows),
            transcendentals=0,
        ),
    )(block, gain, w_query, flat_kv, *sums)


def attend_kernel(
    r, last, model_width, length_ref, offset_ref, q_ref, kv_ref, square_ref, cos_ref, sin_ref, pair_ref, *refs
):
    rows = cos_ref.shape[0]
    n_earlier = 2 * r if last else 0
    earlier, att_ref, outs = refs[:n_earlier], refs[n_earlier], refs[n_earlier + 1 :]
    for i in range(n_earlier):
        outs[i % 2][i // 2 * rows : (i // 2 + 1) * rows] = earlier[i][...]
    mine = slice(r * rows, (r + 1) * rows) if last else slice(0, rows)
    cache_ref = outs[1] if last else outs[0]
    packed = pl.ds(pl.multiple_of(offset_ref[r], ROW_TILE), rows)
    head_size = pair_ref.shape[-1]
    heads = q_ref.shape[1] // head_size
    per_dot = 2 if heads % 2 == 0 else 1
    scale = head_size ** (-0.5)
    length = length_ref[r]
    cosine, sine = cos_ref[...], sin_ref[...]
    mean = jnp.sum(square_ref[packed, :], axis=-1, keepdims=True) / model_width
    row_scale = lax.rsqrt(mean + EPSILON)

    def turn(vector):
        vector = vector * row_scale
        return vector * cosine + pltpu.roll(vector, head_size // 2, 1) * sine

    keys_f = turn(kv_ref[packed, :head_size])
    values_f = kv_ref[packed, head_size:] * row_scale
    live = lax.broadcasted_iota(jnp.int32, (rows, head_size), 0) < length
    own_keys = jnp.where(live, keys_f, 0.0).astype(jnp.bfloat16)
    own_values = jnp.where(live, values_f, 0.0).astype(jnp.bfloat16)
    cache_ref[mine, :head_size] = own_keys
    cache_ref[mine, head_size:] = own_values

    position = lax.broadcasted_iota(jnp.int32, (per_dot * rows, rows), 0) % rows
    other = lax.broadcasted_iota(jnp.int32, (per_dot * rows, rows), 1)
    causal = (other <= position) & (other < length)
    against = (((1,), (1,)), ((), ()))
    for g in range(heads // per_dot):
        part = slice(g * per_dot * head_size, (g + 1) * per_dot * head_size)
        vectors = q_ref[packed, part]
        query = jnp.concatenate(
            [turn(vectors[:, i * head_size : (i + 1) * head_size]) for i in range(per_dot)]
        ).astype(jnp.bfloat16)
        scores = lax.dot_general(query, pair_ref[0], against, preferred_element_type=jnp.float32)
        own_scores = lax.dot_general(query, own_keys, against, preferred_element_type=jnp.float32)
        own_scores = jnp.where(causal, own_scores, -jnp.inf)
        highest = jnp.maximum(
            jnp.max(scores, axis=-1, keepdims=True), jnp.max(own_scores, axis=-1, keepdims=True)
        )
        weights = jnp.exp((scores - highest) * scale)
        own_weights = jnp.exp((own_scores - highest) * scale)
        total = jnp.sum(weights, axis=-1, keepdims=True) + jnp.sum(own_weights, axis=-1, keepdims=True)
        mixed = jnp.dot(weights.astype(jnp.bfloat16), pair_ref[1], preferred_element_type=jnp.float32)
        mixed = mixed + jnp.dot(
            own_weights.astype(jnp.bfloat16), own_values, preferred_element_type=jnp.float32
        )
        mixed = (mixed / total).astype(jnp.bfloat16)
        mixed = jnp.concatenate([mixed[i * rows : (i + 1) * rows] for i in range(per_dot)], axis=1)
        att_ref[:, part] = mixed
        if last:
            outs[0][mine, part] = mixed


def attend(r, suffix_len, model_width, lengths, offsets, sums, tables, pair, earlier, last):
    width = sums[0].shape[1]
    _, prefix_len, head_size = pair.shape
    vmem = pl.BlockSpec(memory_space=pltpu.VMEM)
    smem = pl.BlockSpec(memory_space=pltpu.SMEM)
    widths = (width, 2 * head_size)
    all_rows = (r + 1) * suffix_len
    shapes = [(suffix_len, width)]
    shapes += [(all_rows, w) for w in widths] if last else [(suffix_len, widths[1])]
    earlier = earlier if last else []
    return pl.pallas_call(
        functools.partial(attend_kernel, r, last, model_width),
        in_specs=[smem] * 2 + [vmem] * (6 + len(earlier)),
        out_specs=[vmem] * len(shapes),
        out_shape=[jax.ShapeDtypeStruct(shape, jnp.bfloat16) for shape in shapes],
        compiler_params=pltpu.CompilerParams(vmem_limit_bytes=VMEM_BYTES),
        cost_estimate=pl.CostEstimate(
            flops=4 * suffix_len * width * (prefix_len + suffix_len),
            bytes_accessed=4 * prefix_len * head_size + 4 * suffix_len * (width + 2 * head_size),
            transcendentals=suffix_len * width // head_size * prefix_len,
        ),
    )(lengths, offsets, *sums, *tables, pair, *earlier)


def copies_kernel(plan, *refs):
    arrived = refs[-1]
    copies = [
        pltpu.make_async_copy(source, target, arrived.at[i])
        for i, (source, target) in enumerate(plan(refs[:-1]))
    ]
    for copy in copies:
        copy.start()
    for copy in copies:
        copy.wait()


def copied(plan, n_copies, arrays, outs, out_space=pltpu.HBM):
    size = sum(out.size for out in outs)
    return pl.pallas_call(
        functools.partial(copies_kernel, plan),
        in_specs=[pl.BlockSpec(memory_space=pltpu.HBM)] * len(arrays),
        out_specs=[pl.BlockSpec(memory_space=out_space)] * len(outs),
        out_shape=outs,
        scratch_shapes=[pltpu.SemaphoreType.DMA((n_copies,))],
        compiler_params=pltpu.CompilerParams(vmem_limit_bytes=VMEM_BYTES),
        cost_estimate=pl.CostEstimate(flops=0, bytes_accessed=4 * size, transcendentals=0),
    )(*arrays)


def stage_in(array):
    out = jax.ShapeDtypeStruct(array.shape, array.dtype)
    return copied(lambda refs: [(refs[0], refs[1])], 1, [array], [out], pltpu.VMEM)[0]


def first_rows(array, count):
    out = jax.ShapeDtypeStruct((count, array.shape[1]), array.dtype)
    return copied(
        lambda refs: [(refs[0].at[pl.ds(0, count)], refs[1])], 1, [array], [out], pltpu.VMEM
    )[0]


def stacked(arrays):
    n = len(arrays)
    out = jax.ShapeDtypeStruct((n,) + arrays[0].shape, arrays[0].dtype)
    return copied(lambda refs: [(refs[i], refs[n].at[i]) for i in range(n)], n, arrays, [out])[0]


def most_kernel(n_slots, *refs):
    own_ref, others_ref, hidden_ref, most_ref = refs[-4:]
    req_count, suffix_len, features = hidden_ref.shape
    chunk = chunk_of(features)
    attention = [
        jnp.concatenate([refs[r * n_slots + j][...] for r in range(req_count)]) for j in range(n_slots)
    ]
    for begin in range(0, features, chunk):
        columns = slice(begin, begin + chunk)
        mixed = jnp.dot(attention[0], own_ref[:, columns], preferred_element_type=jnp.float32)
        for j in range(1, n_slots):
            weights = others_ref[:, j - 1, :, columns].reshape(own_ref.shape[0], chunk)
            mixed = mixed + jnp.dot(attention[j], weights, preferred_element_type=jnp.float32)
        for r in range(req_count):
            rows = slice(r * suffix_len, (r + 1) * suffix_len)
            most_ref[rows, columns] = mixed[rows] + hidden_ref[r, :, columns].astype(jnp.float32)


def last_kernel(length_ref, attention_ref, others_ref, most_ref, out_ref):
    req_count, suffix_len, features = out_ref.shape
    chunk = chunk_of(features)
    position = lax.broadcasted_iota(jnp.int32, (suffix_len, chunk), 0)
    for begin in range(0, features, chunk):
        columns = slice(begin, begin + chunk)
        weights = others_ref[:, others_ref.shape[1] - 1, :, columns]
        weights = weights.reshape(attention_ref.shape[1], chunk)
        mixed = jnp.dot(attention_ref[...], weights, preferred_element_type=jnp.float32)
        mixed = mixed + most_ref[:, columns]
        for r in range(req_count):
            part = mixed[r * suffix_len : (r + 1) * suffix_len]
            part = jnp.where(position < length_ref[r], part, 0.0)
            out_ref[r, :, columns] = part.astype(jnp.bfloat16)


def project_out(lengths, attention, last_slot, w_own, w_others, hidden):
    req_count, suffix_len, features = hidden.shape
    n_slots = len(attention[0])
    rows = req_count * suffix_len
    vmem = pl.BlockSpec(memory_space=pltpu.VMEM)
    params = pltpu.CompilerParams(vmem_limit_bytes=VMEM_BYTES)
    flops = 2 * rows * features * w_own.shape[0]
    most = pl.pallas_call(
        functools.partial(most_kernel, n_slots),
        in_specs=[vmem] * (req_count * n_slots + 3),
        out_specs=vmem,
        out_shape=jax.ShapeDtypeStruct((rows, features), jnp.float32),
        compiler_params=params,
        cost_estimate=pl.CostEstimate(
            flops=flops * n_slots,
            bytes_accessed=2 * features * (w_own.shape[0] * n_slots + 3 * rows),
            transcendentals=0,
        ),
    )(*[block for slots in attention for block in slots], w_own, w_others, hidden)
    return pl.pallas_call(
        last_kernel,
        in_specs=[pl.BlockSpec(memory_space=pltpu.SMEM)] + [vmem] * 3,
        out_specs=vmem,
        out_shape=jax.ShapeDtypeStruct(hidden.shape, jnp.bfloat16),
        compiler_params=params,
        cost_estimate=pl.CostEstimate(
            flops=flops,
            bytes_accessed=2 * features * (w_own.shape[0] + 3 * rows),
            transcendentals=0,
        ),
    )(lengths, last_slot, w_others, most)


def shards(hidden, norm_gain, w_query, w_kv, w_out, prefix_cache, lengths, groups, owners):
    n_tp = lax.axis_size("tp")
    n_owners = lax.axis_size("req")
    my_index = lax.axis_index("req")
    place = lax.axis_index("tp")
    req_count, suffix_len, features = hidden.shape
    head_size = w_kv.shape[2]
    model_width = w_query.shape[0]

    flat_kv = w_kv.reshape(model_width, 2 * head_size)
    tables = rope_tables(suffix_len, head_size)

    share = w_out.shape[0] // n_owners
    my_rows = lax.dynamic_slice_in_dim(w_out, my_index * share, share, axis=0)
    moved = []
    for j in range(1, n_tp):
        begin = ring_place(place, j) * features
        moved.append(shift(lax.dynamic_slice_in_dim(my_rows, begin, features, axis=1), j))

    _, prefix_len, _, head_size = prefix_cache.shape
    prefixes = lax.all_gather(prefix_cache.reshape(prefix_len * 2, head_size), "req", axis=0)
    local_groups = lax.dynamic_slice_in_dim(groups, my_index * req_count, req_count)
    owner_of = jnp.sum(
        jnp.where(local_groups[:, None] == jnp.arange(n_owners)[None, :], owners[None, :], 0), axis=-1
    ).astype(jnp.int32)

    def weights_of(begin):
        return (
            lax.dynamic_slice_in_dim(norm_gain, begin, features).reshape(1, features),
            lax.dynamic_slice_in_dim(w_query, begin, features, axis=0),
            lax.dynamic_slice_in_dim(flat_kv, begin, features, axis=0),
        )

    total_rows = req_count * suffix_len
    packed = hidden.reshape(total_rows, features)
    offsets = [jnp.int32(0)]
    for r in range(1, req_count):
        offsets.append(offsets[-1] + (lengths[r - 1] + ROW_TILE - 1) // ROW_TILE * ROW_TILE)
        packed = lax.dynamic_update_slice(packed, hidden[r], (offsets[r], 0))
    live_rows = offsets[-1] + lengths[-1]
    offsets = jnp.stack(offsets)
    capacities = [total_rows * k // 16 for k in (16, 15, 14, 12, 8)]
    branch = sum((live_rows <= capacity).astype(jnp.int32) for capacity in capacities[1:])

    begins = [ring_place(place, -step) * features for step in range(n_tp)]
    own_sums = project(packed, weights_of(begins[0]), [], total_rows, in_loop=False)
    state = (packed, own_sums, moved, tables, begins, owner_of, offsets, branch)
    state = lax.optimization_barrier(state)
    packed, own_sums, moved, tables, begins, owner_of, offsets, branch = state
    w_others = lax.all_gather(stacked(moved), "req", axis=0)

    def ring_of(capacity):
        def run(packed, sums):
            block = first_rows(packed, capacity) if capacity < total_rows else packed
            for step in range(n_tp - 1):
                coming = shift(block, 1)
                if step > 0:
                    sums = project(block, weights, sums, total_rows)
                state = (coming, sums, weights_of(begins[step + 1]))
                block, sums, weights = lax.optimization_barrier(state)
            return project(block, weights, sums, total_rows, in_loop=False)

        return run

    sums = lax.switch(branch, [ring_of(c) for c in capacities], packed, own_sums)

    earlier, gathered = [], []
    for r in range(req_count):
        pair = lax.dynamic_index_in_dim(prefixes, owner_of[r], 0, keepdims=False)
        pair = pair.reshape(prefix_len, 2, head_size).transpose(1, 0, 2)
        results = attend(
            r, suffix_len, model_width, lengths, offsets, sums, tables, pair, earlier, r == req_count - 1
        )
        earlier = earlier + list(results[:2])
        gathered.append([results[0]] + [shift(results[0], j) for j in range(1, n_tp - 1)])
        prefixes = lax.optimization_barrier(prefixes)
    _, all_attention, all_caches = results
    last_slot = shift(all_attention, n_tp - 1)
    place, _ = lax.optimization_barrier((place, all_caches))
    w_own = lax.dynamic_slice_in_dim(w_out, place * features, features, axis=1)
    suffix_cache = all_caches.reshape(req_count, suffix_len, 2, head_size)
    w_others, suffix_cache = lax.optimization_barrier((w_others, suffix_cache))
    out_hidden = project_out(lengths, gathered, last_slot, w_own, stage_in(w_others), hidden)
    return (out_hidden, suffix_cache)


def solution(mesh):
    return jax.shard_map(
        shards,
        mesh=mesh,
        in_specs=(
            P("req", None, "tp"),
            P(),
            P(None, "tp"),
            P(None, None, "tp"),
            P("tp", None),
            P("req", None, None, "tp"),
            P("req"),
            P(),
            P(),
        ),
        out_specs=(P("req", None, "tp"), P("req", None, None, "tp")),
        check_vma=False,
    )
```
